32 devices in a mesh: groups: 2 (over x), expert: 16 (over z, y, core), mp: 1.
Axes of the slice: x: 2, y: 2, z: 4, core: 2. Of those that a mesh axis runs over, the one named last changes fastest.
Arguments:
- tokens: bfloat16 [2048, 2560], P(('groups', 'expert'), 'mp'), parts along dimension 0, may hold values from -6 to 6
- routes: int32 [2048, 6], P('groups'), parts along dimension 0, may hold values from 0 to 15, all different within a row; in each aligned block of 64 rows (0 to 63, 64 to 127, ...) at most 48 rows name the same one
- quant_gate: bfloat16 [32, 2560, 768], P('expert', None, 'mp'), may hold values from -6 to 6
- quant_up: bfloat16 [32, 2560, 768], P('expert', None, 'mp'), may hold values from -6 to 6
- gate_scales: float32 [32, 20, 6], P(None, None, 'mp'), may hold values from 0.5 to 2
- up_scales: float32 [32, 20, 6], P(None, None, 'mp'), may hold values from 0.5 to 2
- cluster_ids: int32 [32, 1], replicated, may hold values from 0 to 15
- frequency: float32 [32], replicated, may hold values from 0.1 to 10
Outputs:
- merged_gate: bfloat16 [32, 2560, 768], P(('groups', 'expert'), None, 'mp'), parts along dimension 0
- merged_up: bfloat16 [32, 2560, 768], P(('groups', 'expert'), None, 'mp'), parts along dimension 0
- hidden_out: bfloat16 [2048, 6, 768], P(('groups', 'expert'), None, 'mp'), parts along dimension 0
The draws below stay inside these ranges and needn't reach their ends.
There are 2 independent parts, one for each index of `groups`. The reference program is written for one: setup_inputs(seed, part) draws one part's arguments, and reference() takes and returns one part's arrays. A program takes and returns all parts, laid end to end along the dimension named above; an argument that names none is the same for every part. Nothing has to cross between parts.
Inputs may be any that keep to these rules, and one draw needn't show every extreme that they name: `routes`: in each aligned block of 64 tokens (the tokens of one device) no merged expert is named by more than 48 tokens, and some merged expert is named by exactly 48; the 6 ids of one token differ. `cluster_ids`: every merged expert has at least one source expert.
All inputs are finite; a program needn't handle non-finite values.
Results may differ from the reference program's by a relative error of at most 0.0058.
Values may be sent and summed in bfloat16 or wider, within the bound.
No kernel may reach another device: no remote copies, remote signals or barrier semaphores. Data moves between devices by JAX's collectives and lax.ppermute only.
A program may use at most 128 MiB of HBM per device.

```python
import math
import jax
import jax.numpy as jnp
import numpy as np
from jax import lax

D = 2560
FF = 768
BLOCK = 128
TOP = 6
TOKENS_PER_SHARD = 64
TOKENS = 1024
MERGED = 16
SOURCES = 32
CAP = 48


def levels(own_key, dims, shards, smallest, largest):
    level = 1.0
    for dim, parts in shards:
        heights = jax.random.uniform(jax.random.fold_in(jax.random.fold_in(own_key, 6), dim), (parts,), jnp.float32, smallest / len(shards), largest / len(shards))
        level = level * jnp.repeat(jnp.exp(heights), dims[dim] // parts).reshape((-1,) + (1,) * (len(dims) - 1 - dim))
    return level


def different_ones(own_key, rows, amount, top, lift):
    order = jax.random.permutation(jax.random.fold_in(own_key, 1), amount)
    pull = order
    for power in range(3):
        pull = pull * pull // amount
    pull = pull * lift // amount
    lots = jax.random.randint(jax.random.fold_in(own_key, 2), (rows, amount), 0, 4096) + pull
    fixed_rows = jax.random.permutation(jax.random.fold_in(own_key, 3), rows)[jnp.arange(amount) % rows]
    lots = jnp.where(jnp.arange(rows)[:, None] == fixed_rows[None, :], 1 << 14, lots)
    priority = lots * amount + jnp.arange(amount)
    return lax.top_k(priority.astype(jnp.int32), top)[1].astype(jnp.int32)


def routed_block(rng, own, number, rows, amount, top, most, slope):
    sequence = jax.random.permutation(rng, amount)
    crowded, common = load_shares(amount, rows * top, most, slope, True), load_shares(amount, rows * top, most, slope, False)
    places = jnp.arange(amount)

    def named(sizes, turn):
        used = int((sizes > 0).sum())
        fixed = max(1, used // 4)
        moved = fixed + (places - fixed + turn * (used - fixed)) % max(1, amount - fixed)
        return jnp.zeros((amount,), jnp.int32).at[sequence[jnp.where(places < fixed, places, moved)]].set(jnp.asarray(sizes, jnp.int32))

    sizes = jnp.where(number % 4 == 0, named(crowded, number // 4), named(common, number - number // 4 - 1))
    mixed = jax.random.permutation(jax.random.fold_in(own, 3), amount)
    donor, sink = mixed[0:amount // 2 * 2:2], mixed[1:amount // 2 * 2:2]
    margin = jnp.minimum(sizes[donor] - 1, most - sizes[sink]) // 2
    margin = jnp.where((donor == sequence[0]) | (sink == sequence[0]) | (sizes[sink] == 0), 0, jnp.maximum(margin, 0))
    moved = jax.random.randint(jax.random.fold_in(own, 4), (amount // 2,), 0, 1 << 20) % (margin + 1)
    sizes = sizes.at[donor].add(-moved).at[sink].add(moved)
    items = jnp.searchsorted(jnp.cumsum(sizes), jnp.arange(rows * top), side="right").astype(jnp.int32)
    grid = items.reshape(top, rows).T
    grid = grid[jax.random.permutation(jax.random.fold_in(own, 1), rows)]
    turn = jax.random.randint(jax.random.fold_in(own, 2), (rows, 1), 0, top)
    return jnp.take_along_axis(grid, (jnp.arange(top)[None, :] + turn) % top, axis=1)


def load_shares(amount, total, most, slope, full):
    weights = [(1 << 20) // math.isqrt(standing ** slope) + 1 for standing in range(1, amount + 1)]
    largest = most if full else min(most, max(-(-total // amount), total * weights[0] // sum(weights)))
    least = 1 if total - largest >= amount - 1 else 0
    given, surplus = [largest] + [least] * (amount - 1), total - largest - least * (amount - 1)
    while surplus > 0:
        free = [i for i in range(1, amount) if given[i] < largest] or [i for i in range(1, amount) if given[i] < most]
        whole, left = sum([weights[i] for i in free]), surplus
        for i in free:
            addition = min(most - given[i], max(1, left * weights[i] // whole), surplus)
            given[i] = given[i] + addition
            surplus = surplus - addition
    return np.array(given)


def bell_draw(key, extent, width, bound, cuts=(), held_as=jnp.bfloat16):
    array = jax.random.normal(key, extent, jnp.float32) * width
    if len(cuts) > 0:
        array = levels(key, extent, cuts, -0.22, 0.18) * array
    return jnp.clip(array, min=-bound, max=bound).astype(held_as)


def setup_inputs(seed: int = 0, part: int = 0) -> dict:
    seeds = jax.random.split(jax.random.key(seed), 9)
    own_keys = jax.random.split(jax.random.fold_in(seeds[8], part), 9)
    tokens = bell_draw(own_keys[0], (TOKENS, D), 1.0, 6.0, ((0, 16),))
    routes_keys = jax.random.split(jax.random.fold_in(own_keys[1], 1), TOKENS // TOKENS_PER_SHARD)
    routes_turns = jax.random.permutation(jax.random.fold_in(own_keys[1], 3), TOKENS // TOKENS_PER_SHARD)
    routes = jax.vmap(lambda own, number: routed_block(jax.random.fold_in(own_keys[1], 2), own, number, TOKENS_PER_SHARD, MERGED, TOP, CAP, 2))(routes_keys, routes_turns).reshape((TOKENS, TOP))
    quant_gate = bell_draw(seeds[2], (SOURCES, D, FF), 1.0, 6.0, ((0, 16),))
    quant_up = bell_draw(seeds[3], (SOURCES, D, FF), 1.0, 6.0, ((0, 16),))
    gate_scales = jnp.clip(jnp.exp(jax.random.uniform(seeds[4], (SOURCES, D // BLOCK, FF // BLOCK), jnp.float32, math.log(0.5), math.log(2.0))), 0.5, 2.0)
    up_scales = jnp.clip(jnp.exp(jax.random.uniform(seeds[5], (SOURCES, D // BLOCK, FF // BLOCK), jnp.float32, math.log(0.5), math.log(2.0))), 0.5, 2.0)
    cluster_ids = different_ones(seeds[6], SOURCES, MERGED, 1, 1024)
    frequency = jnp.clip(jnp.exp(jax.random.uniform(seeds[7], (SOURCES,), jnp.float32, math.log(0.1), math.log(10.0))), 0.1, 10.0)
    return dict(tokens=tokens, routes=routes, quant_gate=quant_gate, quant_up=quant_up, gate_scales=gate_scales, up_scales=up_scales, cluster_ids=cluster_ids, frequency=frequency)


def combine_weights(cluster_ids, frequency):
    member = (cluster_ids[:, 0][None, :] == jnp.arange(MERGED, dtype=jnp.int32)[:, None]).astype(jnp.float32)
    weighted = member * frequency[None, :]
    return weighted / lax.optimization_barrier(jnp.sum(weighted, axis=1, keepdims=True))

def merge_matrix(quant, scales, cluster_blend):
    broadcast_scales = jnp.repeat(jnp.repeat(scales, BLOCK, axis=1), BLOCK, axis=2)
    restore_weight_scale = quant.astype(jnp.float32) * broadcast_scales
    reduced_sum = jnp.einsum('ca,awg->cwg', cluster_blend, restore_weight_scale, precision=lax.Precision.HIGHEST)
    return reduced_sum.astype(jnp.bfloat16)

def reference(tokens, routes, quant_gate, quant_up, gate_scales, up_scales, cluster_ids, frequency):
    cluster_blend = combine_weights(cluster_ids, frequency)
    merged_gate = merge_matrix(quant_gate, gate_scales, cluster_blend)
    merged_up = merge_matrix(quant_up, up_scales, cluster_blend)
    factor = 1.0 / math.sqrt(D)

    def add_expert(reduced_sum, expert_index):
        gate_value = jnp.dot(tokens, merged_gate[expert_index], preferred_element_type=jnp.float32) * factor
        up_projection_value = jnp.dot(tokens, merged_up[expert_index], preferred_element_type=jnp.float32) * factor
        hidden = lax.optimization_barrier((jax.nn.silu(gate_value) * up_projection_value).astype(jnp.bfloat16))
        hidden = hidden.astype(jnp.float32)
        chosen = (routes == expert_index).astype(jnp.float32)
        return (reduced_sum + chosen[:, :, None] * hidden[:, None, :], None)
    initial = jnp.zeros((TOKENS, TOP, FF), jnp.float32)
    reduced_sum, _ = lax.scan(add_expert, initial, jnp.arange(MERGED, dtype=jnp.int32))
    return (merged_gate, merged_up, reduced_sum.astype(jnp.bfloat16))
```

```python
import math

import jax
import jax.numpy as jnp
from jax import lax
from jax.experimental import pallas as pl
from jax.experimental.pallas import tpu as pltpu
from jax.sharding import PartitionSpec as P

D = 2560
BLOCK = 128
PLANES = 4
VMEM_LIMIT = 48 * 1024 * 1024


def cluster_weights(cluster_ids, frequency):
    ids = cluster_ids[:, 0]
    same = (ids[:, None] == ids[None, :]).astype(jnp.float32)
    return frequency / jnp.sum(same * frequency[None, :], axis=1)


def pack(info, gate, up, after, column, plane):
    sources, depth, _ = gate.shape
    rows = depth // plane

    def kernel(info_ref, gate_ref, up_ref, after_ref, *rest):
        outs, sems = rest[:plane], rest[plane]
        place = info_ref[0]

        def move(source):
            copies = [
                pltpu.make_async_copy(
                    source.at[
                        :,
                        pl.ds(pl.multiple_of((place ^ shift) * rows, 16), rows),
                        pl.ds(column * BLOCK, BLOCK),
                    ],
                    outs[shift],
                    sems.at[shift],
                )
                for shift in range(plane)
            ]
            for copy in copies:
                copy.start()
            for copy in copies:
                copy.wait()

        @pl.when(info_ref[2] == 0)
        def _():
            move(gate_ref)

        @pl.when(info_ref[2] != 0)
        def _():
            move(up_ref)

    any_spec = pl.BlockSpec(memory_space=pl.ANY)
    return pl.pallas_call(
        kernel,
        out_shape=[jax.ShapeDtypeStruct((sources, rows, BLOCK), gate.dtype)] * plane,
        in_specs=[pl.BlockSpec(memory_space=pltpu.SMEM)] + [any_spec] * 3,
        out_specs=[any_spec] * plane,
        scratch_shapes=[pltpu.SemaphoreType.DMA((plane,))],
        cost_estimate=pl.CostEstimate(
            flops=0, bytes_accessed=4 * sources * depth * BLOCK, transcendentals=0
        ),
        name="pack",
    )(info, gate, up, after)


def merge(info, ids, weights, scales, near, far, received, column, scale_blocks):
    plane, sources, rows, width = near.shape
    step = math.gcd(rows, BLOCK)
    row_blocks, column_blocks = scale_blocks

    def kernel(info_ref, ids_ref, weights_ref, scales_ref, near_ref, far_ref, *rest):
        total = rest[-1]
        place, inner = info_ref[0], info_ref[1]
        outer = jnp.where(inner == 1, 0, PLANES - 1)
        other_outer = PLANES - 1 - outer
        other_inner = PLANES - 1 - inner
        to_inner, to_outer = (
            (inner, outer) if received is not None else (other_inner, other_outer)
        )
        row_block = (place * rows + pl.program_id(0) * step) // BLOCK

        @pl.when(info_ref[3] == 1)
        def _():
            if received is None:
                total[...] = jnp.zeros_like(total)
            else:
                total[...] = rest[0][...].astype(jnp.float32)
            for block, held in ((near_ref, inner), (far_ref, outer)):
                for shift in range(plane):
                    for number in range(sources):
                        source = (held * plane + (place ^ shift)) * sources + number
                        target = ids_ref[source]
                        target_plane = target // plane
                        slot = (target % plane) ^ place

                        @pl.when((target_plane == to_inner) | (target_plane == to_outer))
                        def _():
                            scale = scales_ref[
                                (source * row_blocks + row_block) * column_blocks + column
                            ]
                            index = jnp.where(target_plane == to_outer, plane, 0) + slot
                            total[index] += block[shift, number].astype(jnp.float32) * (
                                weights_ref[source] * scale
                            )

            if received is None:
                rest[0][...] = total[...].astype(jnp.bfloat16)
            else:
                rest[1][...] = total[:plane].astype(jnp.bfloat16)
                rest[2][...] = total[plane:].astype(jnp.bfloat16)

    smem = pl.BlockSpec(memory_space=pltpu.SMEM)
    stack = pl.BlockSpec((plane, sources, step, width), lambda i: (0, 0, i, 0))
    both = pl.BlockSpec((2 * plane, step, width), lambda i: (0, i, 0))
    one = pl.BlockSpec((plane, step, width), lambda i: (0, i, 0))
    if received is None:
        operands, in_specs = (), []
        out_shape = jax.ShapeDtypeStruct((2 * plane, rows, width), jnp.bfloat16)
        out_specs = both
    else:
        operands, in_specs = (received,), [both]
        out_shape = [jax.ShapeDtypeStruct((plane, rows, width), jnp.bfloat16)] * 2
        out_specs = [one, one]
    return pl.pallas_call(
        kernel,
        grid=(rows // step,),
        out_shape=out_shape,
        in_specs=[smem] * 4 + [stack, stack] + in_specs,
        out_specs=out_specs,
        scratch_shapes=[pltpu.VMEM((2 * plane, step, width), jnp.float32)],
        compiler_params=pltpu.CompilerParams(vmem_limit_bytes=VMEM_LIMIT),
        cost_estimate=pl.CostEstimate(
            flops=4 * near.size, bytes_accessed=8 * near.size, transcendentals=0
        ),
        name="merge",
    )(info, ids, weights, scales, near, far, *operands)


def run_chunk(info, grouped, own, partner, outputs, column, shape):
    plane, rows, width = own.shape
    depth, full = shape
    count = grouped.shape[0]
    factor = 1.0 / math.sqrt(D)

    def kernel(info_ref, grouped_ref, own_ref, partner_ref, *rest):
        gate_out, up_out, hidden_ref, whole, sems, out_sems = rest[len(outputs) :]
        place = info_ref[0]

        def load(pieces, start, base):
            return [
                pltpu.make_async_copy(
                    pieces.at[shift],
                    whole.at[
                        pl.ds(pl.multiple_of((place ^ shift) * rows, 16), rows),
                        pl.ds(start, width),
                    ],
                    sems.at[base + shift],
                )
                for shift in range(plane)
            ]

        def fill(gate, up):
            copies = load(gate, 0, 0) + load(up, width, plane)
            for copy in copies:
                copy.start()
            for copy in copies:
                copy.wait()

        @pl.when(info_ref[2] == 0)
        def _():
            fill(own_ref, partner_ref)

        @pl.when(info_ref[2] != 0)
        def _():
            fill(partner_ref, own_ref)

        stores = [
            pltpu.make_async_copy(
                whole.at[:, pl.ds(index * width, width)],
                out.at[0, :, pl.ds(column * width, width)],
                out_sems.at[index],
            )
            for index, out in enumerate((gate_out, up_out))
        ]
        for store in stores:
            store.start()
        values = jnp.dot(grouped_ref[...], whole[...], preferred_element_type=jnp.float32)
        gate_value = values[:, :width] * factor
        up_value = values[:, width:] * factor
        hidden_ref[...] = (gate_value / (1.0 + jnp.exp(-gate_value)) * up_value).astype(
            jnp.bfloat16
        )
        for store in stores:
            store.wait()

    any_spec = pl.BlockSpec(memory_space=pl.ANY)
    weights = jax.ShapeDtypeStruct((1, depth, full), jnp.bfloat16)
    return pl.pallas_call(
        kernel,
        out_shape=[weights, weights, jax.ShapeDtypeStruct((count, width), jnp.bfloat16)],
        in_specs=[
            pl.BlockSpec(memory_space=pltpu.SMEM),
            pl.BlockSpec(memory_space=pltpu.VMEM),
            any_spec,
            any_spec,
        ]
        + [any_spec] * len(outputs),
        out_specs=[any_spec, any_spec, pl.BlockSpec(memory_space=pltpu.VMEM)],
        scratch_shapes=[
            pltpu.VMEM((depth, 2 * width), jnp.bfloat16),
            pltpu.SemaphoreType.DMA((2 * plane,)),
            pltpu.SemaphoreType.DMA((2,)),
        ],
        input_output_aliases={4 + index: index for index in range(len(outputs))},
        compiler_params=pltpu.CompilerParams(vmem_limit_bytes=VMEM_LIMIT),
        cost_estimate=pl.CostEstimate(
            flops=4 * count * depth * width,
            bytes_accessed=2 * (grouped.size + 4 * depth * width),
            transcendentals=count * width,
        ),
        name="run_chunk",
    )(info, grouped, own, partner, *outputs)


def route_slots(routes, merged_count, tok_dev):
    experts = jnp.arange(merged_count, dtype=jnp.int32)
    hit_table = jnp.sum((routes[:, :, None] == experts).astype(jnp.int32), axis=1)
    hit_table = hit_table.reshape(-1, tok_dev, merged_count)
    position_lookup = jnp.cumsum(hit_table, axis=1) - hit_table
    return (hit_table, position_lookup)


def shards(tokens, routes, quant_gate, quant_up, gate_scales, up_scales, cluster_ids, frequency):
    expert_count = lax.axis_size("expert")
    own_index = lax.axis_index("expert")
    group_count = lax.axis_size("groups")
    half = lax.axis_index("groups") % 2
    plane = expert_count // PLANES
    place, level = own_index % plane, own_index // plane
    is_inner = (level == 1) | (level == 2)
    depth, full = quant_gate.shape[1:]
    chunks = full // BLOCK
    tok_dev = tokens.shape[0]
    top_count = routes.shape[1]
    capacity = min(tok_dev, 2 * tok_dev * top_count // expert_count)

    def wires(pairs):
        return [(a * plane + p, b * plane + p) for a, b in pairs for p in range(plane)]

    inward = wires([(0, 1), (3, 2)])
    across = wires([(1, 2), (2, 1)])
    outward = wires([(1, 0), (2, 3)])
    within = {
        shift: [(i, i // plane * plane + (i % plane ^ shift)) for i in range(expert_count)]
        for shift in range(1, plane)
    }
    partners = [(g, g ^ 1) for g in range(group_count)]

    def swap_within(pieces):
        return [pieces[0]] + [
            lax.ppermute(pieces[shift], "expert", within[shift]) for shift in range(1, plane)
        ]

    info = jnp.stack([place, level, half, is_inner.astype(jnp.int32)]).astype(jnp.int32)
    ids = cluster_ids[:, 0]
    weights = cluster_weights(cluster_ids, frequency)
    scales = jnp.where(half == 0, gate_scales, up_scales)
    scale_blocks = scales.shape[1:]
    scales = scales.reshape(-1)

    hit_table, position_lookup = route_slots(routes, expert_count, tok_dev)
    positions = jnp.arange(capacity, dtype=jnp.int32)
    everyone = lax.all_gather(tokens, "expert", axis=0, tiled=True)
    column_hits = lax.dynamic_index_in_dim(hit_table, own_index, 2, keepdims=False)
    column_slots = lax.dynamic_index_in_dim(position_lookup, own_index, 2, keepdims=False)
    placing = (
        (column_hits[:, None, :] == 1) & (column_slots[:, None, :] == positions[None, :, None])
    ).astype(jnp.bfloat16)
    spread = everyone.reshape(expert_count, tok_dev, everyone.shape[1])
    arrived = jnp.einsum(
        "jct,jtd->jcd", placing, spread, preferred_element_type=jnp.float32
    ).astype(jnp.bfloat16)
    arrived = lax.all_gather(arrived, "mp", axis=2, tiled=True)
    grouped = arrived.reshape(expert_count * capacity, arrived.shape[2])

    experts = jnp.arange(expert_count, dtype=jnp.int32)
    local_routes = lax.dynamic_slice_in_dim(routes, own_index * tok_dev, tok_dev, 0)
    own_slots = lax.dynamic_index_in_dim(position_lookup, own_index, 0, keepdims=False)
    chosen = local_routes[:, :, None] == experts
    slot_of = jnp.sum(jnp.where(chosen, own_slots[:, None, :], 0), axis=2)
    picking = (chosen[:, :, :, None] & (slot_of[:, :, None, None] == positions)).astype(
        jnp.bfloat16
    )
    picking = picking.reshape(tok_dev * top_count, expert_count * capacity)

    arrivals = []
    hiddens = []
    outputs = ()
    for column in range(chunks):
        after = arrivals[column - 2] if column >= 2 else info
        pieces = pack(info, quant_gate, quant_up, after, column, plane)
        near = jnp.stack(swap_within(pieces))
        far = lax.ppermute(near, "expert", inward)
        arrivals.append(far)
        partial = merge(info, ids, weights, scales, near, far, None, column, scale_blocks)
        received = lax.ppermute(partial, "expert", across)
        to_inner, to_outer = merge(
            info, ids, weights, scales, near, far, received, column, scale_blocks
        )
        mine = jnp.where(is_inner, to_inner, lax.ppermute(to_outer, "expert", outward))
        own = jnp.stack(swap_within([mine[shift] for shift in range(plane)]))
        partner = lax.ppermute(own, "groups", partners)
        *outputs, hidden = run_chunk(
            info, grouped, own, partner, tuple(outputs), column, (depth, full)
        )
        hiddens.append(hidden.reshape(expert_count, capacity, BLOCK))

    cut = max(1, chunks - 2)
    finished = []
    for batch in (hiddens[:cut], hiddens[cut:]):
        hidden = jnp.concatenate(batch, axis=2)
        returned = lax.all_to_all(hidden, "expert", split_axis=0, concat_axis=0, tiled=True)
        rows = returned.reshape(expert_count * capacity, returned.shape[2])
        finished.append(
            jnp.dot(picking, rows, preferred_element_type=jnp.float32).astype(jnp.bfloat16)
        )
    output = jnp.concatenate(finished, axis=1)
    merged_gate, merged_up = outputs
    return (merged_gate, merged_up, output.reshape(tok_dev, top_count, full))


def solution(mesh):
    return jax.shard_map(
        shards,
        mesh=mesh,
        in_specs=(
            P(("groups", "expert"), "mp"),
            P("groups", None),
            P("expert", None, "mp"),
            P("expert", None, "mp"),
            P(None, None, "mp"),
            P(None, None, "mp"),
            P(),
            P(),
        ),
        out_specs=(
            P(("groups", "expert"), None, "mp"),
            P(("groups", "expert"), None, "mp"),
            P(("groups", "expert"), None, "mp"),
        ),
        check_vma=False,
    )
```

```python
import math

import jax
import jax.numpy as jnp
from jax import lax
from jax.experimental import pallas as pl
from jax.experimental.pallas import tpu as pltpu
from jax.sharding import PartitionSpec as P

D = 2560
BLOCK = 128
PLANES = 4
VMEM_LIMIT = 48 * 1024 * 1024


def cluster_weights(cluster_ids, frequency):
    ids = cluster_ids[:, 0]
    same = (ids[:, None] == ids[None, :]).astype(jnp.float32)
    return frequency / jnp.sum(same * frequency[None, :], axis=1)


def pack(info, gate, up, after, column, plane):
    sources, depth, _ = gate.shape
    rows = depth // plane

    def kernel(info_ref, gate_ref, up_ref, after_ref, *rest):
        outs, held, in_sems, out_sems = rest[:plane], *rest[plane:]
        place = info_ref[0]

        def move(source):
            loads = [
                pltpu.make_async_copy(
                    source.at[
                        :,
                        pl.ds(pl.multiple_of((place ^ shift) * rows, 16), rows),
                        pl.ds(column * BLOCK, BLOCK),
                    ],
                    held.at[shift],
                    in_sems.at[shift],
                )
                for shift in range(plane)
            ]
            stores = [
                pltpu.make_async_copy(held.at[shift], outs[shift], out_sems.at[shift])
                for shift in range(plane)
            ]
            for load in loads:
                load.start()
            for load, store in zip(loads, stores):
                load.wait()
                store.start()
            for store in stores:
                store.wait()

        @pl.when(info_ref[2] == 0)
        def _():
            move(gate_ref)

        @pl.when(info_ref[2] != 0)
        def _():
            move(up_ref)

    any_spec = pl.BlockSpec(memory_space=pl.ANY)
    return pl.pallas_call(
        kernel,
        out_shape=[jax.ShapeDtypeStruct((sources, rows, BLOCK), gate.dtype)] * plane,
        in_specs=[pl.BlockSpec(memory_space=pltpu.SMEM)] + [any_spec] * 3,
        out_specs=[any_spec] * plane,
        scratch_shapes=[
            pltpu.VMEM((plane, sources, rows, BLOCK), gate.dtype),
            pltpu.SemaphoreType.DMA((plane,)),
            pltpu.SemaphoreType.DMA((plane,)),
        ],
        compiler_params=pltpu.CompilerParams(vmem_limit_bytes=VMEM_LIMIT),
        cost_estimate=pl.CostEstimate(
            flops=0, bytes_accessed=4 * sources * depth * BLOCK, transcendentals=0
        ),
        name="pack",
    )(info, gate, up, after)


def merge(info, ids, weights, scales, near, far, received, column, scale_blocks):
    plane, sources, rows, width = near.shape
    step = math.gcd(rows, BLOCK)
    row_blocks, column_blocks = scale_blocks

    def kernel(info_ref, ids_ref, weights_ref, scales_ref, near_ref, far_ref, *rest):
        total = rest[-1]
        place, inner = info_ref[0], info_ref[1]
        outer = jnp.where(inner == 1, 0, PLANES - 1)
        other_outer = PLANES - 1 - outer
        other_inner = PLANES - 1 - inner
        to_inner, to_outer = (
            (inner, outer) if received is not None else (other_inner, other_outer)
        )
        row_block = (place * rows + pl.program_id(0) * step) // BLOCK

        @pl.when(info_ref[3] == 1)
        def _():
            if received is None:
                total[...] = jnp.zeros_like(total)
            else:
                total[...] = rest[0][...].astype(jnp.float32)
            for block, held in ((near_ref, inner), (far_ref, outer)):
                for shift in range(plane):
                    for number in range(sources):
                        source = (held * plane + (place ^ shift)) * sources + number
                        target = ids_ref[source]
                        target_plane = target // plane
                        slot = (target % plane) ^ place

                        @pl.when((target_plane == to_inner) | (target_plane == to_outer))
                        def _():
                            scale = scales_ref[
                                (source * row_blocks + row_block) * column_blocks + column
                            ]
                            index = jnp.where(target_plane == to_outer, plane, 0) + slot
                            total[index] += block[shift, number].astype(jnp.float32) * (
                                weights_ref[source] * scale
                            )

            if received is None:
                rest[0][...] = total[...].astype(jnp.bfloat16)
            else:
                rest[1][...] = total[:plane].astype(jnp.bfloat16)
                rest[2][...] = total[plane:].astype(jnp.bfloat16)

    smem = pl.BlockSpec(memory_space=pltpu.SMEM)
    stack = pl.BlockSpec((plane, sources, step, width), lambda i: (0, 0, i, 0))
    both = pl.BlockSpec((2 * plane, step, width), lambda i: (0, i, 0))
    one = pl.BlockSpec((plane, step, width), lambda i: (0, i, 0))
    if received is None:
        operands, in_specs = (), []
        out_shape = jax.ShapeDtypeStruct((2 * plane, rows, width), jnp.bfloat16)
        out_specs = both
    else:
        operands, in_specs = (received,), [both]
        out_shape = [jax.ShapeDtypeStruct((plane, rows, width), jnp.bfloat16)] * 2
        out_specs = [one, one]
    return pl.pallas_call(
        kernel,
        grid=(rows // step,),
        out_shape=out_shape,
        in_specs=[smem] * 4 + [stack, stack] + in_specs,
        out_specs=out_specs,
        scratch_shapes=[pltpu.VMEM((2 * plane, step, width), jnp.float32)],
        compiler_params=pltpu.CompilerParams(vmem_limit_bytes=VMEM_LIMIT),
        cost_estimate=pl.CostEstimate(
            flops=4 * near.size, bytes_accessed=8 * near.size, transcendentals=0
        ),
        name="merge",
    )(info, ids, weights, scales, near, far, *operands)


def run_chunk(info, grouped, own, partner, outputs, column, shape):
    plane, rows, width = own.shape
    depth, full = shape
    count = grouped.shape[0]
    factor = 1.0 / math.sqrt(D)

    def kernel(info_ref, grouped_ref, own_ref, partner_ref, *rest):
        gate_out, up_out, hidden_ref, whole, sems, out_sems = rest[len(outputs) :]
        place = info_ref[0]

        def load(pieces, start, base):
            return [
                pltpu.make_async_copy(
                    pieces.at[shift],
                    whole.at[
                        pl.ds(pl.multiple_of((place ^ shift) * rows, 16), rows),
                        pl.ds(start, width),
                    ],
                    sems.at[base + shift],
                )
                for shift in range(plane)
            ]

        def fill(gate, up):
            copies = load(gate, 0, 0) + load(up, width, plane)
            for copy in copies:
                copy.start()
            for copy in copies:
                copy.wait()

        @pl.when(info_ref[2] == 0)
        def _():
            fill(own_ref, partner_ref)

        @pl.when(info_ref[2] != 0)
        def _():
            fill(partner_ref, own_ref)

        stores = [
            pltpu.make_async_copy(
                whole.at[:, pl.ds(index * width, width)],
                out.at[0, :, pl.ds(column * width, width)],
                out_sems.at[index],
            )
            for index, out in enumerate((gate_out, up_out))
        ]
        for store in stores:
            store.start()
        values = jnp.dot(grouped_ref[...], whole[...], preferred_element_type=jnp.float32)
        gate_value = values[:, :width] * factor
        up_value = values[:, width:] * factor
        hidden_ref[...] = (gate_value / (1.0 + jnp.exp(-gate_value)) * up_value).astype(
            jnp.bfloat16
        )
        for store in stores:
            store.wait()

    any_spec = pl.BlockSpec(memory_space=pl.ANY)
    weights = jax.ShapeDtypeStruct((1, depth, full), jnp.bfloat16)
    return pl.pallas_call(
        kernel,
        out_shape=[weights, weights, jax.ShapeDtypeStruct((count, width), jnp.bfloat16)],
        in_specs=[
            pl.BlockSpec(memory_space=pltpu.SMEM),
            pl.BlockSpec(memory_space=pltpu.VMEM),
            any_spec,
            any_spec,
        ]
        + [any_spec] * len(outputs),
        out_specs=[any_spec, any_spec, pl.BlockSpec(memory_space=pltpu.VMEM)],
        scratch_shapes=[
            pltpu.VMEM((depth, 2 * width), jnp.bfloat16),
            pltpu.SemaphoreType.DMA((2 * plane,)),
            pltpu.SemaphoreType.DMA((2,)),
        ],
        input_output_aliases={4 + index: index for index in range(len(outputs))},
        compiler_params=pltpu.CompilerParams(vmem_limit_bytes=VMEM_LIMIT),
        cost_estimate=pl.CostEstimate(
            flops=4 * count * depth * width,
            bytes_accessed=2 * (grouped.size + 4 * depth * width),
            transcendentals=count * width,
        ),
        name="run_chunk",
    )(info, grouped, own, partner, *outputs)


def route_slots(routes, merged_count, tok_dev):
    experts = jnp.arange(merged_count, dtype=jnp.int32)
    hit_table = jnp.sum((routes[:, :, None] == experts).astype(jnp.int32), axis=1)
    hit_table = hit_table.reshape(-1, tok_dev, merged_count)
    position_lookup = jnp.cumsum(hit_table, axis=1) - hit_table
    return (hit_table, position_lookup)


def shards(tokens, routes, quant_gate, quant_up, gate_scales, up_scales, cluster_ids, frequency):
    expert_count = lax.axis_size("expert")
    own_index = lax.axis_index("expert")
    group_count = lax.axis_size("groups")
    half = lax.axis_index("groups") % 2
    plane = expert_count // PLANES
    place, level = own_index % plane, own_index // plane
    is_inner = (level == 1) | (level == 2)
    depth, full = quant_gate.shape[1:]
    chunks = full // BLOCK
    tok_dev = tokens.shape[0]
    top_count = routes.shape[1]
    capacity = min(tok_dev, 2 * tok_dev * top_count // expert_count)

    def wires(pairs):
        return [(a * plane + p, b * plane + p) for a, b in pairs for p in range(plane)]

    inward = wires([(0, 1), (3, 2)])
    across = wires([(1, 2), (2, 1)])
    outward = wires([(1, 0), (2, 3)])
    within = {
        shift: [(i, i // plane * plane + (i % plane ^ shift)) for i in range(expert_count)]
        for shift in range(1, plane)
    }
    partners = [(g, g ^ 1) for g in range(group_count)]

    def swap_within(pieces):
        return [pieces[0]] + [
            lax.ppermute(pieces[shift], "expert", within[shift]) for shift in range(1, plane)
        ]

    info = jnp.stack([place, level, half, is_inner.astype(jnp.int32)]).astype(jnp.int32)
    ids = cluster_ids[:, 0]
    weights = cluster_weights(cluster_ids, frequency)
    scales = jnp.where(half == 0, gate_scales, up_scales)
    scale_blocks = scales.shape[1:]
    scales = scales.reshape(-1)

    hit_table, position_lookup = route_slots(routes, expert_count, tok_dev)
    positions = jnp.arange(capacity, dtype=jnp.int32)
    everyone = lax.all_gather(tokens, "expert", axis=0, tiled=True)
    column_hits = lax.dynamic_index_in_dim(hit_table, own_index, 2, keepdims=False)
    column_slots = lax.dynamic_index_in_dim(position_lookup, own_index, 2, keepdims=False)
    placing = (
        (column_hits[:, None, :] == 1) & (column_slots[:, None, :] == positions[None, :, None])
    ).astype(jnp.bfloat16)
    spread = everyone.reshape(expert_count, tok_dev, everyone.shape[1])
    arrived = jnp.einsum(
        "jct,jtd->jcd", placing, spread, preferred_element_type=jnp.float32
    ).astype(jnp.bfloat16)
    arrived = lax.all_gather(arrived, "mp", axis=2, tiled=True)
    grouped = arrived.reshape(expert_count * capacity, arrived.shape[2])

    experts = jnp.arange(expert_count, dtype=jnp.int32)
    local_routes = lax.dynamic_slice_in_dim(routes, own_index * tok_dev, tok_dev, 0)
    own_slots = lax.dynamic_index_in_dim(position_lookup, own_index, 0, keepdims=False)
    chosen = local_routes[:, :, None] == experts
    slot_of = jnp.sum(jnp.where(chosen, own_slots[:, None, :], 0), axis=2)
    picking = (chosen[:, :, :, None] & (slot_of[:, :, None, None] == positions)).astype(
        jnp.bfloat16
    )
    picking = picking.reshape(tok_dev * top_count, expert_count * capacity)

    arrivals = []
    hiddens = []
    outputs = ()
    for column in range(chunks):
        after = arrivals[column - 2] if column >= 2 else info
        pieces = pack(info, quant_gate, quant_up, after, column, plane)
        near = jnp.stack(swap_within(pieces))
        far = lax.ppermute(near, "expert", inward)
        arrivals.append(far)
        partial = merge(info, ids, weights, scales, near, far, None, column, scale_blocks)
        received = lax.ppermute(partial, "expert", across)
        to_inner, to_outer = merge(
            info, ids, weights, scales, near, far, received, column, scale_blocks
        )
        mine = jnp.where(is_inner, to_inner, lax.ppermute(to_outer, "expert", outward))
        own = jnp.stack(swap_within([mine[shift] for shift in range(plane)]))
        partner = lax.ppermute(own, "groups", partners)
        *outputs, hidden = run_chunk(
            info, grouped, own, partner, tuple(outputs), column, (depth, full)
        )
        hiddens.append(hidden.reshape(expert_count, capacity, BLOCK))

    cut = max(1, chunks - 2)
    finished = []
    for batch in (hiddens[:cut], hiddens[cut:]):
        hidden = jnp.concatenate(batch, axis=2)
        returned = lax.all_to_all(hidden, "expert", split_axis=0, concat_axis=0, tiled=True)
        rows = returned.reshape(expert_count * capacity, returned.shape[2])
        finished.append(
            jnp.dot(picking, rows, preferred_element_type=jnp.float32).astype(jnp.bfloat16)
        )
    output = jnp.concatenate(finished, axis=1)
    merged_gate, merged_up = outputs
    return (merged_gate, merged_up, output.reshape(tok_dev, top_count, full))


def solution(mesh):
    return jax.shard_map(
        shards,
        mesh=mesh,
        in_specs=(
            P(("groups", "expert"), "mp"),
            P("groups", None),
            P("expert", None, "mp"),
            P("expert", None, "mp"),
            P(None, None, "mp"),
            P(None, None, "mp"),
            P(),
            P(),
        ),
        out_specs=(
            P(("groups", "expert"), None, "mp"),
            P(("groups", "expert"), None, "mp"),
            P(("groups", "expert"), None, "mp"),
        ),
        check_vma=False,
    )
```

```python
import math
import random

import jax
import jax.numpy as jnp
from jax import lax
from jax.experimental import pallas as pl
from jax.experimental.pallas import tpu as pltpu
from jax.sharding import PartitionSpec as P

D = 2560
BLOCK = 128
PLANES = 4
TOKEN = jax.ShapeDtypeStruct((8, 128), jnp.float32)
ANY = pl.BlockSpec(memory_space=pl.ANY)
SMEM = pl.BlockSpec(memory_space=pltpu.SMEM)
VMEM = pl.BlockSpec(memory_space=pltpu.VMEM)
VMEM_LIMIT = 48 * 1024 * 1024


def cluster_weights(cluster_ids, frequency):
    ids = cluster_ids[:, 0]
    same = (ids[:, None] == ids[None, :]).astype(jnp.float32)
    return frequency / jnp.sum(same * frequency[None, :], axis=1)


def step_call(kernel, token, operands, in_specs, out_shape, out_specs, cost, **options):
    count = len(operands)

    def ordered(*refs):
        kernel(*refs[:count], *refs[count + 1 : count + 1 + len(out_shape)], *refs[count + 2 + len(out_shape) :])

    *results, token = pl.pallas_call(
        ordered,
        out_shape=[*out_shape, TOKEN],
        in_specs=[*in_specs, ANY],
        out_specs=[*out_specs, ANY],
        compiler_params=pltpu.CompilerParams(vmem_limit_bytes=VMEM_LIMIT),
        cost_estimate=pl.CostEstimate(flops=cost[0], bytes_accessed=cost[1], transcendentals=0),
        **options,
    )(*operands, token)
    return results, token


def pack(token, info, gate, up, start, width, plane):
    sources, depth, _ = gate.shape
    rows = depth // plane

    def kernel(info_ref, gate_ref, up_ref, *rest):
        outs, held, in_sems, out_sems = rest[:plane], *rest[plane:]
        place = info_ref[0]

        def move(source):
            loads = [
                pltpu.make_async_copy(
                    source.at[
                        :,
                        pl.ds(pl.multiple_of((place ^ shift) * rows, 16), rows),
                        pl.ds(start, width),
                    ],
                    held.at[shift],
                    in_sems.at[shift],
                )
                for shift in range(plane)
            ]
            stores = [
                pltpu.make_async_copy(held.at[shift], outs[shift], out_sems.at[shift])
                for shift in range(plane)
            ]
            for load in loads:
                load.start()
            for load, store in zip(loads, stores):
                load.wait()
                store.start()
            for store in stores:
                store.wait()

        @pl.when(info_ref[2] == 0)
        def _():
            move(gate_ref)

        @pl.when(info_ref[2] != 0)
        def _():
            move(up_ref)

    return step_call(
        kernel,
        token,
        (info, gate, up),
        [SMEM, ANY, ANY],
        [jax.ShapeDtypeStruct((sources, rows, width), gate.dtype)] * plane,
        [ANY] * plane,
        (0, 4 * sources * depth * width),
        scratch_shapes=[
            pltpu.VMEM((plane, sources, rows, width), gate.dtype),
            pltpu.SemaphoreType.DMA((plane,)),
            pltpu.SemaphoreType.DMA((plane,)),
        ],
        name="pack",
    )


def stack(token, pieces):
    plane = len(pieces)

    def kernel(*refs):
        for shift in range(plane):
            refs[plane][shift] = refs[shift][...]

    (whole,), token = step_call(
        kernel,
        token,
        tuple(pieces),
        [VMEM] * plane,
        [jax.ShapeDtypeStruct((plane,) + pieces[0].shape, pieces[0].dtype)],
        [VMEM],
        (0, 4 * plane * pieces[0].size),
        name="stack",
    )
    return whole, token


def hold(token, value, earlier):
    def kernel(*refs):
        pass

    (value,), token = step_call(
        kernel,
        token,
        (value, *earlier),
        [ANY] * (1 + len(earlier)),
        [jax.ShapeDtypeStruct(value.shape, value.dtype)],
        [ANY],
        (0, 0),
        input_output_aliases={0: 0},
        name="hold",
    )
    return value, token


def merge(token, info, ids, weights, scales, near, far, received, start, scale_blocks):
    plane, sources, rows, width = near.shape
    step = math.gcd(rows, BLOCK)
    row_blocks, column_blocks = scale_blocks
    first = start // BLOCK

    def kernel(info_ref, ids_ref, weights_ref, scales_ref, near_ref, far_ref, *rest):
        total = rest[-1]
        place, inner = info_ref[0], info_ref[1]
        outer = jnp.where(inner == 1, 0, PLANES - 1)
        to_inner = inner if received is not None else PLANES - 1 - inner
        to_outer = outer if received is not None else PLANES - 1 - outer
        row_block = (place * rows + pl.program_id(0) * step) // BLOCK

        @pl.when(info_ref[3] == 1)
        def _():
            if received is None:
                total[...] = jnp.zeros_like(total)
            else:
                total[...] = rest[0][...].astype(jnp.float32)
            for block, held in ((near_ref, inner), (far_ref, outer)):
                for shift in range(plane):
                    for number in range(sources):
                        source = (held * plane + (place ^ shift)) * sources + number
                        target = ids_ref[source]
                        target_plane = target // plane
                        slot = (target % plane) ^ place

                        @pl.when((target_plane == to_inner) | (target_plane == to_outer))
                        def _():
                            index = jnp.where(target_plane == to_outer, plane, 0) + slot
                            base = (source * row_blocks + row_block) * column_blocks + first
                            for part in range(width // BLOCK):
                                lanes = pl.ds(part * BLOCK, BLOCK)
                                factor = weights_ref[source] * scales_ref[base + part]
                                total[index, :, lanes] += (
                                    block[shift, number, :, lanes].astype(jnp.float32) * factor
                                )

            if received is None:
                rest[0][...] = total[...].astype(jnp.bfloat16)
            else:
                rest[1][...] = total[:plane].astype(jnp.bfloat16)
                rest[2][...] = total[plane:].astype(jnp.bfloat16)

    pieces = pl.BlockSpec((plane, sources, step, width), lambda i: (0, 0, i, 0))
    both = pl.BlockSpec((2 * plane, step, width), lambda i: (0, i, 0))
    one = pl.BlockSpec((plane, step, width), lambda i: (0, i, 0))
    if received is None:
        extra, extra_specs = (), []
        out_shape = [jax.ShapeDtypeStruct((2 * plane, rows, width), jnp.bfloat16)]
        out_specs = [both]
    else:
        extra, extra_specs = (received,), [both]
        out_shape = [jax.ShapeDtypeStruct((plane, rows, width), jnp.bfloat16)] * 2
        out_specs = [one, one]
    return step_call(
        kernel,
        token,
        (info, ids, weights, scales, near, far, *extra),
        [SMEM] * 4 + [pieces, pieces] + extra_specs,
        out_shape,
        out_specs,
        (4 * near.size, 8 * near.size),
        grid=(rows // step,),
        scratch_shapes=[pltpu.VMEM((2 * plane, step, width), jnp.float32)],
        name="merge",
    )


def choose(token, info, inside, outside):
    plane, rows, width = inside.shape

    def kernel(info_ref, inside_ref, outside_ref, *rest):
        outs, sems = rest[:plane], rest[plane]

        def move(source):
            copies = [
                pltpu.make_async_copy(source.at[shift], outs[shift], sems.at[shift])
                for shift in range(plane)
            ]
            for copy in copies:
                copy.start()
            for copy in copies:
                copy.wait()

        @pl.when(info_ref[3] == 1)
        def _():
            move(inside_ref)

        @pl.when(info_ref[3] != 1)
        def _():
            move(outside_ref)

    return step_call(
        kernel,
        token,
        (info, inside, outside),
        [SMEM, ANY, ANY],
        [jax.ShapeDtypeStruct((rows, width), inside.dtype)] * plane,
        [VMEM] * plane,
        (0, 4 * inside.size),
        scratch_shapes=[pltpu.SemaphoreType.DMA((plane,))],
        name="choose",
    )


def run_chunk(token, info, grouped, own, partner, outputs, start, shape, blocks):
    plane, rows, width = own.shape
    depth, full = shape
    count = grouped.shape[0]
    each = count // len(blocks)
    factor = 1.0 / math.sqrt(D)

    def kernel(info_ref, grouped_ref, own_ref, partner_ref, *rest):
        gate_out, up_out, hidden_ref, whole, sems, out_sems = rest[len(outputs) :]
        place = info_ref[0]

        def load(pieces, column, base):
            return [
                pltpu.make_async_copy(
                    pieces.at[shift],
                    whole.at[
                        pl.ds(pl.multiple_of((place ^ shift) * rows, 16), rows),
                        pl.ds(column, width),
                    ],
                    sems.at[base + shift],
                )
                for shift in range(plane)
            ]

        def fill(gate, up):
            copies = load(gate, 0, 0) + load(up, width, plane)
            for copy in copies:
                copy.start()
            for copy in copies:
                copy.wait()

        @pl.when(info_ref[2] == 0)
        def _():
            fill(own_ref, partner_ref)

        @pl.when(info_ref[2] != 0)
        def _():
            fill(partner_ref, own_ref)

        stores = [
            pltpu.make_async_copy(
                whole.at[:, pl.ds(index * width, width)],
                out.at[0, :, pl.ds(start, width)],
                out_sems.at[index],
            )
            for index, out in enumerate((gate_out, up_out))
        ]
        for store in stores:
            store.start()
        values = jnp.dot(grouped_ref[...], whole[...], preferred_element_type=jnp.float32)
        gate_value = values[:, :width] * factor
        up_value = values[:, width:] * factor
        hidden = (gate_value / (1.0 + jnp.exp(-gate_value)) * up_value).astype(jnp.bfloat16)
        for index, block in enumerate(blocks):
            hidden_ref[block] = hidden[index * each : (index + 1) * each]
        for store in stores:
            store.wait()

    weights = jax.ShapeDtypeStruct((1, depth, full), jnp.bfloat16)
    return step_call(
        kernel,
        token,
        (info, grouped, own, partner, *outputs),
        [SMEM, VMEM, ANY, ANY] + [ANY] * len(outputs),
        [weights, weights, jax.ShapeDtypeStruct((len(blocks), each, width), jnp.bfloat16)],
        [ANY, ANY, VMEM],
        (4 * count * depth * width, 2 * (grouped.size + 4 * depth * width)),
        scratch_shapes=[
            pltpu.VMEM((depth, 2 * width), jnp.bfloat16),
            pltpu.SemaphoreType.DMA((2 * plane,)),
            pltpu.SemaphoreType.DMA((2,)),
        ],
        input_output_aliases={4 + index: index for index in range(len(outputs))},
        name="run_chunk",
    )


STEPS = {
    "run": (("x", "run before"), (2.0, 1.2), None),
    "join": (("e",), (1.0, 0.7), ("x", 12.0, "x")),
    "choose": (("d",), (3.0, 0.8), ("e", 7.0, "y")),
    "finish": (("m",), (3.0, 3.0), ("d", 13.0, "out")),
    "partial": (("a",), (4.0, 2.2), ("m", 25.0, "middle")),
    "send": (("stack", "a before"), (1.5, 0.0), ("a", 25.0, "in")),
    "stack": (("b",), (1.0, 1.0), None),
    "pack": (("stack before",), (5.0, 1.0), ("b", 13.0, "y")),
}
LATENCY = 1.5
TRIES = 1500


def play(widths, delay):
    ready = {}
    links = {}
    now = 0.0
    order = []
    left = [(name, chunk) for name in STEPS for chunk in range(len(widths))]
    while left:
        best = None
        for name, chunk in left:
            needs = []
            for need in STEPS[name][0]:
                if not need.endswith(" before"):
                    needs.append((need, chunk))
                elif chunk > 0:
                    needs.append((need[: -len(" before")], chunk - 1))
            if all(need in ready for need in needs):
                begin = max([now] + [ready[need] for need in needs])
                rank = begin + delay[(name, chunk)]
                if best is None or rank < best[0]:
                    best = (rank, begin, name, chunk)
        _, begin, name, chunk = best
        _, (fixed, each), sent = STEPS[name]
        now = begin + fixed + each * widths[chunk]
        ready[(name, chunk)] = now
        if sent is not None:
            what, cost, link = sent
            links[link] = max(now, links.get(link, 0.0)) + cost * widths[chunk]
            ready[(what, chunk)] = links[link] + LATENCY
        left.remove((name, chunk))
        order.append((name, chunk))
    return now, order


def plan(widths):
    draw = random.Random(0)
    steps = [(name, chunk) for name in STEPS for chunk in range(len(widths))]
    best = None
    for attempt in range(TRIES):
        if attempt == 0 or draw.random() < 0.3:
            delay = {step: draw.uniform(-15.0, 15.0) + 3.0 * step[1] for step in steps}
        else:
            delay = dict(best[2])
            for _ in range(draw.randint(1, 3)):
                delay[draw.choice(steps)] += draw.gauss(0.0, 10.0)
        end, order = play(widths, delay)
        if best is None or end < best[0]:
            best = (end, order, delay)
    return best[1]


def route_slots(routes, merged_count, tok_dev):
    experts = jnp.arange(merged_count, dtype=jnp.int32)
    hit_table = jnp.sum((routes[:, :, None] == experts).astype(jnp.int32), axis=1)
    hit_table = hit_table.reshape(-1, tok_dev, merged_count)
    position_lookup = jnp.cumsum(hit_table, axis=1) - hit_table
    return (hit_table, position_lookup)


def chunk_widths(blocks):
    if blocks < 4:
        return [1] * blocks
    return [1, 2] + [1] * (blocks - 3)


def shards(tokens, routes, quant_gate, quant_up, gate_scales, up_scales, cluster_ids, frequency):
    expert_count = lax.axis_size("expert")
    own_index = lax.axis_index("expert")
    group_count = lax.axis_size("groups")
    half = lax.axis_index("groups") % 2
    plane = expert_count // PLANES
    place, level = own_index % plane, own_index // plane
    is_inner = (level == 1) | (level == 2)
    depth, full = quant_gate.shape[1:]
    tok_dev = tokens.shape[0]
    top_count = routes.shape[1]
    capacity = min(tok_dev, 2 * tok_dev * top_count // expert_count)

    def wires(pairs):
        return [(a * plane + p, b * plane + p) for a, b in pairs for p in range(plane)]

    inward = wires([(0, 1), (3, 2)])
    across = wires([(1, 2), (2, 1)])
    outward = wires([(1, 0), (2, 3)])
    within = {
        shift: [(i, i // plane * plane + (i % plane ^ shift)) for i in range(expert_count)]
        for shift in range(1, plane)
    }
    partners = [(g, g ^ 1) for g in range(group_count)]

    def swap_within(pieces):
        return [pieces[0]] + [
            lax.ppermute(pieces[shift], "expert", within[shift]) for shift in range(1, plane)
        ]

    info = jnp.stack([place, level, half, is_inner.astype(jnp.int32)]).astype(jnp.int32)
    ids = cluster_ids[:, 0]
    weights = cluster_weights(cluster_ids, frequency)
    scales = jnp.where(half == 0, gate_scales, up_scales)
    scale_blocks = scales.shape[1:]
    scales = scales.reshape(-1)

    blocks = [z * plane + p for p in range(plane) for z in range(PLANES)]
    by_line = [[z * plane + p for z in range(PLANES)] for p in range(plane)]
    by_plane = [[z * plane + p for p in range(plane)] for z in range(PLANES)]
    everyone = lax.all_gather(tokens, "expert", axis=0, tiled=True, axis_index_groups=by_line)
    everyone = lax.all_gather(everyone, "expert", axis=0, tiled=True, axis_index_groups=by_plane)
    spread = everyone.reshape(expert_count, tok_dev, everyone.shape[1])
    hit_table, position_lookup = route_slots(routes, expert_count, tok_dev)
    positions = jnp.arange(capacity, dtype=jnp.int32)

    def in_blocks(table):
        column = lax.dynamic_index_in_dim(table, own_index, 2, keepdims=False)
        column = column.reshape(PLANES, plane, tok_dev).transpose(1, 0, 2)
        return column.reshape(expert_count, 1, tok_dev)

    placing = (
        (in_blocks(hit_table) == 1) & (in_blocks(position_lookup) == positions[None, :, None])
    ).astype(jnp.bfloat16)
    arrived = jnp.einsum(
        "jct,jtd->jcd", placing, spread, preferred_element_type=jnp.float32
    ).astype(jnp.bfloat16)
    arrived = lax.all_gather(arrived, "mp", axis=2, tiled=True)
    grouped = arrived.reshape(expert_count * capacity, arrived.shape[2])

    experts = jnp.arange(expert_count, dtype=jnp.int32)
    local_routes = lax.dynamic_slice_in_dim(routes, own_index * tok_dev, tok_dev, 0)
    own_slots = lax.dynamic_index_in_dim(position_lookup, own_index, 0, keepdims=False)
    chosen = local_routes[:, :, None] == experts
    slot_of = jnp.sum(jnp.where(chosen, own_slots[:, None, :], 0), axis=2)
    picking = (chosen[:, :, :, None] & (slot_of[:, :, None, None] == positions)).astype(
        jnp.bfloat16
    )
    picking = picking.reshape(tok_dev * top_count, expert_count * capacity)

    widths = chunk_widths(full // BLOCK)
    starts = [BLOCK * sum(widths[:chunk]) for chunk in range(len(widths))]
    token = jnp.zeros(TOKEN.shape, TOKEN.dtype)
    held, near, far, received, inside, outside, mine, own, partner, hiddens = (
        {} for _ in range(10)
    )
    outputs = ()
    for name, c in plan(widths):
        start, width = starts[c], widths[c] * BLOCK
        if name == "pack":
            pieces, token = pack(token, info, quant_gate, quant_up, start, width, plane)
            held[c] = swap_within(pieces)
        elif name == "stack":
            near[c], token = stack(token, held[c])
        elif name == "send":
            near[c], token = hold(token, near[c], [far[c - 1]] if c else [])
            far[c] = lax.ppermute(near[c], "expert", inward)
        elif name == "partial":
            (partial,), token = merge(
                token, info, ids, weights, scales, near[c], far[c], None, start, scale_blocks
            )
            received[c] = lax.ppermute(partial, "expert", across)
        elif name == "finish":
            (inside[c], outward_rows), token = merge(
                token, info, ids, weights, scales, near[c], far[c], received[c], start, scale_blocks
            )
            outside[c] = lax.ppermute(outward_rows, "expert", outward)
        elif name == "choose":
            pieces, token = choose(token, info, inside[c], outside[c])
            mine[c] = swap_within(pieces)
        elif name == "join":
            own[c], token = stack(token, mine[c])
            partner[c] = lax.ppermute(own[c], "groups", partners)
        else:
            (*outputs, hiddens[c]), token = run_chunk(
                token, info, grouped, own[c], partner[c], outputs, start, (depth, full), blocks
            )

    last = len(widths) - 1
    finished = []
    for batch in (range(last), range(last, last + 1)):
        hidden = jnp.concatenate([hiddens[c] for c in batch], axis=2)
        returned = lax.all_to_all(hidden, "expert", split_axis=0, concat_axis=0, tiled=True)
        rows = returned.reshape(expert_count * capacity, returned.shape[2])
        finished.append(
            jnp.dot(picking, rows, preferred_element_type=jnp.float32).astype(jnp.bfloat16)
        )
    output = jnp.concatenate(finished, axis=1)
    merged_gate, merged_up = outputs
    return (merged_gate, merged_up, output.reshape(tok_dev, top_count, full))


def solution(mesh):
    return jax.shard_map(
        shards,
        mesh=mesh,
        in_specs=(
            P(("groups", "expert"), "mp"),
            P("groups", None),
            P("expert", None, "mp"),
            P("expert", None, "mp"),
            P(None, None, "mp"),
            P(None, None, "mp"),
            P(),
            P(),
        ),
        out_specs=(
            P(("groups", "expert"), None, "mp"),
            P(("groups", "expert"), None, "mp"),
            P(("groups", "expert"), None, "mp"),
        ),
        check_vma=False,
    )
```

```python
import math
import random

import jax
import jax.numpy as jnp
from jax import lax
from jax.experimental import pallas as pl
from jax.experimental.pallas import tpu as pltpu
from jax.sharding import PartitionSpec as P

D = 2560
BLOCK = 128
PLANES = 4
TOKEN = jax.ShapeDtypeStruct((8, 128), jnp.float32)
ANY = pl.BlockSpec(memory_space=pl.ANY)
SMEM = pl.BlockSpec(memory_space=pltpu.SMEM)
VMEM = pl.BlockSpec(memory_space=pltpu.VMEM)
VMEM_LIMIT = 60 * 1024 * 1024


def cluster_weights(cluster_ids, frequency):
    ids = cluster_ids[:, 0]
    same = (ids[:, None] == ids[None, :]).astype(jnp.float32)
    return frequency / jnp.sum(same * frequency[None, :], axis=1)


def step_call(kernel, token, operands, in_specs, out_shape, out_specs, cost, **options):
    count = len(operands)

    def ordered(*refs):
        kernel(*refs[:count], *refs[count + 1 : count + 1 + len(out_shape)], *refs[count + 2 + len(out_shape) :])

    *results, token = pl.pallas_call(
        ordered,
        out_shape=[*out_shape, TOKEN],
        in_specs=[*in_specs, ANY],
        out_specs=[*out_specs, ANY],
        compiler_params=pltpu.CompilerParams(vmem_limit_bytes=VMEM_LIMIT),
        cost_estimate=pl.CostEstimate(flops=cost[0], bytes_accessed=cost[1], transcendentals=0),
        **options,
    )(*operands, token)
    return results, token


def pack(token, info, gate, up, start, width, plane):
    sources, depth, _ = gate.shape
    rows = depth // plane

    def kernel(info_ref, gate_ref, up_ref, *rest):
        outs, held, in_sems, out_sems = rest[:plane], *rest[plane:]
        place = info_ref[0]

        def move(source):
            loads = [
                pltpu.make_async_copy(
                    source.at[
                        :,
                        pl.ds(pl.multiple_of((place ^ shift) * rows, 16), rows),
                        pl.ds(start, width),
                    ],
                    held.at[shift],
                    in_sems.at[shift],
                )
                for shift in range(plane)
            ]
            stores = [
                pltpu.make_async_copy(held.at[shift], outs[shift], out_sems.at[shift])
                for shift in range(plane)
            ]
            for load in loads:
                load.start()
            for load, store in zip(loads, stores):
                load.wait()
                store.start()
            for store in stores:
                store.wait()

        @pl.when(info_ref[2] == 0)
        def _():
            move(gate_ref)

        @pl.when(info_ref[2] != 0)
        def _():
            move(up_ref)

    return step_call(
        kernel,
        token,
        (info, gate, up),
        [SMEM, ANY, ANY],
        [jax.ShapeDtypeStruct((sources, rows, width), gate.dtype)] * plane,
        [ANY] * plane,
        (0, 4 * sources * depth * width),
        scratch_shapes=[
            pltpu.VMEM((plane, sources, rows, width), gate.dtype),
            pltpu.SemaphoreType.DMA((plane,)),
            pltpu.SemaphoreType.DMA((plane,)),
        ],
        name="pack",
    )


def merge(token, info, ids, weights, scales, near, far, received, start, scale_blocks):
    plane = len(near)
    sources, rows, width = near[0].shape
    step = math.gcd(rows, BLOCK)
    row_blocks, column_blocks = scale_blocks
    first = start // BLOCK

    def kernel(info_ref, ids_ref, weights_ref, scales_ref, *rest):
        blocks, rest, total = rest[: 2 * plane], rest[2 * plane : -1], rest[-1]
        place, inner = info_ref[0], info_ref[1]
        outer = jnp.where(inner == 1, 0, PLANES - 1)
        to_inner = inner if received is not None else PLANES - 1 - inner
        to_outer = outer if received is not None else PLANES - 1 - outer
        row_block = (place * rows + pl.program_id(0) * step) // BLOCK

        @pl.when(info_ref[3] == 1)
        def _():
            if received is None:
                total[...] = jnp.zeros_like(total)
            else:
                total[...] = rest[0][...].astype(jnp.float32)
            for index, block in enumerate(blocks):
                held = inner if index < plane else outer
                for number in range(sources):
                    source = (held * plane + (place ^ (index % plane))) * sources + number
                    target = ids_ref[source]
                    target_plane = target // plane
                    slot = (target % plane) ^ place

                    @pl.when((target_plane == to_inner) | (target_plane == to_outer))
                    def _():
                        into = jnp.where(target_plane == to_outer, plane, 0) + slot
                        base = (source * row_blocks + row_block) * column_blocks + first
                        for part in range(width // BLOCK):
                            lanes = pl.ds(part * BLOCK, BLOCK)
                            factor = weights_ref[source] * scales_ref[base + part]
                            total[into, :, lanes] += (
                                block[number, :, lanes].astype(jnp.float32) * factor
                            )

            if received is None:
                rest[0][...] = total[...].astype(jnp.bfloat16)
            else:
                for index in range(2 * plane):
                    rest[1 + index][...] = total[index].astype(jnp.bfloat16)

    pieces = pl.BlockSpec((sources, step, width), lambda i: (0, i, 0))
    both = pl.BlockSpec((2 * plane, step, width), lambda i: (0, i, 0))
    one = pl.BlockSpec((step, width), lambda i: (i, 0))
    if received is None:
        extra, extra_specs = (), []
        out_shape = [jax.ShapeDtypeStruct((2 * plane, rows, width), jnp.bfloat16)]
        out_specs = [both]
    else:
        extra, extra_specs = (received,), [both]
        out_shape = [jax.ShapeDtypeStruct((rows, width), jnp.bfloat16)] * (2 * plane)
        out_specs = [one] * (2 * plane)
    size = plane * near[0].size
    return step_call(
        kernel,
        token,
        (info, ids, weights, scales, *near, *far, *extra),
        [SMEM] * 4 + [pieces] * (2 * plane) + extra_specs,
        out_shape,
        out_specs,
        (4 * size, 8 * size),
        grid=(rows // step,),
        scratch_shapes=[pltpu.VMEM((2 * plane, step, width), jnp.float32)],
        name="merge",
    )


def join(token, info, inside, outside):
    plane = len(inside)
    rows, width = inside[0].shape

    def kernel(info_ref, *rest):
        out, sems = rest[2 * plane :]

        def move(sources):
            copies = [
                pltpu.make_async_copy(sources[shift], out.at[shift], sems.at[shift])
                for shift in range(plane)
            ]
            for copy in copies:
                copy.start()
            for copy in copies:
                copy.wait()

        @pl.when(info_ref[3] == 1)
        def _():
            move(rest[:plane])

        @pl.when(info_ref[3] != 1)
        def _():
            move(rest[plane : 2 * plane])

    (own,), token = step_call(
        kernel,
        token,
        (info, *inside, *outside),
        [SMEM] + [ANY] * (2 * plane),
        [jax.ShapeDtypeStruct((plane, rows, width), inside[0].dtype)],
        [VMEM],
        (0, 4 * plane * rows * width),
        scratch_shapes=[pltpu.SemaphoreType.DMA((plane,))],
        name="join",
    )
    return own, token


def pair(token, tokens, other):
    def kernel(tokens_ref, other_ref, out_ref):
        out_ref[0] = tokens_ref[...]
        out_ref[1] = other_ref[...]

    (both,), token = step_call(
        kernel,
        token,
        (tokens, other),
        [VMEM, VMEM],
        [jax.ShapeDtypeStruct((2,) + tokens.shape, tokens.dtype)],
        [VMEM],
        (0, 8 * tokens.size),
        name="pair",
    )
    return both, token


def line(token, info, tokens, other, crossed, forwarded):
    def kernel(info_ref, tokens_ref, other_ref, crossed_ref, forwarded_ref, out_ref):
        level = info_ref[1]
        low = level < PLANES // 2
        out_ref[level] = tokens_ref[...]
        out_ref[level ^ 1] = other_ref[...]

        def put(pair_ref):
            out_ref[jnp.where(low, 2, 1)] = pair_ref[0]
            out_ref[jnp.where(low, 3, 0)] = pair_ref[1]

        @pl.when(info_ref[3] == 1)
        def _():
            put(crossed_ref)

        @pl.when(info_ref[3] != 1)
        def _():
            put(forwarded_ref)

    (whole,), token = step_call(
        kernel,
        token,
        (info, tokens, other, crossed, forwarded),
        [SMEM] + [VMEM] * 4,
        [jax.ShapeDtypeStruct((PLANES,) + tokens.shape, tokens.dtype)],
        [VMEM],
        (0, 16 * tokens.size),
        name="line",
    )
    return whole, token


def dispatch(token, placing, lines):
    count, capacity, tok_dev = placing.shape
    width = lines[0].shape[2]

    def kernel(placing_ref, *rest):
        out_ref = rest[len(lines)]
        for block in range(count):
            rows = rest[block // PLANES][block % PLANES]
            out_ref[block * capacity : (block + 1) * capacity] = jnp.dot(
                placing_ref[block], rows, preferred_element_type=jnp.float32
            ).astype(jnp.bfloat16)

    (grouped,), token = step_call(
        kernel,
        token,
        (placing, *lines),
        [VMEM] * (1 + len(lines)),
        [jax.ShapeDtypeStruct((count * capacity, width), jnp.bfloat16)],
        [VMEM],
        (2 * count * capacity * tok_dev * width, 4 * count * tok_dev * width),
        name="dispatch",
    )
    return grouped, token


def run_chunk(token, info, grouped, own, partner, outputs, start, shape, devices):
    plane, rows, width = own.shape
    depth, full = shape
    count = grouped.shape[0]
    each = count // devices
    factor = 1.0 / math.sqrt(D)

    def kernel(info_ref, grouped_ref, own_ref, partner_ref, *rest):
        gate_out, up_out, hidden_ref, whole, sems, out_sems = rest[len(outputs) :]
        place = info_ref[0]

        def load(pieces, column, base):
            return [
                pltpu.make_async_copy(
                    pieces.at[shift],
                    whole.at[
                        pl.ds(pl.multiple_of((place ^ shift) * rows, 16), rows),
                        pl.ds(column, width),
                    ],
                    sems.at[base + shift],
                )
                for shift in range(plane)
            ]

        def fill(gate, up):
            copies = load(gate, 0, 0) + load(up, width, plane)
            for copy in copies:
                copy.start()
            for copy in copies:
                copy.wait()

        @pl.when(info_ref[2] == 0)
        def _():
            fill(own_ref, partner_ref)

        @pl.when(info_ref[2] != 0)
        def _():
            fill(partner_ref, own_ref)

        stores = [
            pltpu.make_async_copy(
                whole.at[:, pl.ds(index * width, width)],
                out.at[0, :, pl.ds(start, width)],
                out_sems.at[index],
            )
            for index, out in enumerate((gate_out, up_out))
        ]
        for store in stores:
            store.start()
        values = jnp.dot(grouped_ref[...], whole[...], preferred_element_type=jnp.float32)
        gate_value = values[:, :width] * factor
        up_value = values[:, width:] * factor
        hidden = (gate_value / (1.0 + jnp.exp(-gate_value)) * up_value).astype(jnp.bfloat16)
        for index in range(devices):
            device = (index % PLANES) * plane + (place ^ (index // PLANES))
            hidden_ref[device] = hidden[index * each : (index + 1) * each]
        for store in stores:
            store.wait()

    weights = jax.ShapeDtypeStruct((1, depth, full), jnp.bfloat16)
    return step_call(
        kernel,
        token,
        (info, grouped, own, partner, *outputs),
        [SMEM, VMEM, ANY, ANY] + [ANY] * len(outputs),
        [weights, weights, jax.ShapeDtypeStruct((devices, each, width), jnp.bfloat16)],
        [ANY, ANY, VMEM],
        (4 * count * depth * width, 2 * (grouped.size + 4 * depth * width)),
        scratch_shapes=[
            pltpu.VMEM((depth, 2 * width), jnp.bfloat16),
            pltpu.SemaphoreType.DMA((2 * plane,)),
            pltpu.SemaphoreType.DMA((2,)),
        ],
        input_output_aliases={4 + index: index for index in range(len(outputs))},
        name="run_chunk",
    )


STEPS = {
    "pair": (("t1",), (3.0, 0.0), (("t2", 13.0, "middle"),)),
    "line": (("t3",), (4.0, 0.0), (("t4", 40.0, "y"),)),
    "dispatch": (("t4",), (6.0, 0.0), ()),
    "pack": (("pack before",), (8.0, 0.6), (("a", 25.0, "in"), ("b", 13.0, "y"))),
    "partial": (("a", "b"), (5.0, 1.5), (("m", 25.0, "middle"),)),
    "finish": (("m",), (8.0, 2.0), (("d", 13.0, "out"), ("e", 13.0, "y"))),
    "join": (("d", "e"), (2.5, 0.5), (("x", 12.0, "x"),)),
    "run": (("x", "dispatch", "run before"), (2.0, 1.5), ()),
}
ONCE = ("pair", "line", "dispatch")
LATENCY = 2.0
RETURN = 30.0
TRIES = 2500


def needs_of(name, chunk):
    needs = []
    for need in STEPS[name][0]:
        if need in ONCE or need[0] == "t":
            needs.append((need, 0))
        elif not need.endswith(" before"):
            needs.append((need, chunk))
        elif chunk > 0:
            needs.append((need[: -len(" before")], chunk - 1))
    return needs


def advance(now, until, links, done):
    while now < until:
        left = [min(load.values()) * len(load) for load in links.values() if load]
        span = min(left + [until - now])
        for load in links.values():
            for key in load:
                load[key] -= span / len(load)
        for load in links.values():
            for key in [key for key, rest in load.items() if rest <= 1e-6]:
                del load[key]
                done[key] = now + span + LATENCY
        now += span
    return now


def play(widths, order):
    links = {"in": {}, "middle": {}, "out": {}, "y": {}, "x": {}}
    done = {("t1", 0): 8.0}
    clock = 0.0
    now = 0.0
    for name, chunk in order:
        for need in needs_of(name, chunk):
            if need == ("t3", 0):
                need = ("t2", 0)
                extra = 16.0
            else:
                extra = 0.0
            while need not in done:
                clock = advance(clock, clock + 1.0, links, done)
            now = max(now, done[need] + extra)
        _, (fixed, each), sent = STEPS[name]
        width = 1 if name in ONCE else widths[chunk]
        now += fixed + each * width
        clock = advance(clock, max(clock, now), links, done)
        done[(name, chunk)] = now
        for what, cost, link in sent:
            links[link][(what, chunk)] = cost * width
    back = done[("run", max(0, len(widths) - 2))] + RETURN
    return max(now, back) + 0.02 * sum(done[("run", chunk)] for chunk in range(len(widths)))


def arrange(steps, rank):
    sender = {what: name for name, step in STEPS.items() for what, _, _ in step[2]}
    placed, order, left = set(), [], sorted(steps, key=lambda step: rank[step])
    while left:
        for step in left:
            needs = [(sender.get(n, n), c) for n, c in needs_of(*step) if n not in ("t1", "t3")]
            if step == ("line", 0):
                needs = [("pair", 0)]
            if all(need in placed for need in needs):
                break
        left.remove(step)
        placed.add(step)
        order.append(step)
    return order


def plan(widths):
    draw = random.Random(0)
    offset = {"pack": 0, "partial": 35, "finish": 65, "join": 95, "run": 115}
    rank = {(name, 0): value for name, value in zip(ONCE, (8, 20, 75))}
    time = 0.0
    for chunk, width in enumerate(widths):
        for name, value in offset.items():
            rank[(name, chunk)] = time + value
        time += 27.0 * width
    steps = list(rank)
    order = arrange(steps, rank)
    best = (play(widths, order), order, rank)
    for _ in range(TRIES):
        trial = dict(best[2])
        for _ in range(draw.randint(1, 3)):
            trial[draw.choice(steps)] += draw.gauss(0.0, 15.0)
        order = arrange(steps, trial)
        end = play(widths, order)
        if end <= best[0]:
            best = (end, order, trial)
    return best[1]


def route_slots(routes, merged_count, tok_dev):
    experts = jnp.arange(merged_count, dtype=jnp.int32)
    hit_table = jnp.sum((routes[:, :, None] == experts).astype(jnp.int32), axis=1)
    hit_table = hit_table.reshape(-1, tok_dev, merged_count)
    position_lookup = jnp.cumsum(hit_table, axis=1) - hit_table
    return (hit_table, position_lookup)


def chunk_widths(blocks):
    if blocks < 6:
        return [1] * blocks
    return [1, 1, blocks - 4, 1, 1]


def shards(tokens, routes, quant_gate, quant_up, gate_scales, up_scales, cluster_ids, frequency):
    expert_count = lax.axis_size("expert")
    own_index = lax.axis_index("expert")
    group_count = lax.axis_size("groups")
    half = lax.axis_index("groups") % 2
    plane = expert_count // PLANES
    place, level = own_index % plane, own_index // plane
    is_inner = (level == 1) | (level == 2)
    depth, full = quant_gate.shape[1:]
    tok_dev = tokens.shape[0]
    top_count = routes.shape[1]
    capacity = min(tok_dev, 2 * tok_dev * top_count // expert_count)

    def wires(pairs, shift):
        return [(a * plane + p, b * plane + (p ^ shift)) for a, b in pairs for p in range(plane)]

    def send(value, pairs, shift=0):
        return lax.ppermute(value, "expert", wires(pairs, shift))

    inward = [(0, 1), (3, 2)]
    outward = [(1, 0), (2, 3)]
    across = [(1, 2), (2, 1)]
    inner = [(1, 1), (2, 2)]
    every = [(z, z) for z in range(PLANES)]
    shifts = range(plane)
    partners = [(g, g ^ 1) for g in range(group_count)]

    info = jnp.stack([place, level, half, is_inner.astype(jnp.int32)]).astype(jnp.int32)
    ids = cluster_ids[:, 0]
    weights = cluster_weights(cluster_ids, frequency)
    scales = jnp.where(half == 0, gate_scales, up_scales)
    scale_blocks = scales.shape[1:]
    scales = scales.reshape(-1)

    hit_table, position_lookup = route_slots(routes, expert_count, tok_dev)
    positions = jnp.arange(capacity, dtype=jnp.int32)

    def in_blocks(table):
        column = lax.dynamic_index_in_dim(table, own_index, 2, keepdims=False)
        column = column.reshape(PLANES, plane, tok_dev)
        column = jnp.take(column, place ^ jnp.arange(plane, dtype=jnp.int32), axis=1)
        return column.transpose(1, 0, 2).reshape(expert_count, 1, tok_dev)

    placing = (
        (in_blocks(hit_table) == 1) & (in_blocks(position_lookup) == positions[None, :, None])
    ).astype(jnp.bfloat16)

    experts = jnp.arange(expert_count, dtype=jnp.int32)
    local_routes = lax.dynamic_slice_in_dim(routes, own_index * tok_dev, tok_dev, 0)
    own_slots = lax.dynamic_index_in_dim(position_lookup, own_index, 0, keepdims=False)
    chosen = local_routes[:, :, None] == experts
    slot_of = jnp.sum(jnp.where(chosen, own_slots[:, None, :], 0), axis=2)
    picking = (chosen[:, :, :, None] & (slot_of[:, :, None, None] == positions)).astype(
        jnp.bfloat16
    )
    picking = picking.reshape(tok_dev * top_count, expert_count * capacity)

    widths = chunk_widths(full // BLOCK)
    starts = [BLOCK * sum(widths[:chunk]) for chunk in range(len(widths))]
    token = jnp.zeros(TOKEN.shape, TOKEN.dtype)
    neighbour = send(tokens, inward + outward)
    near, far, received, inside, outside, own, partner, hiddens = ({} for _ in range(8))
    outputs = ()
    for name, c in plan(widths):
        start, width = starts[c], widths[c] * BLOCK
        if name == "pair":
            both, token = pair(token, tokens, neighbour)
            crossed = send(both, across)
            forwarded = send(crossed, outward)
        elif name == "line":
            whole, token = line(token, info, tokens, neighbour, crossed, forwarded)
            lines = {0: whole}
            bit = plane // 2
            while bit:
                for shift in list(lines):
                    lines[shift ^ bit] = send(lines[shift], every, bit)
                bit //= 2
        elif name == "dispatch":
            grouped, token = dispatch(token, placing, [lines[shift] for shift in shifts])
            grouped = lax.all_gather(grouped, "mp", axis=1, tiled=True)
        elif name == "pack":
            pieces, token = pack(token, info, quant_gate, quant_up, start, width, plane)
            far[c] = [send(pieces[shift], inward, shift) for shift in shifts]
            near[c] = [send(pieces[shift], inner, shift) if shift else pieces[0] for shift in shifts]
        elif name == "partial":
            (partial,), token = merge(
                token, info, ids, weights, scales, near[c], far[c], None, start, scale_blocks
            )
            received[c] = send(partial, across)
        elif name == "finish":
            rows, token = merge(
                token, info, ids, weights, scales, near[c], far[c], received[c], start, scale_blocks
            )
            outside[c] = [send(rows[plane + shift], outward, shift) for shift in shifts]
            inside[c] = [send(rows[shift], inner, shift) if shift else rows[0] for shift in shifts]
        elif name == "join":
            own[c], token = join(token, info, inside[c], outside[c])
            partner[c] = lax.ppermute(own[c], "groups", partners)
        else:
            (*outputs, hiddens[c]), token = run_chunk(
                token, info, grouped, own[c], partner[c], outputs, start, (depth, full), expert_count
            )

    last = len(widths) - 1
    finished = []
    for batch in (range(last), range(last, last + 1)):
        hidden = jnp.concatenate([hiddens[c] for c in batch], axis=2)
        returned = lax.all_to_all(hidden, "expert", split_axis=0, concat_axis=0, tiled=True)
        rows = returned.reshape(expert_count * capacity, returned.shape[2])
        finished.append(
            jnp.dot(picking, rows, preferred_element_type=jnp.float32).astype(jnp.bfloat16)
        )
    output = jnp.concatenate(finished, axis=1)
    merged_gate, merged_up = outputs
    return (merged_gate, merged_up, output.reshape(tok_dev, top_count, full))


def solution(mesh):
    return jax.shard_map(
        shards,
        mesh=mesh,
        in_specs=(
            P(("groups", "expert"), "mp"),
            P("groups", None),
            P("expert", None, "mp"),
            P("expert", None, "mp"),
            P(None, None, "mp"),
            P(None, None, "mp"),
            P(),
            P(),
        ),
        out_specs=(
            P(("groups", "expert"), None, "mp"),
            P(("groups", "expert"), None, "mp"),
            P(("groups", "expert"), None, "mp"),
        ),
        check_vma=False,
    )
```

```python
import math
import random

import jax
import jax.numpy as jnp
from jax import lax
from jax.experimental import pallas as pl
from jax.experimental.pallas import tpu as pltpu
from jax.sharding import PartitionSpec as P

D = 2560
BLOCK = 128
PLANES = 4
TOKEN = jax.ShapeDtypeStruct((8, 128), jnp.float32)
ANY = pl.BlockSpec(memory_space=pl.ANY)
SMEM = pl.BlockSpec(memory_space=pltpu.SMEM)
VMEM = pl.BlockSpec(memory_space=pltpu.VMEM)
VMEM_LIMIT = 60 * 1024 * 1024


def cluster_weights(cluster_ids, frequency):
    ids = cluster_ids[:, 0]
    same = (ids[:, None] == ids[None, :]).astype(jnp.float32)
    return frequency / jnp.sum(same * frequency[None, :], axis=1)


def step_call(kernel, token, operands, in_specs, out_shape, out_specs, cost, **options):
    count = len(operands)

    def ordered(*refs):
        kernel(*refs[:count], *refs[count + 1 : count + 1 + len(out_shape)], *refs[count + 2 + len(out_shape) :])

    *results, token = pl.pallas_call(
        ordered,
        out_shape=[*out_shape, TOKEN],
        in_specs=[*in_specs, ANY],
        out_specs=[*out_specs, ANY],
        compiler_params=pltpu.CompilerParams(vmem_limit_bytes=VMEM_LIMIT),
        cost_estimate=pl.CostEstimate(flops=cost[0], bytes_accessed=cost[1], transcendentals=0),
        **options,
    )(*operands, token)
    return results, token


def pack(token, info, gate, up, start, width, plane):
    sources, depth, _ = gate.shape
    rows = depth // plane

    def kernel(info_ref, gate_ref, up_ref, *rest):
        out, held, in_sems, out_sems = rest

        def move(source):
            loads = [
                pltpu.make_async_copy(
                    source.at[
                        :,
                        pl.ds(part * rows, rows),
                        pl.ds(start, width),
                    ],
                    held.at[part],
                    in_sems.at[part],
                )
                for part in range(plane)
            ]
            stores = [
                pltpu.make_async_copy(held.at[part], out.at[part], out_sems.at[part])
                for part in range(plane)
            ]
            for load in loads:
                load.start()
            for load, store in zip(loads, stores):
                load.wait()
                store.start()
            for store in stores:
                store.wait()

        @pl.when(info_ref[2] == 0)
        def _():
            move(gate_ref)

        @pl.when(info_ref[2] != 0)
        def _():
            move(up_ref)

    return step_call(
        kernel,
        token,
        (info, gate, up),
        [SMEM, ANY, ANY],
        [jax.ShapeDtypeStruct((plane, sources, rows, width), gate.dtype)],
        [ANY],
        (0, 4 * sources * depth * width),
        scratch_shapes=[
            pltpu.VMEM((plane, sources, rows, width), gate.dtype),
            pltpu.SemaphoreType.DMA((plane,)),
            pltpu.SemaphoreType.DMA((plane,)),
        ],
        name="pack",
    )


def hold(token, value, earlier):
    def kernel(*refs):
        pass

    (value,), token = step_call(
        kernel,
        token,
        (value, *earlier),
        [ANY] * (1 + len(earlier)),
        [jax.ShapeDtypeStruct(value.shape, value.dtype)],
        [ANY],
        (0, 0),
        input_output_aliases={0: 0},
        name="hold",
    )
    return value, token


def merge(token, info, ids, weights, scales, near, far, received, start, scale_blocks):
    plane, sources, rows, width = near.shape
    step = math.gcd(rows, BLOCK)
    row_blocks, column_blocks = scale_blocks
    first = start // BLOCK

    def kernel(info_ref, ids_ref, weights_ref, scales_ref, near_ref, far_ref, *rest):
        total = rest[-1]
        place, inner = info_ref[0], info_ref[1]
        outer = jnp.where(inner == 1, 0, PLANES - 1)
        to_inner = inner if received is not None else PLANES - 1 - inner
        to_outer = outer if received is not None else PLANES - 1 - outer
        row_block = (place * rows + pl.program_id(0) * step) // BLOCK

        @pl.when(info_ref[3] == 1)
        def _():
            if received is None:
                total[...] = jnp.zeros_like(total)
            else:
                total[...] = rest[0][...].astype(jnp.float32)
            for block, held in ((near_ref, inner), (far_ref, outer)):
                for piece in range(plane):
                    for number in range(sources):
                        source = (held * plane + piece) * sources + number
                        target = ids_ref[source]
                        target_plane = target // plane
                        slot = target % plane

                        @pl.when((target_plane == to_inner) | (target_plane == to_outer))
                        def _():
                            index = jnp.where(target_plane == to_outer, plane, 0) + slot
                            base = (source * row_blocks + row_block) * column_blocks + first
                            for part in range(width // BLOCK):
                                lanes = pl.ds(part * BLOCK, BLOCK)
                                factor = weights_ref[source] * scales_ref[base + part]
                                total[index, :, lanes] += (
                                    block[piece, number, :, lanes].astype(jnp.float32) * factor
                                )

            if received is None:
                rest[0][...] = total[...].astype(jnp.bfloat16)
            else:
                rest[1][...] = total[:plane].astype(jnp.bfloat16)
                rest[2][...] = total[plane:].astype(jnp.bfloat16)

    pieces = pl.BlockSpec((plane, sources, step, width), lambda i: (0, 0, i, 0))
    both = pl.BlockSpec((2 * plane, step, width), lambda i: (0, i, 0))
    one = pl.BlockSpec((plane, step, width), lambda i: (0, i, 0))
    if received is None:
        extra, extra_specs = (), []
        out_shape = [jax.ShapeDtypeStruct((2 * plane, rows, width), jnp.bfloat16)]
        out_specs = [both]
    else:
        extra, extra_specs = (received,), [both]
        out_shape = [jax.ShapeDtypeStruct((plane, rows, width), jnp.bfloat16)] * 2
        out_specs = [one, one]
    return step_call(
        kernel,
        token,
        (info, ids, weights, scales, near, far, *extra),
        [SMEM] * 4 + [pieces, pieces] + extra_specs,
        out_shape,
        out_specs,
        (4 * near.size, 8 * near.size),
        grid=(rows // step,),
        scratch_shapes=[pltpu.VMEM((2 * plane, step, width), jnp.float32)],
        name="merge",
    )


def choose(token, info, inside, outside):
    def kernel(info_ref, inside_ref, outside_ref, out_ref, sem):
        def move(source):
            copy = pltpu.make_async_copy(source, out_ref, sem)
            copy.start()
            copy.wait()

        @pl.when(info_ref[3] == 1)
        def _():
            move(inside_ref)

        @pl.when(info_ref[3] != 1)
        def _():
            move(outside_ref)

    (rows,), token = step_call(
        kernel,
        token,
        (info, inside, outside),
        [SMEM, ANY, ANY],
        [jax.ShapeDtypeStruct(inside.shape, inside.dtype)],
        [VMEM],
        (0, 4 * inside.size),
        scratch_shapes=[pltpu.SemaphoreType.DMA],
        name="choose",
    )
    return rows, token


def pair(token, tokens, other):
    def kernel(tokens_ref, other_ref, out_ref):
        out_ref[0] = tokens_ref[...]
        out_ref[1] = other_ref[...]

    (both,), token = step_call(
        kernel,
        token,
        (tokens, other),
        [VMEM, VMEM],
        [jax.ShapeDtypeStruct((2,) + tokens.shape, tokens.dtype)],
        [VMEM],
        (0, 8 * tokens.size),
        name="pair",
    )
    return both, token


def line(token, info, tokens, other, crossed, forwarded):
    def kernel(info_ref, tokens_ref, other_ref, crossed_ref, forwarded_ref, out_ref):
        level = info_ref[1]
        low = level < PLANES // 2
        out_ref[level] = tokens_ref[...]
        out_ref[level ^ 1] = other_ref[...]

        def put(pair_ref):
            out_ref[jnp.where(low, 2, 1)] = pair_ref[0]
            out_ref[jnp.where(low, 3, 0)] = pair_ref[1]

        @pl.when(info_ref[3] == 1)
        def _():
            put(crossed_ref)

        @pl.when(info_ref[3] != 1)
        def _():
            put(forwarded_ref)

    (whole,), token = step_call(
        kernel,
        token,
        (info, tokens, other, crossed, forwarded),
        [SMEM] + [VMEM] * 4,
        [jax.ShapeDtypeStruct((PLANES,) + tokens.shape, tokens.dtype)],
        [VMEM],
        (0, 16 * tokens.size),
        name="line",
    )
    return whole, token


def run_chunk(token, info, grouped, own, partner, outputs, start, full, blocks):
    depth, width = own.shape
    count = grouped.shape[0]
    each = count // len(blocks)
    factor = 1.0 / math.sqrt(D)

    def kernel(info_ref, grouped_ref, own_ref, partner_ref, *rest):
        gate_out, up_out, hidden_ref, sems = rest[len(outputs) :]

        def work(gate_ref, up_ref):
            stores = [
                pltpu.make_async_copy(source, out.at[0, :, pl.ds(start, width)], sems.at[index])
                for index, (source, out) in enumerate(((gate_ref, gate_out), (up_ref, up_out)))
            ]
            for store in stores:
                store.start()
            rows = grouped_ref[...]
            gate_value = jnp.dot(rows, gate_ref[...], preferred_element_type=jnp.float32) * factor
            up_value = jnp.dot(rows, up_ref[...], preferred_element_type=jnp.float32) * factor
            hidden = (gate_value / (1.0 + jnp.exp(-gate_value)) * up_value).astype(jnp.bfloat16)
            for index, block in enumerate(blocks):
                hidden_ref[block] = hidden[index * each : (index + 1) * each]
            for store in stores:
                store.wait()

        @pl.when(info_ref[2] == 0)
        def _():
            work(own_ref, partner_ref)

        @pl.when(info_ref[2] != 0)
        def _():
            work(partner_ref, own_ref)

    weights = jax.ShapeDtypeStruct((1, depth, full), jnp.bfloat16)
    return step_call(
        kernel,
        token,
        (info, grouped, own, partner, *outputs),
        [SMEM, VMEM, VMEM, VMEM] + [ANY] * len(outputs),
        [weights, weights, jax.ShapeDtypeStruct((len(blocks), each, width), jnp.bfloat16)],
        [ANY, ANY, VMEM],
        (4 * count * depth * width, 2 * (grouped.size + 4 * depth * width)),
        scratch_shapes=[pltpu.SemaphoreType.DMA((2,))],
        input_output_aliases={4 + index: index for index in range(len(outputs))},
        name="run_chunk",
    )


STEPS = {
    "pair": (("t1",), (3.0, 0.0), (("t2", 13.0, "middle"),)),
    "line": (("t3",), (4.0, 0.0), ()),
    "pack": (("pack before",), (7.0, 0.6), (("b", 13.0, "y"),)),
    "send": (("b", "send before"), (2.0, 0.0), (("a", 25.0, "in"),)),
    "partial": (("a",), (5.0, 1.5), (("m", 25.0, "middle"),)),
    "finish": (("m",), (5.0, 2.0), (("d", 13.0, "out"),)),
    "choose": (("d",), (6.0, 0.5), (("e", 7.0, "y"),)),
    "trade": (("e",), (2.5, 0.0), (("x", 12.0, "x"),)),
    "run": (("x", "line", "run before"), (2.0, 1.5), ()),
}
ONCE = ("pair", "line")
LATENCY = 2.0
RETURN = 30.0
TRIES = 2500


def needs_of(name, chunk):
    needs = []
    for need in STEPS[name][0]:
        if need in ONCE or need[0] == "t":
            needs.append((need, 0))
        elif not need.endswith(" before"):
            needs.append((need, chunk))
        elif chunk > 0:
            needs.append((need[: -len(" before")], chunk - 1))
    return needs


def advance(now, until, links, done):
    while now < until:
        left = [min(load.values()) * len(load) for load in links.values() if load]
        span = min(left + [until - now])
        for load in links.values():
            for key in load:
                load[key] -= span / len(load)
        for load in links.values():
            for key in [key for key, rest in load.items() if rest <= 1e-6]:
                del load[key]
                done[key] = now + span + LATENCY
        now += span
    return now


def play(widths, order):
    links = {"in": {}, "middle": {}, "out": {}, "y": {}, "x": {}}
    done = {("t1", 0): 8.0}
    clock = 0.0
    now = 0.0
    for name, chunk in order:
        for need in needs_of(name, chunk):
            if need == ("t3", 0):
                need = ("t2", 0)
                extra = 16.0
            else:
                extra = 0.0
            while need not in done:
                clock = advance(clock, clock + 1.0, links, done)
            now = max(now, done[need] + extra)
        _, (fixed, each), sent = STEPS[name]
        while sent and sent[0][2] == "y" and links["y"]:
            clock = advance(clock, clock + 1.0, links, done)
            now = max(now, clock)
        width = 1 if name in ONCE else widths[chunk]
        now += fixed + each * width
        clock = advance(clock, max(clock, now), links, done)
        done[(name, chunk)] = now
        for what, cost, link in sent:
            links[link][(what, chunk)] = cost * width
    back = done[("run", max(0, len(widths) - 2))] + RETURN
    return max(now, back) + 0.02 * sum(done[("run", chunk)] for chunk in range(len(widths)))


def arrange(steps, rank):
    sender = {what: name for name, step in STEPS.items() for what, _, _ in step[2]}
    placed, order, left = set(), [], sorted(steps, key=lambda step: rank[step])
    while left:
        for step in left:
            needs = [(sender.get(n, n), c) for n, c in needs_of(*step) if n not in ("t1", "t3")]
            if step == ("line", 0):
                needs = [("pair", 0)]
            if all(need in placed for need in needs):
                break
        left.remove(step)
        placed.add(step)
        order.append(step)
    return order


def plan(widths):
    draw = random.Random(0)
    offset = dict(pack=0, send=20, partial=45, finish=75, choose=95, trade=110, run=125)
    rank = {(name, 0): value for name, value in zip(ONCE, (8, 25))}
    time = 0.0
    for chunk, width in enumerate(widths):
        for name, value in offset.items():
            rank[(name, chunk)] = time + value
        time += 27.0 * width
    steps = list(rank)
    order = arrange(steps, rank)
    best = (play(widths, order), order, rank)
    for _ in range(TRIES):
        trial = dict(best[2])
        for _ in range(draw.randint(1, 3)):
            trial[draw.choice(steps)] += draw.gauss(0.0, 15.0)
        order = arrange(steps, trial)
        end = play(widths, order)
        if end <= best[0]:
            best = (end, order, trial)
    return best[1]


def route_slots(routes, merged_count, tok_dev):
    experts = jnp.arange(merged_count, dtype=jnp.int32)
    hit_table = jnp.sum((routes[:, :, None] == experts).astype(jnp.int32), axis=1)
    hit_table = hit_table.reshape(-1, tok_dev, merged_count)
    position_lookup = jnp.cumsum(hit_table, axis=1) - hit_table
    return (hit_table, position_lookup)


def chunk_widths(blocks):
    if blocks < 6:
        return [1] * blocks
    return [1, 1, blocks - 4, 1, 1]


def shards(tokens, routes, quant_gate, quant_up, gate_scales, up_scales, cluster_ids, frequency):
    expert_count = lax.axis_size("expert")
    own_index = lax.axis_index("expert")
    group_count = lax.axis_size("groups")
    half = lax.axis_index("groups") % 2
    plane = expert_count // PLANES
    place, level = own_index % plane, own_index // plane
    is_inner = (level == 1) | (level == 2)
    depth, full = quant_gate.shape[1:]
    tok_dev = tokens.shape[0]
    top_count = routes.shape[1]
    capacity = min(tok_dev, 2 * tok_dev * top_count // expert_count)

    def send(value, pairs):
        wires = [(a * plane + p, b * plane + p) for a, b in pairs for p in range(plane)]
        return lax.ppermute(value, "expert", wires)

    def exchange(pieces):
        return lax.all_to_all(pieces, "expert", 0, 0, tiled=True, axis_index_groups=by_plane)

    inward = [(0, 1), (3, 2)]
    outward = [(1, 0), (2, 3)]
    across = [(1, 2), (2, 1)]
    by_plane = [[z * plane + p for p in range(plane)] for z in range(PLANES)]
    partners = [(g, g ^ 1) for g in range(group_count)]

    info = jnp.stack([place, level, half, is_inner.astype(jnp.int32)]).astype(jnp.int32)
    ids = cluster_ids[:, 0]
    weights = cluster_weights(cluster_ids, frequency)
    scales = jnp.where(half == 0, gate_scales, up_scales)
    scale_blocks = scales.shape[1:]
    scales = scales.reshape(-1)

    hit_table, position_lookup = route_slots(routes, expert_count, tok_dev)
    positions = jnp.arange(capacity, dtype=jnp.int32)

    blocks = [z * plane + p for p in range(plane) for z in range(PLANES)]

    def in_blocks(table):
        column = lax.dynamic_index_in_dim(table, own_index, 2, keepdims=False)
        column = column.reshape(PLANES, plane, tok_dev).transpose(1, 0, 2)
        return column.reshape(expert_count, 1, tok_dev)

    placing = (
        (in_blocks(hit_table) == 1) & (in_blocks(position_lookup) == positions[None, :, None])
    ).astype(jnp.bfloat16)

    experts = jnp.arange(expert_count, dtype=jnp.int32)
    local_routes = lax.dynamic_slice_in_dim(routes, own_index * tok_dev, tok_dev, 0)
    own_slots = lax.dynamic_index_in_dim(position_lookup, own_index, 0, keepdims=False)
    chosen = local_routes[:, :, None] == experts
    slot_of = jnp.sum(jnp.where(chosen, own_slots[:, None, :], 0), axis=2)
    picking = (chosen[:, :, :, None] & (slot_of[:, :, None, None] == positions)).astype(
        jnp.bfloat16
    )
    picking = picking.reshape(tok_dev * top_count, expert_count * capacity)

    widths = chunk_widths(full // BLOCK)
    starts = [BLOCK * sum(widths[:chunk]) for chunk in range(len(widths))]
    token = jnp.zeros(TOKEN.shape, TOKEN.dtype)
    neighbour = send(tokens, inward + outward)
    near, far, received, inside, outside, own, partner, hiddens = ({} for _ in range(8))
    outputs = ()
    for name, c in plan(widths):
        start, width = starts[c], widths[c] * BLOCK
        if name == "pair":
            both, token = pair(token, tokens, neighbour)
            crossed = send(both, across)
            forwarded = send(crossed, outward)
        elif name == "line":
            whole, token = line(token, info, tokens, neighbour, crossed, forwarded)
            everyone = lax.all_gather(whole, "expert", axis=0, tiled=True, axis_index_groups=by_plane)
            arrived = jnp.einsum(
                "jct,jtd->jcd", placing, everyone, preferred_element_type=jnp.float32
            ).astype(jnp.bfloat16)
            arrived = lax.all_gather(arrived, "mp", axis=2, tiled=True)
            grouped = arrived.reshape(expert_count * capacity, depth)
        elif name == "pack":
            (pieces,), token = pack(token, info, quant_gate, quant_up, start, width, plane)
            near[c] = exchange(pieces)
        elif name == "send":
            near[c], token = hold(token, near[c], [])
            far[c] = send(near[c], inward)
        elif name == "partial":
            (partial,), token = merge(
                token, info, ids, weights, scales, near[c], far[c], None, start, scale_blocks
            )
            received[c] = send(partial, across)
        elif name == "finish":
            (inside[c], outward_rows), token = merge(
                token, info, ids, weights, scales, near[c], far[c], received[c], start, scale_blocks
            )
            outside[c] = send(outward_rows, outward)
        elif name == "choose":
            rows, token = choose(token, info, inside[c], outside[c])
            own[c] = exchange(rows)
        elif name == "trade":
            own[c], token = hold(token, own[c].reshape(depth, width), [])
            partner[c] = lax.ppermute(own[c], "groups", partners)
        else:
            (*outputs, hiddens[c]), token = run_chunk(
                token, info, grouped, own[c], partner[c], outputs, start, full, blocks
            )

    last = len(widths) - 1
    finished = []
    for batch in (range(last), range(last, last + 1)):
        hidden = jnp.concatenate([hiddens[c] for c in batch], axis=2)
        returned = lax.all_to_all(hidden, "expert", split_axis=0, concat_axis=0, tiled=True)
        rows = returned.reshape(expert_count * capacity, returned.shape[2])
        finished.append(
            jnp.dot(picking, rows, preferred_element_type=jnp.float32).astype(jnp.bfloat16)
        )
    output = jnp.concatenate(finished, axis=1)
    merged_gate, merged_up = outputs
    return (merged_gate, merged_up, output.reshape(tok_dev, top_count, full))


def solution(mesh):
    return jax.shard_map(
        shards,
        mesh=mesh,
        in_specs=(
            P(("groups", "expert"), "mp"),
            P("groups", None),
            P("expert", None, "mp"),
            P("expert", None, "mp"),
            P(None, None, "mp"),
            P(None, None, "mp"),
            P(),
            P(),
        ),
        out_specs=(
            P(("groups", "expert"), None, "mp"),
            P(("groups", "expert"), None, "mp"),
            P(("groups", "expert"), None, "mp"),
        ),
        check_vma=False,
    )
```

```python
import math

import jax
import jax.numpy as jnp
from jax import lax
from jax.experimental import pallas as pl
from jax.experimental.pallas import tpu as pltpu
from jax.sharding import PartitionSpec as P

D = 2560
BLOCK = 128
PLANES = 4
TOKEN = jax.ShapeDtypeStruct((8, 128), jnp.float32)
ANY = pl.BlockSpec(memory_space=pl.ANY)
SMEM = pl.BlockSpec(memory_space=pltpu.SMEM)
VMEM = pl.BlockSpec(memory_space=pltpu.VMEM)
VMEM_LIMIT = 60 * 1024 * 1024


def cluster_weights(cluster_ids, frequency):
    ids = cluster_ids[:, 0]
    same = (ids[:, None] == ids[None, :]).astype(jnp.float32)
    return frequency / jnp.sum(same * frequency[None, :], axis=1)


def step_call(kernel, token, operands, in_specs, out_shape, out_specs, **options):
    count = len(operands)

    def ordered(*refs):
        kernel(*refs[:count], *refs[count + 1 : count + 1 + len(out_shape)], *refs[count + 2 + len(out_shape) :])

    *results, token = pl.pallas_call(
        ordered,
        out_shape=[*out_shape, TOKEN],
        in_specs=[*in_specs, ANY],
        out_specs=[*out_specs, ANY],
        compiler_params=pltpu.CompilerParams(vmem_limit_bytes=VMEM_LIMIT),
        cost_estimate=pl.CostEstimate(flops=0, bytes_accessed=0, transcendentals=0),
        **options,
    )(*operands, token)
    return results, token


def pack(token, info, gate, up, start, width, devices):
    sources, depth, _ = gate.shape
    rows = depth // devices

    def kernel(info_ref, gate_ref, up_ref, *rest):
        out, held, in_sems, out_sems = rest

        def move(source):
            loads = [
                pltpu.make_async_copy(
                    source.at[
                        :,
                        pl.ds(part * rows, rows),
                        pl.ds(start, width),
                    ],
                    held.at[part],
                    in_sems.at[part],
                )
                for part in range(devices)
            ]
            stores = [
                pltpu.make_async_copy(held.at[part], out.at[part], out_sems.at[part])
                for part in range(devices)
            ]
            for load in loads:
                load.start()
            for load, store in zip(loads, stores):
                load.wait()
                store.start()
            for store in stores:
                store.wait()

        @pl.when(info_ref[1] == 0)
        def _():
            move(gate_ref)

        @pl.when(info_ref[1] != 0)
        def _():
            move(up_ref)

    return step_call(
        kernel,
        token,
        (info, gate, up),
        [SMEM, ANY, ANY],
        [jax.ShapeDtypeStruct((devices, sources, rows, width), gate.dtype)],
        [ANY],
        scratch_shapes=[
            pltpu.VMEM((devices, sources, rows, width), gate.dtype),
            pltpu.SemaphoreType.DMA((devices,)),
            pltpu.SemaphoreType.DMA((devices,)),
        ],
        name="pack",
    )


def hold(token, value, earlier):
    def kernel(*refs):
        pass

    (value,), token = step_call(
        kernel,
        token,
        (value, *earlier),
        [ANY] * (1 + len(earlier)),
        [jax.ShapeDtypeStruct(value.shape, value.dtype)],
        [ANY],
        input_output_aliases={0: 0},
        name="hold",
    )
    return value, token


def merge(token, slots, factors, rows_of, received, start, blocks):
    devices, sources, rows, width = rows_of.shape
    steps, column_blocks = blocks
    step = rows // steps
    first = start // BLOCK
    base_slot = 0 if received is None else devices * sources

    def kernel(slots_ref, factors_ref, rows_ref, *rest):
        out_ref, total = rest[-2:]
        piece = pl.program_id(0)

        @pl.when(piece == 0)
        def _():
            if received is None:
                total[...] = jnp.zeros_like(total)
            else:
                total[...] = rest[0][...].astype(jnp.float32)

        for number in range(sources):
            source = piece * sources + number
            slot = slots_ref[base_slot + source]

            @pl.when(slot >= 0)
            def _():
                for index in range(steps):
                    for part in range(width // BLOCK):
                        base = (source * steps + index) * column_blocks + first
                        lanes = slice(part * BLOCK, (part + 1) * BLOCK)
                        place = slice(index * step, (index + 1) * step)
                        total[slot, place, lanes] += (
                            rows_ref[0, number, place, lanes].astype(jnp.float32)
                            * factors_ref[base + part]
                        )

        @pl.when(piece == devices - 1)
        def _():
            out_ref[...] = total[...].astype(jnp.bfloat16)

    whole = pl.BlockSpec((devices, rows, width), lambda i: (0, 0, 0))
    extra = () if received is None else (received,)
    (merged,), token = step_call(
        kernel,
        token,
        (slots, factors, rows_of, *extra),
        [SMEM, SMEM, pl.BlockSpec((1, sources, rows, width), lambda i: (i, 0, 0, 0))]
        + [whole] * len(extra),
        [jax.ShapeDtypeStruct((devices, rows, width), jnp.bfloat16)],
        [whole],
        grid=(devices,),
        scratch_shapes=[pltpu.VMEM((devices, rows, width), jnp.float32)],
        name="merge",
    )
    return merged, token


def pair(token, tokens, other):
    def kernel(tokens_ref, other_ref, out_ref):
        out_ref[0] = tokens_ref[...]
        out_ref[1] = other_ref[...]

    (both,), token = step_call(
        kernel,
        token,
        (tokens, other),
        [VMEM, VMEM],
        [jax.ShapeDtypeStruct((2,) + tokens.shape, tokens.dtype)],
        [VMEM],
        name="pair",
    )
    return both, token


def line(token, info, both, nearby, tables):
    _, tok_dev, width = both.shape

    def kernel(info_ref, both_ref, nearby_ref, *rest):
        out_ref = rest[len(tables)]
        level = info_ref[0]
        for index, other in enumerate((both_ref, nearby_ref)):
            out_ref[level ^ index] = other[0]
            out_ref[level ^ index ^ (PLANES // 2)] = other[1]

    (whole,), _ = step_call(
        kernel,
        token,
        (info, both, nearby, *tables),
        [SMEM] + [VMEM] * 2 + [ANY] * len(tables),
        [jax.ShapeDtypeStruct((PLANES, tok_dev, width), both.dtype)],
        [VMEM],
        name="line",
    )
    return whole


def run_chunk(token, info, grouped, own, partner, outputs, start, full, blocks):
    depth, width = own.shape
    count = grouped.shape[0]
    each = count // len(blocks)
    factor = 1.0 / math.sqrt(D)

    def kernel(info_ref, grouped_ref, own_ref, partner_ref, *rest):
        gate_out, up_out, hidden_ref, whole, in_sems, out_sems = rest[len(outputs) :]
        halves = [whole.at[:, pl.ds(index * width, width)] for index in range(2)]

        def fill(*sources):
            loads = [
                pltpu.make_async_copy(source, half, in_sems.at[index])
                for index, (source, half) in enumerate(zip(sources, halves))
            ]
            for load in loads:
                load.start()
            for load in loads:
                load.wait()

        @pl.when(info_ref[1] == 0)
        def _():
            fill(own_ref, partner_ref)

        @pl.when(info_ref[1] != 0)
        def _():
            fill(partner_ref, own_ref)

        stores = [
            pltpu.make_async_copy(half, out.at[0, :, pl.ds(start, width)], out_sems.at[index])
            for index, (half, out) in enumerate(zip(halves, (gate_out, up_out)))
        ]
        for store in stores:
            store.start()
        values = jnp.dot(grouped_ref[...], whole[...], preferred_element_type=jnp.float32)
        gate_value = values[:, :width] * factor
        up_value = values[:, width:] * factor
        hidden = (gate_value / (1.0 + jnp.exp(-gate_value)) * up_value).astype(jnp.bfloat16)
        for index, block in enumerate(blocks):
            hidden_ref[block] = hidden[index * each : (index + 1) * each]
        for store in stores:
            store.wait()

    weights = jax.ShapeDtypeStruct((1, depth, full), jnp.bfloat16)
    return step_call(
        kernel,
        token,
        (info, grouped, own, partner, *outputs),
        [SMEM, VMEM, ANY, ANY] + [ANY] * len(outputs),
        [weights, weights, jax.ShapeDtypeStruct((len(blocks), each, width), jnp.bfloat16)],
        [ANY, ANY, VMEM],
        scratch_shapes=[
            pltpu.VMEM((depth, 2 * width), jnp.bfloat16),
            pltpu.SemaphoreType.DMA((2,)),
            pltpu.SemaphoreType.DMA((2,)),
        ],
        input_output_aliases={4 + index: index for index in range(len(outputs))},
        name="run_chunk",
    )


def plan(count):
    order = [("pack", 0), ("pair", 0)]
    for chunk in range(count):
        if chunk + 1 < count:
            order.append(("pack", chunk + 1))
        order.append(("partial", chunk))
        if chunk == 0:
            order.append(("line", 0))
        if chunk >= 2:
            order.extend([("finish", chunk - 2), ("trade", chunk - 2)])
    for chunk in range(max(0, count - 2), count):
        order.extend([("finish", chunk), ("trade", chunk)])
    for chunk in range(count):
        place = order.index(("trade", chunk))
        later = [i for i, (name, _) in enumerate(order) if i > place and name in ("partial", "trade")]
        order.insert(later[0] + 1 if later else len(order), ("run", chunk))
    return order


def route_slots(routes, merged_count, tok_dev):
    experts = jnp.arange(merged_count, dtype=jnp.int32)
    hit_table = jnp.sum((routes[:, :, None] == experts).astype(jnp.int32), axis=1)
    hit_table = hit_table.reshape(-1, tok_dev, merged_count)
    position_lookup = jnp.cumsum(hit_table, axis=1) - hit_table
    return (hit_table, position_lookup)


def chunk_widths(blocks):
    if blocks < 4:
        return [1] * blocks
    middle, odd = divmod(blocks - 2, 2)
    return [1] + [2] * middle + [1] * odd + [1]


def shards(tokens, routes, quant_gate, quant_up, gate_scales, up_scales, cluster_ids, frequency):
    expert_count = lax.axis_size("expert")
    own_index = lax.axis_index("expert")
    group_count = lax.axis_size("groups")
    half = lax.axis_index("groups") % 2
    plane = expert_count // PLANES
    level = own_index // plane
    halfway = expert_count // 2
    side, place = own_index // halfway, own_index % halfway
    depth, full = quant_gate.shape[1:]
    tok_dev = tokens.shape[0]
    top_count = routes.shape[1]
    capacity = min(tok_dev, 2 * tok_dev * top_count // expert_count)

    by_plane = [[z * plane + p for p in range(plane)] for z in range(PLANES)]
    by_half = [[part * halfway + i for i in range(halfway)] for part in range(2)]
    across = [(i, (i + halfway) % expert_count) for i in range(expert_count)]
    beside = [(i, (i // plane ^ 1) * plane + i % plane) for i in range(expert_count)]
    partners = [(g, g ^ 1) for g in range(group_count)]

    def exchange(pieces):
        return lax.all_to_all(pieces, "expert", 0, 0, tiled=True, axis_index_groups=by_half)

    info = jnp.stack([level, half]).astype(jnp.int32)
    sources = quant_gate.shape[0]
    rows = depth // halfway
    step = math.gcd(rows, BLOCK)
    held = side * halfway * sources + jnp.arange(halfway * sources, dtype=jnp.int32)
    target = jnp.take(cluster_ids[:, 0], held)
    slots = jnp.concatenate(
        [
            jnp.where(target // halfway != side, target % halfway, -1),
            jnp.where(target // halfway == side, target % halfway, -1),
        ]
    )
    weights = jnp.take(cluster_weights(cluster_ids, frequency), held)
    scales = jnp.take(jnp.where(half == 0, gate_scales, up_scales), held, axis=0)
    row_blocks = (place * rows + step * jnp.arange(rows // step, dtype=jnp.int32)) // BLOCK
    factors = jnp.take(scales, row_blocks, axis=1) * weights[:, None, None]
    blocks_of_rows = factors.shape[1:]
    factors = factors.reshape(-1)

    hit_table, position_lookup = route_slots(routes, expert_count, tok_dev)
    positions = jnp.arange(capacity, dtype=jnp.int32)

    blocks = [z * plane + p for p in range(plane) for z in range(PLANES)]

    def in_blocks(table):
        column = lax.dynamic_index_in_dim(table, own_index, 2, keepdims=False)
        column = column.reshape(PLANES, plane, tok_dev).transpose(1, 0, 2)
        return column.reshape(expert_count, 1, tok_dev)

    placing = (
        (in_blocks(hit_table) == 1) & (in_blocks(position_lookup) == positions[None, :, None])
    ).astype(jnp.bfloat16)

    experts = jnp.arange(expert_count, dtype=jnp.int32)
    local_routes = lax.dynamic_slice_in_dim(routes, own_index * tok_dev, tok_dev, 0)
    own_slots = lax.dynamic_index_in_dim(position_lookup, own_index, 0, keepdims=False)
    chosen = local_routes[:, :, None] == experts
    slot_of = jnp.sum(jnp.where(chosen, own_slots[:, None, :], 0), axis=2)
    picking = (chosen[:, :, :, None] & (slot_of[:, :, None, None] == positions)).astype(
        jnp.bfloat16
    )
    picking = picking.reshape(tok_dev * top_count, expert_count * capacity)

    widths = chunk_widths(full // BLOCK)
    starts = [BLOCK * sum(widths[:chunk]) for chunk in range(len(widths))]
    token = jnp.zeros(TOKEN.shape, TOKEN.dtype)
    opposite = lax.ppermute(tokens, "expert", across)
    gathered, received, own, partner, hiddens = ({} for _ in range(5))
    outputs = ()
    for name, c in plan(len(widths)):
        start, width = starts[c], widths[c] * BLOCK
        if name == "pair":
            both, token = pair(token, tokens, opposite)
            nearby = lax.ppermute(both, "expert", beside)
        elif name == "line":
            whole = line(token, info, both, nearby, (placing, picking))
            everyone = lax.all_gather(whole, "expert", axis=0, tiled=True, axis_index_groups=by_plane)
            arrived = jnp.einsum(
                "jct,jtd->jcd", placing, everyone, preferred_element_type=jnp.float32
            ).astype(jnp.bfloat16)
            arrived = lax.all_gather(arrived, "mp", axis=2, tiled=True)
            grouped = arrived.reshape(expert_count * capacity, depth)
        elif name == "pack":
            (pieces,), token = pack(token, info, quant_gate, quant_up, start, width, halfway)
            gathered[c] = exchange(pieces)
        elif name == "partial":
            partial, token = merge(token, slots, factors, gathered[c], None, start, blocks_of_rows)
            received[c] = lax.ppermute(partial, "expert", across)
        elif name == "finish":
            merged, token = merge(
                token, slots, factors, gathered[c], received[c], start, blocks_of_rows
            )
            own[c] = exchange(merged)
        elif name == "trade":
            own[c], token = hold(token, own[c].reshape(depth, width), [])
            partner[c] = lax.ppermute(own[c], "groups", partners)
        else:
            (*outputs, hiddens[c]), token = run_chunk(
                token, info, grouped, own[c], partner[c], outputs, start, full, blocks
            )

    last = len(widths) - 1
    finished = []
    before = []
    for batch in (range(last), range(last, last + 1)):
        hidden = jnp.concatenate([hiddens[c] for c in batch], axis=2)
        hidden, token = hold(token, hidden, before)
        returned = lax.all_to_all(hidden, "expert", split_axis=0, concat_axis=0, tiled=True)
        before = [returned]
        rows = returned.reshape(expert_count * capacity, returned.shape[2])
        finished.append(
            jnp.dot(picking, rows, preferred_element_type=jnp.float32).astype(jnp.bfloat16)
        )
    output = jnp.concatenate(finished, axis=1)
    merged_gate, merged_up = outputs
    return (merged_gate, merged_up, output.reshape(tok_dev, top_count, full))


def solution(mesh):
    return jax.shard_map(
        shards,
        mesh=mesh,
        in_specs=(
            P(("groups", "expert"), "mp"),
            P("groups", None),
            P("expert", None, "mp"),
            P("expert", None, "mp"),
            P(None, None, "mp"),
            P(None, None, "mp"),
            P(),
            P(),
        ),
        out_specs=(
            P(("groups", "expert"), None, "mp"),
            P(("groups", "expert"), None, "mp"),
            P(("groups", "expert"), None, "mp"),
        ),
        check_vma=False,
    )
```

```python
import math

import jax
import jax.numpy as jnp
from jax import lax
from jax.experimental import pallas as pl
from jax.experimental.pallas import tpu as pltpu
from jax.sharding import PartitionSpec as P

D = 2560
BLOCK = 128
PLANES = 4
TOKEN = jax.ShapeDtypeStruct((8, 128), jnp.float32)
ANY = pl.BlockSpec(memory_space=pl.ANY)
SMEM = pl.BlockSpec(memory_space=pltpu.SMEM)
VMEM = pl.BlockSpec(memory_space=pltpu.VMEM)
VMEM_LIMIT = 60 * 1024 * 1024


def cluster_weights(cluster_ids, frequency):
    ids = cluster_ids[:, 0]
    same = (ids[:, None] == ids[None, :]).astype(jnp.float32)
    return frequency / jnp.sum(same * frequency[None, :], axis=1)


def step_call(kernel, token, operands, in_specs, out_shape, out_specs, **options):
    count = len(operands)

    def ordered(*refs):
        kernel(*refs[:count], *refs[count + 1 : count + 1 + len(out_shape)], *refs[count + 2 + len(out_shape) :])

    *results, token = pl.pallas_call(
        ordered,
        out_shape=[*out_shape, TOKEN],
        in_specs=[*in_specs, ANY],
        out_specs=[*out_specs, ANY],
        compiler_params=pltpu.CompilerParams(vmem_limit_bytes=VMEM_LIMIT),
        cost_estimate=pl.CostEstimate(flops=0, bytes_accessed=0, transcendentals=0),
        **options,
    )(*operands, token)
    return results, token


def pack(token, info, gate, up, start, width, devices):
    sources, depth, _ = gate.shape
    rows = depth // devices

    def kernel(info_ref, gate_ref, up_ref, *rest):
        out, held, in_sems, out_sems = rest

        def move(source):
            loads = [
                pltpu.make_async_copy(
                    source.at[
                        :,
                        pl.ds(part * rows, rows),
                        pl.ds(start, width),
                    ],
                    held.at[part],
                    in_sems.at[part],
                )
                for part in range(devices)
            ]
            stores = [
                pltpu.make_async_copy(held.at[part], out.at[part], out_sems.at[part])
                for part in range(devices)
            ]
            for load in loads:
                load.start()
            for load, store in zip(loads, stores):
                load.wait()
                store.start()
            for store in stores:
                store.wait()

        @pl.when(info_ref[1] == 0)
        def _():
            move(gate_ref)

        @pl.when(info_ref[1] != 0)
        def _():
            move(up_ref)

    return step_call(
        kernel,
        token,
        (info, gate, up),
        [SMEM, ANY, ANY],
        [jax.ShapeDtypeStruct((devices, sources, rows, width), gate.dtype)],
        [ANY],
        scratch_shapes=[
            pltpu.VMEM((devices, sources, rows, width), gate.dtype),
            pltpu.SemaphoreType.DMA((devices,)),
            pltpu.SemaphoreType.DMA((devices,)),
        ],
        name="pack",
    )


def hold(token, value, earlier):
    def kernel(*refs):
        pass

    (value,), token = step_call(
        kernel,
        token,
        (value, *earlier),
        [ANY] * (1 + len(earlier)),
        [jax.ShapeDtypeStruct(value.shape, value.dtype)],
        [ANY],
        input_output_aliases={0: 0},
        name="hold",
    )
    return value, token


def merge(token, slots, factors, rows_of, received, start, blocks):
    devices, sources, rows, width = rows_of.shape
    steps, column_blocks = blocks
    step = rows // steps
    first = start // BLOCK
    base_slot = 0 if received is None else devices * sources

    middle = devices // 2
    halves = (slice(0, middle), slice(middle, devices))

    def kernel(slots_ref, factors_ref, rows_ref, *rest):
        total = rest[-1]
        piece = pl.program_id(0)

        @pl.when(piece == 0)
        def _():
            if received is None:
                total[...] = jnp.zeros_like(total)
            else:
                for part, share in enumerate(halves):
                    total[share] = rest[part][...].astype(jnp.float32)

        for number in range(sources):
            source = piece * sources + number
            slot = slots_ref[base_slot + source]

            @pl.when(slot >= 0)
            def _():
                for index in range(steps):
                    for part in range(width // BLOCK):
                        base = (source * steps + index) * column_blocks + first
                        lanes = slice(part * BLOCK, (part + 1) * BLOCK)
                        place = slice(index * step, (index + 1) * step)
                        total[slot, place, lanes] += (
                            rows_ref[0, number, place, lanes].astype(jnp.float32)
                            * factors_ref[base + part]
                        )

        @pl.when(piece == devices - 1)
        def _():
            if received is None:
                for part, share in enumerate(halves):
                    rest[part][...] = total[share].astype(jnp.bfloat16)
            else:
                rest[2][...] = total[...].astype(jnp.bfloat16)

    whole = pl.BlockSpec((devices, rows, width), lambda i: (0, 0, 0))
    half = pl.BlockSpec((middle, rows, width), lambda i: (0, 0, 0))
    extra = () if received is None else tuple(received)
    out_count = 2 if received is None else 1
    return step_call(
        kernel,
        token,
        (slots, factors, rows_of, *extra),
        [SMEM, SMEM, pl.BlockSpec((1, sources, rows, width), lambda i: (i, 0, 0, 0))]
        + [half] * len(extra),
        [jax.ShapeDtypeStruct((devices // out_count, rows, width), jnp.bfloat16)] * out_count,
        [whole] if received is not None else [half, half],
        grid=(devices,),
        scratch_shapes=[pltpu.VMEM((devices, rows, width), jnp.float32)],
        name="merge",
    )


def pair(token, tokens, other):
    def kernel(tokens_ref, other_ref, out_ref):
        out_ref[0] = tokens_ref[...]
        out_ref[1] = other_ref[...]

    (both,), token = step_call(
        kernel,
        token,
        (tokens, other),
        [VMEM, VMEM],
        [jax.ShapeDtypeStruct((2,) + tokens.shape, tokens.dtype)],
        [VMEM],
        name="pair",
    )
    return both, token


def line(token, info, both, nearby, tables):
    _, tok_dev, width = both.shape

    def kernel(info_ref, both_ref, nearby_ref, *rest):
        out_ref = rest[len(tables)]
        level = info_ref[0]
        for index, other in enumerate((both_ref, nearby_ref)):
            out_ref[level ^ index] = other[0]
            out_ref[level ^ index ^ (PLANES // 2)] = other[1]

    (whole,), _ = step_call(
        kernel,
        token,
        (info, both, nearby, *tables),
        [SMEM] + [VMEM] * 2 + [ANY] * len(tables),
        [jax.ShapeDtypeStruct((PLANES, tok_dev, width), both.dtype)],
        [VMEM],
        name="line",
    )
    return whole


def run_chunk(token, info, grouped, own, partner, outputs, start, full, blocks):
    depth, width = own.shape
    count = grouped.shape[0]
    each = count // len(blocks)
    factor = 1.0 / math.sqrt(D)

    def kernel(info_ref, grouped_ref, own_ref, partner_ref, *rest):
        gate_out, up_out, hidden_ref, whole, in_sems, out_sems = rest[len(outputs) :]
        halves = [whole.at[:, pl.ds(index * width, width)] for index in range(2)]

        def fill(*sources):
            loads = [
                pltpu.make_async_copy(source, half, in_sems.at[index])
                for index, (source, half) in enumerate(zip(sources, halves))
            ]
            for load in loads:
                load.start()
            for load in loads:
                load.wait()

        @pl.when(info_ref[1] == 0)
        def _():
            fill(own_ref, partner_ref)

        @pl.when(info_ref[1] != 0)
        def _():
            fill(partner_ref, own_ref)

        stores = [
            pltpu.make_async_copy(half, out.at[0, :, pl.ds(start, width)], out_sems.at[index])
            for index, (half, out) in enumerate(zip(halves, (gate_out, up_out)))
        ]
        for store in stores:
            store.start()
        values = jnp.dot(grouped_ref[...], whole[...], preferred_element_type=jnp.float32)
        gate_value = values[:, :width] * factor
        up_value = values[:, width:] * factor
        hidden = (gate_value / (1.0 + jnp.exp(-gate_value)) * up_value).astype(jnp.bfloat16)
        for index, block in enumerate(blocks):
            hidden_ref[block] = hidden[index * each : (index + 1) * each]
        for store in stores:
            store.wait()

    weights = jax.ShapeDtypeStruct((1, depth, full), jnp.bfloat16)
    return step_call(
        kernel,
        token,
        (info, grouped, own, partner, *outputs),
        [SMEM, VMEM, ANY, ANY] + [ANY] * len(outputs),
        [weights, weights, jax.ShapeDtypeStruct((len(blocks), each, width), jnp.bfloat16)],
        [ANY, ANY, VMEM],
        scratch_shapes=[
            pltpu.VMEM((depth, 2 * width), jnp.bfloat16),
            pltpu.SemaphoreType.DMA((2,)),
            pltpu.SemaphoreType.DMA((2,)),
        ],
        input_output_aliases={4 + index: index for index in range(len(outputs))},
        name="run_chunk",
    )


def plan(count):
    order = [("pack", 0)]
    for chunk in range(count + 1):
        if chunk + 1 < count:
            order.append(("pack", chunk + 1))
        if chunk >= 2:
            order.append(("trade", chunk - 2))
        if chunk < count:
            order.append(("partial", chunk))
        if chunk == 0:
            order.append(("pair", 0))
        if chunk == 1:
            order.append(("line", 0))
        if chunk >= 1:
            order.append(("finish", chunk - 1))
        if chunk >= 3:
            order.append(("run", chunk - 3))
        if chunk >= 1:
            order.append(("back", chunk - 1))
    order.append(("run", count - 2))
    order.append(("trade", count - 1))
    order.append(("give", 0))
    order.append(("run", count - 1))
    order.append(("give", 1))
    return order


def route_slots(routes, merged_count, tok_dev):
    experts = jnp.arange(merged_count, dtype=jnp.int32)
    hit_table = jnp.sum((routes[:, :, None] == experts).astype(jnp.int32), axis=1)
    hit_table = hit_table.reshape(-1, tok_dev, merged_count)
    position_lookup = jnp.cumsum(hit_table, axis=1) - hit_table
    return (hit_table, position_lookup)


def chunk_widths(blocks):
    if blocks < 4:
        return [1] * blocks
    middle, odd = divmod(blocks - 2, 2)
    return [1] + [2] * middle + [1] * odd + [1]


def shards(tokens, routes, quant_gate, quant_up, gate_scales, up_scales, cluster_ids, frequency):
    expert_count = lax.axis_size("expert")
    own_index = lax.axis_index("expert")
    group_count = lax.axis_size("groups")
    half = lax.axis_index("groups") % 2
    plane = expert_count // PLANES
    level = own_index // plane
    halfway = expert_count // 2
    side, place = own_index // halfway, own_index % halfway
    depth, full = quant_gate.shape[1:]
    tok_dev = tokens.shape[0]
    top_count = routes.shape[1]
    capacity = min(tok_dev, 2 * tok_dev * top_count // expert_count)

    by_plane = [[z * plane + p for p in range(plane)] for z in range(PLANES)]
    by_half = [[part * halfway + i for i in range(halfway)] for part in range(2)]
    across = [(i, (i + halfway) % expert_count) for i in range(expert_count)]
    beside = [(i, (i // plane ^ 1) * plane + i % plane) for i in range(expert_count)]
    partners = [(g, g ^ 1) for g in range(group_count)]

    def exchange(pieces):
        return lax.all_to_all(pieces, "expert", 0, 0, tiled=True, axis_index_groups=by_half)

    info = jnp.stack([level, half]).astype(jnp.int32)
    sources = quant_gate.shape[0]
    rows = depth // halfway
    step = math.gcd(rows, BLOCK)
    held = side * halfway * sources + jnp.arange(halfway * sources, dtype=jnp.int32)
    target = jnp.take(cluster_ids[:, 0], held)
    slots = jnp.concatenate(
        [
            jnp.where(target // halfway != side, target % halfway, -1),
            jnp.where(target // halfway == side, target % halfway, -1),
        ]
    )
    weights = jnp.take(cluster_weights(cluster_ids, frequency), held)
    scales = jnp.take(jnp.where(half == 0, gate_scales, up_scales), held, axis=0)
    row_blocks = (place * rows + step * jnp.arange(rows // step, dtype=jnp.int32)) // BLOCK
    factors = jnp.take(scales, row_blocks, axis=1) * weights[:, None, None]
    blocks_of_rows = factors.shape[1:]
    factors = factors.reshape(-1)

    hit_table, position_lookup = route_slots(routes, expert_count, tok_dev)
    positions = jnp.arange(capacity, dtype=jnp.int32)

    blocks = [z * plane + p for p in range(plane) for z in range(PLANES)]

    def in_blocks(table):
        column = lax.dynamic_index_in_dim(table, own_index, 2, keepdims=False)
        column = column.reshape(PLANES, plane, tok_dev).transpose(1, 0, 2)
        return column.reshape(expert_count, 1, tok_dev)

    placing = (
        (in_blocks(hit_table) == 1) & (in_blocks(position_lookup) == positions[None, :, None])
    ).astype(jnp.bfloat16)

    experts = jnp.arange(expert_count, dtype=jnp.int32)
    local_routes = lax.dynamic_slice_in_dim(routes, own_index * tok_dev, tok_dev, 0)
    own_slots = lax.dynamic_index_in_dim(position_lookup, own_index, 0, keepdims=False)
    chosen = local_routes[:, :, None] == experts
    slot_of = jnp.sum(jnp.where(chosen, own_slots[:, None, :], 0), axis=2)
    picking = (chosen[:, :, :, None] & (slot_of[:, :, None, None] == positions)).astype(
        jnp.bfloat16
    )
    picking = picking.reshape(tok_dev * top_count, expert_count * capacity)

    widths = chunk_widths(full // BLOCK)
    starts = [BLOCK * sum(widths[:chunk]) for chunk in range(len(widths))]
    token = jnp.zeros(TOKEN.shape, TOKEN.dtype)
    opposite = lax.ppermute(tokens, "expert", across)
    gathered, received, merged, own, partner, hiddens = ({} for _ in range(6))
    outputs, returned, last = (), [], len(widths) - 1
    for name, c in plan(len(widths)):
        start, width = starts[c], widths[c] * BLOCK
        if name == "pair":
            both, token = pair(token, tokens, opposite)
            nearby = lax.ppermute(both, "expert", beside)
        elif name == "line":
            whole = line(token, info, both, nearby, (placing, picking))
            everyone = lax.all_gather(whole, "expert", axis=0, tiled=True, axis_index_groups=by_plane)
            arrived = jnp.einsum(
                "jct,jtd->jcd", placing, everyone, preferred_element_type=jnp.float32
            ).astype(jnp.bfloat16)
            arrived = lax.all_gather(arrived, "mp", axis=2, tiled=True)
            grouped = arrived.reshape(expert_count * capacity, depth)
        elif name == "pack":
            (pieces,), token = pack(token, info, quant_gate, quant_up, start, width, halfway)
            gathered[c] = exchange(pieces)
        elif name == "partial":
            partial, token = merge(token, slots, factors, gathered[c], None, start, blocks_of_rows)
            received[c] = [lax.ppermute(part, "expert", across) for part in partial]
        elif name == "finish":
            (merged[c],), token = merge(
                token, slots, factors, gathered[c], received[c], start, blocks_of_rows
            )
        elif name == "back":
            earlier = [gathered[c + 2]] if c + 2 in gathered else []
            earlier += [received[c + 1][0]] if c + 1 in received else []
            merged[c], token = hold(token, merged[c], earlier)
            own[c] = exchange(merged[c])
        elif name == "trade":
            own[c], token = hold(token, own[c].reshape(depth, width), [])
            partner[c] = lax.ppermute(own[c], "groups", partners)
        elif name == "run":
            (*outputs, hiddens[c]), token = run_chunk(
                token, info, grouped, own[c], partner[c], outputs, start, full, blocks
            )
        else:
            batch = [hiddens[i] for i in (range(last) if c == 0 else range(last, last + 1))]
            hidden, token = hold(token, jnp.concatenate(batch, axis=2), returned[:c])
            returned.append(
                lax.all_to_all(hidden, "expert", split_axis=0, concat_axis=0, tiled=True)
            )

    finished = [
        jnp.dot(
            picking,
            part.reshape(expert_count * capacity, part.shape[2]),
            preferred_element_type=jnp.float32,
        ).astype(jnp.bfloat16)
        for part in returned
    ]
    output = jnp.concatenate(finished, axis=1)
    merged_gate, merged_up = outputs
    return (merged_gate, merged_up, output.reshape(tok_dev, top_count, full))


def solution(mesh):
    return jax.shard_map(
        shards,
        mesh=mesh,
        in_specs=(
            P(("groups", "expert"), "mp"),
            P("groups", None),
            P("expert", None, "mp"),
            P("expert", None, "mp"),
            P(None, None, "mp"),
            P(None, None, "mp"),
            P(),
            P(),
        ),
        out_specs=(
            P(("groups", "expert"), None, "mp"),
            P(("groups", "expert"), None, "mp"),
            P(("groups", "expert"), None, "mp"),
        ),
        check_vma=False,
    )
```

```python
import math

import jax
import jax.numpy as jnp
from jax import lax
from jax.experimental import pallas as pl
from jax.experimental.pallas import tpu as pltpu
from jax.sharding import PartitionSpec as P

D = 2560
BLOCK = 128
TOKEN = jax.ShapeDtypeStruct((8, 128), jnp.float32)
ANY = pl.BlockSpec(memory_space=pl.ANY)
SMEM = pl.BlockSpec(memory_space=pltpu.SMEM)
VMEM = pl.BlockSpec(memory_space=pltpu.VMEM)
VMEM_LIMIT = 60 * 1024 * 1024


def cluster_weights(cluster_ids, frequency):
    ids = cluster_ids[:, 0]
    same = (ids[:, None] == ids[None, :]).astype(jnp.float32)
    return frequency / jnp.sum(same * frequency[None, :], axis=1)


def step_call(kernel, token, operands, in_specs, out_shape, out_specs, **options):
    count = len(operands)

    def ordered(*refs):
        kernel(*refs[:count], *refs[count + 1 : count + 1 + len(out_shape)], *refs[count + 2 + len(out_shape) :])

    *results, token = pl.pallas_call(
        ordered,
        out_shape=[*out_shape, TOKEN],
        in_specs=[*in_specs, ANY],
        out_specs=[*out_specs, ANY],
        compiler_params=pltpu.CompilerParams(vmem_limit_bytes=VMEM_LIMIT),
        cost_estimate=pl.CostEstimate(flops=0, bytes_accessed=0, transcendentals=0),
        **options,
    )(*operands, token)
    return results, token


def pack(token, info, gate, up, start, width, devices):
    sources, depth, _ = gate.shape
    rows = depth // devices

    def kernel(info_ref, gate_ref, up_ref, *rest):
        out, held, in_sems, out_sems = rest

        def move(source):
            loads = [
                pltpu.make_async_copy(
                    source.at[
                        :,
                        pl.ds(part * rows, rows),
                        pl.ds(start, width),
                    ],
                    held.at[part],
                    in_sems.at[part],
                )
                for part in range(devices)
            ]
            stores = [
                pltpu.make_async_copy(held.at[part], out.at[part], out_sems.at[part])
                for part in range(devices)
            ]
            for load in loads:
                load.start()
            for load, store in zip(loads, stores):
                load.wait()
                store.start()
            for store in stores:
                store.wait()

        @pl.when(info_ref[0] == 0)
        def _():
            move(gate_ref)

        @pl.when(info_ref[0] != 0)
        def _():
            move(up_ref)

    return step_call(
        kernel,
        token,
        (info, gate, up),
        [SMEM, ANY, ANY],
        [jax.ShapeDtypeStruct((devices, sources, rows, width), gate.dtype)],
        [ANY],
        scratch_shapes=[
            pltpu.VMEM((devices, sources, rows, width), gate.dtype),
            pltpu.SemaphoreType.DMA((devices,)),
            pltpu.SemaphoreType.DMA((devices,)),
        ],
        name="pack",
    )


def hold(token, value, earlier):
    def kernel(*refs):
        pass

    (value,), token = step_call(
        kernel,
        token,
        (value, *earlier),
        [ANY] * (1 + len(earlier)),
        [jax.ShapeDtypeStruct(value.shape, value.dtype)],
        [ANY],
        input_output_aliases={0: 0},
        name="hold",
    )
    return value, token


def first_share(devices):
    return (5 * devices) // 8


def merge(token, slots, factors, rows_of, received, start, blocks):
    devices, sources, rows, width = rows_of.shape
    steps, column_blocks = blocks
    step = rows // steps
    first = start // BLOCK
    base_slot = 0 if received is None else devices * sources

    cut = first_share(devices)
    halves = (slice(0, cut), slice(cut, devices))

    def kernel(slots_ref, factors_ref, rows_ref, *rest):
        total = rest[-1]
        piece = pl.program_id(0)

        @pl.when(piece == 0)
        def _():
            if received is None:
                total[...] = jnp.zeros_like(total)
            else:
                for part, share in enumerate(halves):
                    total[share] = rest[part][...].astype(jnp.float32)

        for number in range(sources):
            source = piece * sources + number
            slot = slots_ref[base_slot + source]

            @pl.when(slot >= 0)
            def _():
                for index in range(steps):
                    for part in range(width // BLOCK):
                        base = (source * steps + index) * column_blocks + first
                        lanes = slice(part * BLOCK, (part + 1) * BLOCK)
                        place = slice(index * step, (index + 1) * step)
                        total[slot, place, lanes] += (
                            rows_ref[0, number, place, lanes].astype(jnp.float32)
                            * factors_ref[base + part]
                        )

        @pl.when(piece == devices - 1)
        def _():
            if received is None:
                for part, share in enumerate(halves):
                    rest[part][...] = total[share].astype(jnp.bfloat16)
            else:
                rest[2][...] = total[...].astype(jnp.bfloat16)

    whole = pl.BlockSpec((devices, rows, width), lambda i: (0, 0, 0))
    parts = [pl.BlockSpec((count, rows, width), lambda i: (0, 0, 0)) for count in (cut, devices - cut)]
    extra = () if received is None else tuple(received)
    out_counts = (cut, devices - cut) if received is None else (devices,)
    return step_call(
        kernel,
        token,
        (slots, factors, rows_of, *extra),
        [SMEM, SMEM, pl.BlockSpec((1, sources, rows, width), lambda i: (i, 0, 0, 0))]
        + parts[: len(extra)],
        [jax.ShapeDtypeStruct((count, rows, width), jnp.bfloat16) for count in out_counts],
        [whole] if received is not None else parts,
        grid=(devices,),
        scratch_shapes=[pltpu.VMEM((devices, rows, width), jnp.float32)],
        name="merge",
    )


def run_chunk(token, info, grouped, own, partner, outputs, start, full, devices):
    depth, width = own.shape
    count = grouped.shape[0]
    each = count // devices
    factor = 1.0 / math.sqrt(D)

    def kernel(info_ref, grouped_ref, own_ref, partner_ref, *rest):
        gate_out, up_out, hidden_ref, whole, in_sems, out_sems = rest[len(outputs) :]
        halves = [whole.at[:, pl.ds(index * width, width)] for index in range(2)]

        def fill(*sources):
            loads = [
                pltpu.make_async_copy(source, half, in_sems.at[index])
                for index, (source, half) in enumerate(zip(sources, halves))
            ]
            for load in loads:
                load.start()
            for load in loads:
                load.wait()

        @pl.when(info_ref[0] == 0)
        def _():
            fill(own_ref, partner_ref)

        @pl.when(info_ref[0] != 0)
        def _():
            fill(partner_ref, own_ref)

        stores = [
            pltpu.make_async_copy(half, out.at[0, :, pl.ds(start, width)], out_sems.at[index])
            for index, (half, out) in enumerate(zip(halves, (gate_out, up_out)))
        ]
        for store in stores:
            store.start()
        values = jnp.dot(grouped_ref[...], whole[...], preferred_element_type=jnp.float32)
        gate_value = values[:, :width] * factor
        up_value = values[:, width:] * factor
        hidden = (gate_value / (1.0 + jnp.exp(-gate_value)) * up_value).astype(jnp.bfloat16)
        hidden_ref[...] = hidden.reshape(devices, each, width)
        for store in stores:
            store.wait()

    weights = jax.ShapeDtypeStruct((1, depth, full), jnp.bfloat16)
    return step_call(
        kernel,
        token,
        (info, grouped, own, partner, *outputs),
        [SMEM, VMEM, ANY, ANY] + [ANY] * len(outputs),
        [weights, weights, jax.ShapeDtypeStruct((devices, each, width), jnp.bfloat16)],
        [ANY, ANY, VMEM],
        scratch_shapes=[
            pltpu.VMEM((depth, 2 * width), jnp.bfloat16),
            pltpu.SemaphoreType.DMA((2,)),
            pltpu.SemaphoreType.DMA((2,)),
        ],
        input_output_aliases={4 + index: index for index in range(len(outputs))},
        name="run_chunk",
    )


def plan(count):
    order = [("pack", 0)]
    for chunk in range(count + 1):
        if chunk + 1 < count:
            order.append(("pack", chunk + 1))
        if chunk >= 2:
            order.append(("trade", chunk - 2))
        if chunk < count:
            order.append(("partial", chunk))
        if chunk >= 1:
            order.append(("finish", chunk - 1))
        if chunk >= 3:
            order.append(("run", chunk - 3))
        if chunk >= 1:
            order.append(("back", chunk - 1))
    order.append(("run", count - 2))
    order.append(("trade", count - 1))
    order.append(("give", 0))
    order.append(("run", count - 1))
    order.append(("give", 1))
    return order


def route_slots(routes, merged_count, tok_dev):
    experts = jnp.arange(merged_count, dtype=jnp.int32)
    hit_table = jnp.sum((routes[:, :, None] == experts).astype(jnp.int32), axis=1)
    hit_table = hit_table.reshape(-1, tok_dev, merged_count)
    position_lookup = jnp.cumsum(hit_table, axis=1) - hit_table
    return (hit_table, position_lookup)


def chunk_widths(blocks):
    if blocks < 4:
        return [1] * blocks
    middle, odd = divmod(blocks - 2, 2)
    return [1] + [2] * middle + [1] * odd + [1]


def shards(tokens, routes, quant_gate, quant_up, gate_scales, up_scales, cluster_ids, frequency):
    expert_count = lax.axis_size("expert")
    own_index = lax.axis_index("expert")
    group_count = lax.axis_size("groups")
    half = lax.axis_index("groups") % 2
    halfway = expert_count // 2
    side, place = own_index // halfway, own_index % halfway
    depth, full = quant_gate.shape[1:]
    tok_dev = tokens.shape[0]
    top_count = routes.shape[1]
    capacity = min(tok_dev, 2 * tok_dev * top_count // expert_count)

    by_half = [[part * halfway + i for i in range(halfway)] for part in range(2)]
    across = [(i, (i + halfway) % expert_count) for i in range(expert_count)]
    partners = [(g, g ^ 1) for g in range(group_count)]

    def exchange(pieces):
        return lax.all_to_all(pieces, "expert", 0, 0, tiled=True, axis_index_groups=by_half)

    info = jnp.stack([half]).astype(jnp.int32)
    sources = quant_gate.shape[0]
    rows = depth // halfway
    step = math.gcd(rows, BLOCK)
    held = side * halfway * sources + jnp.arange(halfway * sources, dtype=jnp.int32)
    target = jnp.take(cluster_ids[:, 0], held)
    slots = jnp.concatenate(
        [
            jnp.where(target // halfway != side, target % halfway, -1),
            jnp.where(target // halfway == side, target % halfway, -1),
        ]
    )
    weights = jnp.take(cluster_weights(cluster_ids, frequency), held)
    scales = jnp.take(jnp.where(half == 0, gate_scales, up_scales), held, axis=0)
    row_blocks = (place * rows + step * jnp.arange(rows // step, dtype=jnp.int32)) // BLOCK
    factors = jnp.take(scales, row_blocks, axis=1) * weights[:, None, None]
    blocks_of_rows = factors.shape[1:]
    factors = factors.reshape(-1)

    hit_table, position_lookup = route_slots(routes, expert_count, tok_dev)
    positions = jnp.arange(capacity, dtype=jnp.int32)

    def in_blocks(table):
        column = lax.dynamic_index_in_dim(table, own_index, 2, keepdims=False)
        return column.reshape(expert_count, 1, tok_dev)

    placing = (
        (in_blocks(hit_table) == 1) & (in_blocks(position_lookup) == positions[None, :, None])
    ).astype(jnp.bfloat16)

    experts = jnp.arange(expert_count, dtype=jnp.int32)
    local_routes = lax.dynamic_slice_in_dim(routes, own_index * tok_dev, tok_dev, 0)
    own_slots = lax.dynamic_index_in_dim(position_lookup, own_index, 0, keepdims=False)
    chosen = local_routes[:, :, None] == experts
    slot_of = jnp.sum(jnp.where(chosen, own_slots[:, None, :], 0), axis=2)
    picking = (chosen[:, :, :, None] & (slot_of[:, :, None, None] == positions)).astype(
        jnp.bfloat16
    )
    picking = picking.reshape(tok_dev * top_count, expert_count * capacity)

    widths = chunk_widths(full // BLOCK)
    starts = [BLOCK * sum(widths[:chunk]) for chunk in range(len(widths))]
    token = jnp.zeros(TOKEN.shape, TOKEN.dtype)
    everyone = lax.all_gather(tokens, "expert", axis=0, tiled=True)
    arrived = jnp.einsum(
        "jct,jtd->jcd",
        placing,
        everyone.reshape(expert_count, tok_dev, everyone.shape[1]),
        preferred_element_type=jnp.float32,
    ).astype(jnp.bfloat16)
    arrived = lax.all_gather(arrived, "mp", axis=2, tiled=True)
    grouped = arrived.reshape(expert_count * capacity, depth)
    gathered, received, merged, own, partner, hiddens = ({} for _ in range(6))
    outputs, returned, last = (), [], len(widths) - 1
    for name, c in plan(len(widths)):
        start, width = starts[c], widths[c] * BLOCK
        if name == "pack":
            (pieces,), token = pack(token, info, quant_gate, quant_up, start, width, halfway)
            gathered[c] = exchange(pieces)
        elif name == "partial":
            if c == 1:
                gathered[c], token = hold(
                    token, gathered[c], [*received[0], placing, picking]
                )
            partial, token = merge(token, slots, factors, gathered[c], None, start, blocks_of_rows)
            received[c] = [lax.ppermute(part, "expert", across) for part in partial]
        elif name == "finish":
            (merged[c],), token = merge(
                token, slots, factors, gathered[c], received[c], start, blocks_of_rows
            )
        elif name == "back":
            earlier = [gathered[c + 2]] if c + 2 in gathered else []
            earlier += [received[c + 1][0]] if c + 1 in received else []
            earlier += [grouped] if c == 0 else []
            merged[c], token = hold(token, merged[c], earlier)
            own[c] = exchange(merged[c])
        elif name == "trade":
            earlier = [received[c + 1][1]] if c + 1 in received else []
            own[c], token = hold(token, own[c].reshape(depth, width), earlier)
            partner[c] = lax.ppermute(own[c], "groups", partners)
        elif name == "run":
            (*outputs, hiddens[c]), token = run_chunk(
                token, info, grouped, own[c], partner[c], outputs, start, full, expert_count
            )
        else:
            batch = [hiddens[i] for i in (range(last) if c == 0 else range(last, last + 1))]
            hidden, token = hold(token, jnp.concatenate(batch, axis=2), returned[:c])
            returned.append(
                lax.all_to_all(hidden, "expert", split_axis=0, concat_axis=0, tiled=True)
            )

    finished = [
        jnp.dot(
            picking,
            part.reshape(expert_count * capacity, part.shape[2]),
            preferred_element_type=jnp.float32,
        ).astype(jnp.bfloat16)
        for part in returned
    ]
    output = jnp.concatenate(finished, axis=1)
    merged_gate, merged_up = outputs
    return (merged_gate, merged_up, output.reshape(tok_dev, top_count, full))


def solution(mesh):
    return jax.shard_map(
        shards,
        mesh=mesh,
        in_specs=(
            P(("groups", "expert"), "mp"),
            P("groups", None),
            P("expert", None, "mp"),
            P("expert", None, "mp"),
            P(None, None, "mp"),
            P(None, None, "mp"),
            P(),
            P(),
        ),
        out_specs=(
            P(("groups", "expert"), None, "mp"),
            P(("groups", "expert"), None, "mp"),
            P(("groups", "expert"), None, "mp"),
        ),
        check_vma=False,
    )
```

```python
import math

import jax
import jax.numpy as jnp
from jax import lax
from jax.experimental import pallas as pl
from jax.experimental.pallas import tpu as pltpu
from jax.sharding import PartitionSpec as P

D = 2560
BLOCK = 128
TOKEN = jax.ShapeDtypeStruct((8, 128), jnp.float32)
ANY = pl.BlockSpec(memory_space=pl.ANY)
SMEM = pl.BlockSpec(memory_space=pltpu.SMEM)
VMEM = pl.BlockSpec(memory_space=pltpu.VMEM)
VMEM_LIMIT = 60 * 1024 * 1024


def cluster_weights(cluster_ids, frequency):
    ids = cluster_ids[:, 0]
    same = (ids[:, None] == ids[None, :]).astype(jnp.float32)
    return frequency / jnp.sum(same * frequency[None, :], axis=1)


def step_call(kernel, token, operands, in_specs, out_shape, out_specs, **options):
    count = len(operands)

    def ordered(*refs):
        kernel(*refs[:count], *refs[count + 1 : count + 1 + len(out_shape)], *refs[count + 2 + len(out_shape) :])

    *results, token = pl.pallas_call(
        ordered,
        out_shape=[*out_shape, TOKEN],
        in_specs=[*in_specs, ANY],
        out_specs=[*out_specs, ANY],
        compiler_params=pltpu.CompilerParams(vmem_limit_bytes=VMEM_LIMIT),
        cost_estimate=pl.CostEstimate(flops=0, bytes_accessed=0, transcendentals=0),
        **options,
    )(*operands, token)
    return results, token


def pack(token, info, gate, up, start, width, devices):
    sources, depth, _ = gate.shape
    rows = depth // devices

    def kernel(info_ref, gate_ref, up_ref, *rest):
        out, held, in_sems, out_sems = rest

        def move(source):
            loads = [
                pltpu.make_async_copy(
                    source.at[
                        :,
                        pl.ds(part * rows, rows),
                        pl.ds(start, width),
                    ],
                    held.at[part],
                    in_sems.at[part],
                )
                for part in range(devices)
            ]
            stores = [
                pltpu.make_async_copy(held.at[part], out.at[part], out_sems.at[part])
                for part in range(devices)
            ]
            for load in loads:
                load.start()
            for load, store in zip(loads, stores):
                load.wait()
                store.start()
            for store in stores:
                store.wait()

        @pl.when(info_ref[0] == 0)
        def _():
            move(gate_ref)

        @pl.when(info_ref[0] != 0)
        def _():
            move(up_ref)

    return step_call(
        kernel,
        token,
        (info, gate, up),
        [SMEM, ANY, ANY],
        [jax.ShapeDtypeStruct((devices, sources, rows, width), gate.dtype)],
        [ANY],
        scratch_shapes=[
            pltpu.VMEM((devices, sources, rows, width), gate.dtype),
            pltpu.SemaphoreType.DMA((devices,)),
            pltpu.SemaphoreType.DMA((devices,)),
        ],
        name="pack",
    )


def hold(token, value, earlier):
    def kernel(*refs):
        pass

    (value,), token = step_call(
        kernel,
        token,
        (value, *earlier),
        [ANY] * (1 + len(earlier)),
        [jax.ShapeDtypeStruct(value.shape, value.dtype)],
        [ANY],
        input_output_aliases={0: 0},
        name="hold",
    )
    return value, token


def merge(token, info, slots, factors, rows_of, gathered, start, blocks):
    devices, sources, rows, width = rows_of.shape
    steps, column_blocks = blocks
    step = rows // steps
    first = start // BLOCK
    base_slot = 0 if gathered is None else devices * sources

    def kernel(info_ref, slots_ref, factors_ref, rows_ref, *rest):
        piece = pl.program_id(0)
        if gathered is None:
            out_ref, total = rest
        else:
            gathered_ref, out_ref, total, received, sem = rest

        @pl.when(piece == 0)
        def _():
            if gathered is None:
                total[...] = jnp.zeros_like(total)
            else:
                copy = pltpu.make_async_copy(gathered_ref.at[1 - info_ref[1]], received, sem)
                copy.start()
                copy.wait()
                total[...] = received[...].astype(jnp.float32)

        for number in range(sources):
            source = piece * sources + number
            slot = slots_ref[base_slot + source]

            @pl.when(slot >= 0)
            def _():
                for index in range(steps):
                    for part in range(width // BLOCK):
                        base = (source * steps + index) * column_blocks + first
                        lanes = slice(part * BLOCK, (part + 1) * BLOCK)
                        place = slice(index * step, (index + 1) * step)
                        total[slot, place, lanes] += (
                            rows_ref[0, number, place, lanes].astype(jnp.float32)
                            * factors_ref[base + part]
                        )

        @pl.when(piece == devices - 1)
        def _():
            out_ref[...] = total[...].astype(jnp.bfloat16)

    scratch = [pltpu.VMEM((devices, rows, width), jnp.float32)]
    extra = ()
    if gathered is not None:
        scratch += [pltpu.VMEM((devices, rows, width), jnp.bfloat16), pltpu.SemaphoreType.DMA]
        extra = (gathered,)
    (merged,), token = step_call(
        kernel,
        token,
        (info, slots, factors, rows_of, *extra),
        [SMEM, SMEM, SMEM, pl.BlockSpec((1, sources, rows, width), lambda i: (i, 0, 0, 0))]
        + [ANY] * len(extra),
        [jax.ShapeDtypeStruct((devices, rows, width), jnp.bfloat16)],
        [pl.BlockSpec((devices, rows, width), lambda i: (0, 0, 0))],
        grid=(devices,),
        scratch_shapes=scratch,
        name="merge",
    )
    return merged, token


def run_chunk(token, info, grouped, own, partner, outputs, start, full, devices):
    depth, width = own.shape
    count = grouped.shape[0]
    each = count // devices
    factor = 1.0 / math.sqrt(D)

    def kernel(info_ref, grouped_ref, own_ref, partner_ref, *rest):
        gate_out, up_out, hidden_ref, whole, in_sems, out_sems = rest[len(outputs) :]
        halves = [whole.at[:, pl.ds(index * width, width)] for index in range(2)]

        def fill(*sources):
            loads = [
                pltpu.make_async_copy(source, half, in_sems.at[index])
                for index, (source, half) in enumerate(zip(sources, halves))
            ]
            for load in loads:
                load.start()
            for load in loads:
                load.wait()

        @pl.when(info_ref[0] == 0)
        def _():
            fill(own_ref, partner_ref)

        @pl.when(info_ref[0] != 0)
        def _():
            fill(partner_ref, own_ref)

        stores = [
            pltpu.make_async_copy(half, out.at[0, :, pl.ds(start, width)], out_sems.at[index])
            for index, (half, out) in enumerate(zip(halves, (gate_out, up_out)))
        ]
        for store in stores:
            store.start()
        values = jnp.dot(grouped_ref[...], whole[...], preferred_element_type=jnp.float32)
        gate_value = values[:, :width] * factor
        up_value = values[:, width:] * factor
        hidden = (gate_value / (1.0 + jnp.exp(-gate_value)) * up_value).astype(jnp.bfloat16)
        hidden_ref[...] = hidden.reshape(devices, each, width)
        for store in stores:
            store.wait()

    weights = jax.ShapeDtypeStruct((1, depth, full), jnp.bfloat16)
    return step_call(
        kernel,
        token,
        (info, grouped, own, partner, *outputs),
        [SMEM, VMEM, ANY, ANY] + [ANY] * len(outputs),
        [weights, weights, jax.ShapeDtypeStruct((devices, each, width), jnp.bfloat16)],
        [ANY, ANY, VMEM],
        scratch_shapes=[
            pltpu.VMEM((depth, 2 * width), jnp.bfloat16),
            pltpu.SemaphoreType.DMA((2,)),
            pltpu.SemaphoreType.DMA((2,)),
        ],
        input_output_aliases={4 + index: index for index in range(len(outputs))},
        name="run_chunk",
    )


def plan(count):
    order = [("pack", 0)]
    for chunk in range(count + 1):
        if chunk + 1 < count:
            order.append(("pack", chunk + 1))
        if chunk >= 2:
            order.append(("trade", chunk - 2))
        if chunk < count:
            order.append(("partial", chunk))
        if chunk >= 1:
            order.append(("finish", chunk - 1))
        if chunk >= 3:
            order.append(("run", chunk - 3))
        if chunk >= 1:
            order.append(("back", chunk - 1))
    order.append(("run", count - 2))
    order.append(("trade", count - 1))
    order.append(("give", 0))
    order.append(("run", count - 1))
    order.append(("give", 1))
    return order


def route_slots(routes, merged_count, tok_dev):
    experts = jnp.arange(merged_count, dtype=jnp.int32)
    hit_table = jnp.sum((routes[:, :, None] == experts).astype(jnp.int32), axis=1)
    hit_table = hit_table.reshape(-1, tok_dev, merged_count)
    position_lookup = jnp.cumsum(hit_table, axis=1) - hit_table
    return (hit_table, position_lookup)


def chunk_widths(blocks):
    if blocks < 4:
        return [1] * blocks
    middle, odd = divmod(blocks - 2, 2)
    return [1] + [2] * middle + [1] * odd + [1]


def shards(tokens, routes, quant_gate, quant_up, gate_scales, up_scales, cluster_ids, frequency):
    expert_count = lax.axis_size("expert")
    own_index = lax.axis_index("expert")
    group_count = lax.axis_size("groups")
    half = lax.axis_index("groups") % 2
    halfway = expert_count // 2
    side, place = own_index // halfway, own_index % halfway
    depth, full = quant_gate.shape[1:]
    tok_dev = tokens.shape[0]
    top_count = routes.shape[1]
    capacity = min(tok_dev, 2 * tok_dev * top_count // expert_count)

    by_half = [[part * halfway + i for i in range(halfway)] for part in range(2)]
    pairs = [[i, i + halfway] for i in range(halfway)]
    partners = [(g, g ^ 1) for g in range(group_count)]

    def exchange(pieces):
        return lax.all_to_all(pieces, "expert", 0, 0, tiled=True, axis_index_groups=by_half)

    info = jnp.stack([half, side]).astype(jnp.int32)
    sources = quant_gate.shape[0]
    rows = depth // halfway
    step = math.gcd(rows, BLOCK)
    held = side * halfway * sources + jnp.arange(halfway * sources, dtype=jnp.int32)
    target = jnp.take(cluster_ids[:, 0], held)
    slots = jnp.concatenate(
        [
            jnp.where(target // halfway != side, target % halfway, -1),
            jnp.where(target // halfway == side, target % halfway, -1),
        ]
    )
    weights = jnp.take(cluster_weights(cluster_ids, frequency), held)
    scales = jnp.take(jnp.where(half == 0, gate_scales, up_scales), held, axis=0)
    row_blocks = (place * rows + step * jnp.arange(rows // step, dtype=jnp.int32)) // BLOCK
    factors = jnp.take(scales, row_blocks, axis=1) * weights[:, None, None]
    blocks_of_rows = factors.shape[1:]
    factors = factors.reshape(-1)

    hit_table, position_lookup = route_slots(routes, expert_count, tok_dev)
    positions = jnp.arange(capacity, dtype=jnp.int32)

    def in_blocks(table):
        column = lax.dynamic_index_in_dim(table, own_index, 2, keepdims=False)
        return column.reshape(expert_count, 1, tok_dev)

    placing = (
        (in_blocks(hit_table) == 1) & (in_blocks(position_lookup) == positions[None, :, None])
    ).astype(jnp.bfloat16)

    experts = jnp.arange(expert_count, dtype=jnp.int32)
    local_routes = lax.dynamic_slice_in_dim(routes, own_index * tok_dev, tok_dev, 0)
    own_slots = lax.dynamic_index_in_dim(position_lookup, own_index, 0, keepdims=False)
    chosen = local_routes[:, :, None] == experts
    slot_of = jnp.sum(jnp.where(chosen, own_slots[:, None, :], 0), axis=2)
    picking = (chosen[:, :, :, None] & (slot_of[:, :, None, None] == positions)).astype(
        jnp.bfloat16
    )
    picking = picking.reshape(tok_dev * top_count, expert_count * capacity)

    widths = chunk_widths(full // BLOCK)
    starts = [BLOCK * sum(widths[:chunk]) for chunk in range(len(widths))]
    token = jnp.zeros(TOKEN.shape, TOKEN.dtype)
    everyone = lax.all_gather(tokens, "expert", axis=0, tiled=True)
    arrived = jnp.einsum(
        "jct,jtd->jcd",
        placing,
        everyone.reshape(expert_count, tok_dev, everyone.shape[1]),
        preferred_element_type=jnp.float32,
    ).astype(jnp.bfloat16)
    arrived = lax.all_gather(arrived, "mp", axis=2, tiled=True)
    grouped = arrived.reshape(expert_count * capacity, depth)
    gathered, received, merged, own, partner, hiddens = ({} for _ in range(6))
    outputs, returned, last = (), [], len(widths) - 1
    for name, c in plan(len(widths)):
        start, width = starts[c], widths[c] * BLOCK
        if name == "pack":
            (pieces,), token = pack(token, info, quant_gate, quant_up, start, width, halfway)
            gathered[c] = exchange(pieces)
        elif name == "partial":
            if c == 1:
                gathered[c], token = hold(token, gathered[c], [placing, picking])
            partial, token = merge(
                token, info, slots, factors, gathered[c], None, start, blocks_of_rows
            )
            received[c] = lax.all_gather(partial, "expert", axis_index_groups=pairs)
        elif name == "finish":
            merged[c], token = merge(
                token, info, slots, factors, gathered[c], received[c], start, blocks_of_rows
            )
        elif name == "back":
            earlier = [gathered[c + 2]] if c + 2 in gathered else []
            earlier += [grouped] if c == 0 else []
            merged[c], token = hold(token, merged[c], earlier)
            own[c] = exchange(merged[c])
        elif name == "trade":
            own[c], token = hold(token, own[c].reshape(depth, width), [])
            partner[c] = lax.ppermute(own[c], "groups", partners)
        elif name == "run":
            (*outputs, hiddens[c]), token = run_chunk(
                token, info, grouped, own[c], partner[c], outputs, start, full, expert_count
            )
        else:
            batch = [hiddens[i] for i in (range(last) if c == 0 else range(last, last + 1))]
            hidden, token = hold(token, jnp.concatenate(batch, axis=2), returned[:c])
            returned.append(
                lax.all_to_all(hidden, "expert", split_axis=0, concat_axis=0, tiled=True)
            )

    finished = [
        jnp.dot(
            picking,
            part.reshape(expert_count * capacity, part.shape[2]),
            preferred_element_type=jnp.float32,
        ).astype(jnp.bfloat16)
        for part in returned
    ]
    output = jnp.concatenate(finished, axis=1)
    merged_gate, merged_up = outputs
    return (merged_gate, merged_up, output.reshape(tok_dev, top_count, full))


def solution(mesh):
    return jax.shard_map(
        shards,
        mesh=mesh,
        in_specs=(
            P(("groups", "expert"), "mp"),
            P("groups", None),
            P("expert", None, "mp"),
            P("expert", None, "mp"),
            P(None, None, "mp"),
            P(None, None, "mp"),
            P(),
            P(),
        ),
        out_specs=(
            P(("groups", "expert"), None, "mp"),
            P(("groups", "expert"), None, "mp"),
            P(("groups", "expert"), None, "mp"),
        ),
        check_vma=False,
    )
```

```python
import math

import jax
import jax.numpy as jnp
from jax import lax
from jax.experimental import pallas as pl
from jax.experimental.pallas import tpu as pltpu
from jax.sharding import PartitionSpec as P

D = 2560
BLOCK = 128
TOKEN = jax.ShapeDtypeStruct((8, 128), jnp.float32)
ANY = pl.BlockSpec(memory_space=pl.ANY)
SMEM = pl.BlockSpec(memory_space=pltpu.SMEM)
VMEM = pl.BlockSpec(memory_space=pltpu.VMEM)
VMEM_LIMIT = 60 * 1024 * 1024


def cluster_weights(cluster_ids, frequency):
    ids = cluster_ids[:, 0]
    same = (ids[:, None] == ids[None, :]).astype(jnp.float32)
    return frequency / jnp.sum(same * frequency[None, :], axis=1)


def step_call(kernel, token, operands, in_specs, out_shape, out_specs, **options):
    count = len(operands)

    def ordered(*refs):
        kernel(*refs[:count], *refs[count + 1 : count + 1 + len(out_shape)], *refs[count + 2 + len(out_shape) :])

    *results, token = pl.pallas_call(
        ordered,
        out_shape=[*out_shape, TOKEN],
        in_specs=[*in_specs, ANY],
        out_specs=[*out_specs, ANY],
        compiler_params=pltpu.CompilerParams(vmem_limit_bytes=VMEM_LIMIT),
        cost_estimate=pl.CostEstimate(flops=0, bytes_accessed=0, transcendentals=0),
        **options,
    )(*operands, token)
    return results, token


def pack(token, info, gate, up, start, width, devices):
    sources, depth, _ = gate.shape
    rows = depth // devices

    def kernel(info_ref, gate_ref, up_ref, *rest):
        out, held, in_sems, out_sems = rest

        def move(source):
            loads = [
                pltpu.make_async_copy(
                    source.at[
                        :,
                        pl.ds(part * rows, rows),
                        pl.ds(start, width),
                    ],
                    held.at[part],
                    in_sems.at[part],
                )
                for part in range(devices)
            ]
            stores = [
                pltpu.make_async_copy(held.at[part], out.at[part], out_sems.at[part])
                for part in range(devices)
            ]
            for load in loads:
                load.start()
            for load, store in zip(loads, stores):
                load.wait()
                store.start()
            for store in stores:
                store.wait()

        @pl.when(info_ref[0] == 0)
        def _():
            move(gate_ref)

        @pl.when(info_ref[0] != 0)
        def _():
            move(up_ref)

    return step_call(
        kernel,
        token,
        (info, gate, up),
        [SMEM, ANY, ANY],
        [jax.ShapeDtypeStruct((devices, sources, rows, width), gate.dtype)],
        [ANY],
        scratch_shapes=[
            pltpu.VMEM((devices, sources, rows, width), gate.dtype),
            pltpu.SemaphoreType.DMA((devices,)),
            pltpu.SemaphoreType.DMA((devices,)),
        ],
        name="pack",
    )


def hold(token, value, earlier):
    def kernel(*refs):
        pass

    (value,), token = step_call(
        kernel,
        token,
        (value, *earlier),
        [ANY] * (1 + len(earlier)),
        [jax.ShapeDtypeStruct(value.shape, value.dtype)],
        [ANY],
        input_output_aliases={0: 0},
        name="hold",
    )
    return value, token


def first_share(devices):
    return (5 * devices) // 8


def merge(token, info, slots, factors, rows_of, received, start, blocks):
    devices, sources, rows, width = rows_of.shape
    steps, column_blocks = blocks
    step = rows // steps
    first = start // BLOCK
    base_slot = 0 if received is None else devices * sources
    cut = first_share(devices)
    shares = (slice(0, cut), slice(cut, devices))

    def kernel(info_ref, slots_ref, factors_ref, rows_ref, *rest):
        piece = pl.program_id(0)
        if received is None:
            *outs, total = rest
        else:
            paired_ref, sent_ref, out_ref, total, landed, sem = rest

        @pl.when(piece == 0)
        def _():
            if received is None:
                total[...] = jnp.zeros_like(total)
            else:
                copy = pltpu.make_async_copy(paired_ref.at[1 - info_ref[1]], landed, sem)
                copy.start()
                total[shares[1]] = sent_ref[...].astype(jnp.float32)
                copy.wait()
                total[shares[0]] = landed[...].astype(jnp.float32)

        for number in range(sources):
            source = piece * sources + number
            slot = slots_ref[base_slot + source]

            @pl.when(slot >= 0)
            def _():
                for index in range(steps):
                    for part in range(width // BLOCK):
                        base = (source * steps + index) * column_blocks + first
                        lanes = slice(part * BLOCK, (part + 1) * BLOCK)
                        place = slice(index * step, (index + 1) * step)
                        total[slot, place, lanes] += (
                            rows_ref[0, number, place, lanes].astype(jnp.float32)
                            * factors_ref[base + part]
                        )

        @pl.when(piece == devices - 1)
        def _():
            if received is None:
                for out, share in zip(outs, shares):
                    out[...] = total[share].astype(jnp.bfloat16)
            else:
                out_ref[...] = total[...].astype(jnp.bfloat16)

    def block(count):
        return pl.BlockSpec((count, rows, width), lambda i: (0, 0, 0))

    counts = (cut, devices - cut) if received is None else (devices,)
    scratch = [pltpu.VMEM((devices, rows, width), jnp.float32)]
    extra, extra_specs = (), []
    if received is not None:
        scratch += [pltpu.VMEM((cut, rows, width), jnp.bfloat16), pltpu.SemaphoreType.DMA]
        extra, extra_specs = tuple(received), [ANY, block(devices - cut)]
    return step_call(
        kernel,
        token,
        (info, slots, factors, rows_of, *extra),
        [SMEM, SMEM, SMEM, pl.BlockSpec((1, sources, rows, width), lambda i: (i, 0, 0, 0))]
        + extra_specs,
        [jax.ShapeDtypeStruct((count, rows, width), jnp.bfloat16) for count in counts],
        [block(count) for count in counts],
        grid=(devices,),
        scratch_shapes=scratch,
        name="merge",
    )


def run_chunk(token, info, grouped, own, partner, outputs, start, full, devices):
    depth, width = own.shape
    count = grouped.shape[0]
    each = count // devices
    factor = 1.0 / math.sqrt(D)

    def kernel(info_ref, grouped_ref, own_ref, partner_ref, *rest):
        gate_out, up_out, hidden_ref, whole, in_sems, out_sems = rest[len(outputs) :]
        halves = [whole.at[:, pl.ds(index * width, width)] for index in range(2)]

        def fill(*sources):
            loads = [
                pltpu.make_async_copy(source, half, in_sems.at[index])
                for index, (source, half) in enumerate(zip(sources, halves))
            ]
            for load in loads:
                load.start()
            for load in loads:
                load.wait()

        @pl.when(info_ref[0] == 0)
        def _():
            fill(own_ref, partner_ref)

        @pl.when(info_ref[0] != 0)
        def _():
            fill(partner_ref, own_ref)

        stores = [
            pltpu.make_async_copy(half, out.at[0, :, pl.ds(start, width)], out_sems.at[index])
            for index, (half, out) in enumerate(zip(halves, (gate_out, up_out)))
        ]
        for store in stores:
            store.start()
        values = jnp.dot(grouped_ref[...], whole[...], preferred_element_type=jnp.float32)
        gate_value = values[:, :width] * factor
        up_value = values[:, width:] * factor
        hidden = (gate_value / (1.0 + jnp.exp(-gate_value)) * up_value).astype(jnp.bfloat16)
        hidden_ref[...] = hidden.reshape(devices, each, width)
        for store in stores:
            store.wait()

    weights = jax.ShapeDtypeStruct((1, depth, full), jnp.bfloat16)
    return step_call(
        kernel,
        token,
        (info, grouped, own, partner, *outputs),
        [SMEM, VMEM, ANY, ANY] + [ANY] * len(outputs),
        [weights, weights, jax.ShapeDtypeStruct((devices, each, width), jnp.bfloat16)],
        [ANY, ANY, VMEM],
        scratch_shapes=[
            pltpu.VMEM((depth, 2 * width), jnp.bfloat16),
            pltpu.SemaphoreType.DMA((2,)),
            pltpu.SemaphoreType.DMA((2,)),
        ],
        input_output_aliases={4 + index: index for index in range(len(outputs))},
        name="run_chunk",
    )


def plan(count):
    order = [("pack", 0)]
    for chunk in range(count + 1):
        if chunk + 1 < count:
            order.append(("pack", chunk + 1))
        if chunk >= 2:
            order.append(("trade", chunk - 2))
        if chunk < count:
            order.append(("partial", chunk))
        if chunk >= 1:
            order.append(("finish", chunk - 1))
        if chunk >= 3:
            order.append(("run", chunk - 3))
        if chunk >= 1:
            order.append(("back", chunk - 1))
    order.append(("run", count - 2))
    order.append(("trade", count - 1))
    order.append(("give", 0))
    order.append(("run", count - 1))
    order.append(("give", 1))
    return order


def route_slots(routes, merged_count, tok_dev):
    experts = jnp.arange(merged_count, dtype=jnp.int32)
    hit_table = jnp.sum((routes[:, :, None] == experts).astype(jnp.int32), axis=1)
    hit_table = hit_table.reshape(-1, tok_dev, merged_count)
    position_lookup = jnp.cumsum(hit_table, axis=1) - hit_table
    return (hit_table, position_lookup)


def chunk_widths(blocks):
    if blocks < 4:
        return [1] * blocks
    middle, odd = divmod(blocks - 2, 2)
    return [1] + [2] * middle + [1] * odd + [1]


def shards(tokens, routes, quant_gate, quant_up, gate_scales, up_scales, cluster_ids, frequency):
    expert_count = lax.axis_size("expert")
    own_index = lax.axis_index("expert")
    group_count = lax.axis_size("groups")
    half = lax.axis_index("groups") % 2
    halfway = expert_count // 2
    side, place = own_index // halfway, own_index % halfway
    depth, full = quant_gate.shape[1:]
    tok_dev = tokens.shape[0]
    top_count = routes.shape[1]
    capacity = min(tok_dev, 2 * tok_dev * top_count // expert_count)

    by_half = [[part * halfway + i for i in range(halfway)] for part in range(2)]
    pairs = [[i, i + halfway] for i in range(halfway)]
    across = [(i, (i + halfway) % expert_count) for i in range(expert_count)]
    partners = [(g, g ^ 1) for g in range(group_count)]

    def exchange(pieces):
        return lax.all_to_all(pieces, "expert", 0, 0, tiled=True, axis_index_groups=by_half)

    info = jnp.stack([half, side]).astype(jnp.int32)
    sources = quant_gate.shape[0]
    rows = depth // halfway
    step = math.gcd(rows, BLOCK)
    held = side * halfway * sources + jnp.arange(halfway * sources, dtype=jnp.int32)
    target = jnp.take(cluster_ids[:, 0], held)
    slots = jnp.concatenate(
        [
            jnp.where(target // halfway != side, target % halfway, -1),
            jnp.where(target // halfway == side, target % halfway, -1),
        ]
    )
    weights = jnp.take(cluster_weights(cluster_ids, frequency), held)
    scales = jnp.take(jnp.where(half == 0, gate_scales, up_scales), held, axis=0)
    row_blocks = (place * rows + step * jnp.arange(rows // step, dtype=jnp.int32)) // BLOCK
    factors = jnp.take(scales, row_blocks, axis=1) * weights[:, None, None]
    blocks_of_rows = factors.shape[1:]
    factors = factors.reshape(-1)

    hit_table, position_lookup = route_slots(routes, expert_count, tok_dev)
    positions = jnp.arange(capacity, dtype=jnp.int32)

    def in_blocks(table):
        column = lax.dynamic_index_in_dim(table, own_index, 2, keepdims=False)
        return column.reshape(expert_count, 1, tok_dev)

    placing = (
        (in_blocks(hit_table) == 1) & (in_blocks(position_lookup) == positions[None, :, None])
    ).astype(jnp.bfloat16)

    experts = jnp.arange(expert_count, dtype=jnp.int32)
    local_routes = lax.dynamic_slice_in_dim(routes, own_index * tok_dev, tok_dev, 0)
    own_slots = lax.dynamic_index_in_dim(position_lookup, own_index, 0, keepdims=False)
    chosen = local_routes[:, :, None] == experts
    slot_of = jnp.sum(jnp.where(chosen, own_slots[:, None, :], 0), axis=2)
    picking = (chosen[:, :, :, None] & (slot_of[:, :, None, None] == positions)).astype(
        jnp.bfloat16
    )
    picking = picking.reshape(tok_dev * top_count, expert_count * capacity)

    widths = chunk_widths(full // BLOCK)
    starts = [BLOCK * sum(widths[:chunk]) for chunk in range(len(widths))]
    token = jnp.zeros(TOKEN.shape, TOKEN.dtype)
    everyone = lax.all_gather(tokens, "expert", axis=0, tiled=True)
    arrived = jnp.einsum(
        "jct,jtd->jcd",
        placing,
        everyone.reshape(expert_count, tok_dev, everyone.shape[1]),
        preferred_element_type=jnp.float32,
    ).astype(jnp.bfloat16)
    arrived = lax.all_gather(arrived, "mp", axis=2, tiled=True)
    grouped = arrived.reshape(expert_count * capacity, depth)
    gathered, received, merged, own, partner, hiddens = ({} for _ in range(6))
    outputs, returned, last = (), [], len(widths) - 1
    for name, c in plan(len(widths)):
        start, width = starts[c], widths[c] * BLOCK
        if name == "pack":
            (pieces,), token = pack(token, info, quant_gate, quant_up, start, width, halfway)
            gathered[c] = exchange(pieces)
        elif name == "partial":
            if c < 2:
                earlier = [everyone] if c == 0 else [placing, picking]
                gathered[c], token = hold(token, gathered[c], earlier)
            partial, token = merge(
                token, info, slots, factors, gathered[c], None, start, blocks_of_rows
            )
            received[c] = [
                lax.all_gather(partial[0], "expert", axis_index_groups=pairs),
                lax.ppermute(partial[1], "expert", across),
            ]
        elif name == "finish":
            (merged[c],), token = merge(
                token, info, slots, factors, gathered[c], received[c], start, blocks_of_rows
            )
        elif name == "back":
            earlier = [gathered[c + 2]] if c + 2 in gathered else []
            earlier += [grouped] if c == 0 else []
            merged[c], token = hold(token, merged[c], earlier)
            own[c] = exchange(merged[c])
        elif name == "trade":
            own[c], token = hold(token, own[c].reshape(depth, width), [])
            partner[c] = lax.ppermute(own[c], "groups", partners)
        elif name == "run":
            (*outputs, hiddens[c]), token = run_chunk(
                token, info, grouped, own[c], partner[c], outputs, start, full, expert_count
            )
        else:
            batch = [hiddens[i] for i in (range(last) if c == 0 else range(last, last + 1))]
            hidden, token = hold(token, jnp.concatenate(batch, axis=2), returned[:c])
            returned.append(
                lax.all_to_all(hidden, "expert", split_axis=0, concat_axis=0, tiled=True)
            )

    finished = [
        jnp.dot(
            picking,
            part.reshape(expert_count * capacity, part.shape[2]),
            preferred_element_type=jnp.float32,
        ).astype(jnp.bfloat16)
        for part in returned
    ]
    output = jnp.concatenate(finished, axis=1)
    merged_gate, merged_up = outputs
    return (merged_gate, merged_up, output.reshape(tok_dev, top_count, full))


def solution(mesh):
    return jax.shard_map(
        shards,
        mesh=mesh,
        in_specs=(
            P(("groups", "expert"), "mp"),
            P("groups", None),
            P("expert", None, "mp"),
            P("expert", None, "mp"),
            P(None, None, "mp"),
            P(None, None, "mp"),
            P(),
            P(),
        ),
        out_specs=(
            P(("groups", "expert"), None, "mp"),
            P(("groups", "expert"), None, "mp"),
            P(("groups", "expert"), None, "mp"),
        ),
        check_vma=False,
    )
```

```python
import math

import jax
import jax.numpy as jnp
from jax import lax
from jax.experimental import pallas as pl
from jax.experimental.pallas import tpu as pltpu
from jax.sharding import PartitionSpec as P

D = 2560
BLOCK = 128
TOKEN = jax.ShapeDtypeStruct((8, 128), jnp.float32)
ANY = pl.BlockSpec(memory_space=pl.ANY)
SMEM = pl.BlockSpec(memory_space=pltpu.SMEM)
VMEM = pl.BlockSpec(memory_space=pltpu.VMEM)
VMEM_LIMIT = 60 * 1024 * 1024


def cluster_weights(cluster_ids, frequency):
    ids = cluster_ids[:, 0]
    same = (ids[:, None] == ids[None, :]).astype(jnp.float32)
    return frequency / jnp.sum(same * frequency[None, :], axis=1)


def step_call(kernel, token, operands, in_specs, out_shape, out_specs, **options):
    count = len(operands)

    def ordered(*refs):
        kernel(*refs[:count], *refs[count + 1 : count + 1 + len(out_shape)], *refs[count + 2 + len(out_shape) :])

    *results, token = pl.pallas_call(
        ordered,
        out_shape=[*out_shape, TOKEN],
        in_specs=[*in_specs, ANY],
        out_specs=[*out_specs, ANY],
        compiler_params=pltpu.CompilerParams(vmem_limit_bytes=VMEM_LIMIT),
        cost_estimate=pl.CostEstimate(flops=0, bytes_accessed=0, transcendentals=0),
        **options,
    )(*operands, token)
    return results, token


def pack(token, info, gate, up, start, width, devices):
    sources, depth, _ = gate.shape
    rows = depth // devices

    def kernel(info_ref, gate_ref, up_ref, *rest):
        out, held, in_sems, out_sems = rest

        def move(source):
            loads = [
                pltpu.make_async_copy(
                    source.at[
                        :,
                        pl.ds(part * rows, rows),
                        pl.ds(start, width),
                    ],
                    held.at[part],
                    in_sems.at[part],
                )
                for part in range(devices)
            ]
            stores = [
                pltpu.make_async_copy(held.at[part], out.at[part], out_sems.at[part])
                for part in range(devices)
            ]
            for load in loads:
                load.start()
            for load, store in zip(loads, stores):
                load.wait()
                store.start()
            for store in stores:
                store.wait()

        @pl.when(info_ref[0] == 0)
        def _():
            move(gate_ref)

        @pl.when(info_ref[0] != 0)
        def _():
            move(up_ref)

    return step_call(
        kernel,
        token,
        (info, gate, up),
        [SMEM, ANY, ANY],
        [jax.ShapeDtypeStruct((devices, sources, rows, width), gate.dtype)],
        [ANY],
        scratch_shapes=[
            pltpu.VMEM((devices, sources, rows, width), gate.dtype),
            pltpu.SemaphoreType.DMA((devices,)),
            pltpu.SemaphoreType.DMA((devices,)),
        ],
        name="pack",
    )


def hold(token, value, earlier):
    def kernel(*refs):
        pass

    (value,), token = step_call(
        kernel,
        token,
        (value, *earlier),
        [ANY] * (1 + len(earlier)),
        [jax.ShapeDtypeStruct(value.shape, value.dtype)],
        [ANY],
        input_output_aliases={0: 0},
        name="hold",
    )
    return value, token


def merge(token, slots, factors, rows_of, start, blocks):
    devices, sources, rows, width = rows_of.shape
    steps, column_blocks = blocks
    step = rows // steps
    first = start // BLOCK

    def kernel(slots_ref, factors_ref, rows_ref, out_ref, total):
        piece = pl.program_id(0)

        @pl.when(piece == 0)
        def _():
            total[...] = jnp.zeros_like(total)

        for number in range(sources):
            source = piece * sources + number
            slot = slots_ref[source]
            for index in range(steps):
                for part in range(width // BLOCK):
                    base = (source * steps + index) * column_blocks + first
                    lanes = slice(part * BLOCK, (part + 1) * BLOCK)
                    place = slice(index * step, (index + 1) * step)
                    total[slot, place, lanes] += (
                        rows_ref[0, number, place, lanes].astype(jnp.float32)
                        * factors_ref[base + part]
                    )

        @pl.when(piece == devices - 1)
        def _():
            out_ref[...] = total[...].astype(jnp.bfloat16)

    (merged,), token = step_call(
        kernel,
        token,
        (slots, factors, rows_of),
        [SMEM, SMEM, pl.BlockSpec((1, sources, rows, width), lambda i: (i, 0, 0, 0))],
        [jax.ShapeDtypeStruct((devices, rows, width), jnp.bfloat16)],
        [pl.BlockSpec((devices, rows, width), lambda i: (0, 0, 0))],
        grid=(devices,),
        scratch_shapes=[pltpu.VMEM((devices, rows, width), jnp.float32)],
        name="merge",
    )
    return merged, token


def run_chunk(token, info, grouped, own, partner, outputs, start, full, devices):
    depth, width = own.shape
    count = grouped.shape[0]
    each = count // devices
    factor = 1.0 / math.sqrt(D)

    def kernel(info_ref, grouped_ref, own_ref, partner_ref, *rest):
        gate_out, up_out, hidden_ref, whole, in_sems, out_sems = rest[len(outputs) :]
        halves = [whole.at[:, pl.ds(index * width, width)] for index in range(2)]

        def fill(*sources):
            loads = [
                pltpu.make_async_copy(source, half, in_sems.at[index])
                for index, (source, half) in enumerate(zip(sources, halves))
            ]
            for load in loads:
                load.start()
            for load in loads:
                load.wait()

        @pl.when(info_ref[0] == 0)
        def _():
            fill(own_ref, partner_ref)

        @pl.when(info_ref[0] != 0)
        def _():
            fill(partner_ref, own_ref)

        stores = [
            pltpu.make_async_copy(half, out.at[0, :, pl.ds(start, width)], out_sems.at[index])
            for index, (half, out) in enumerate(zip(halves, (gate_out, up_out)))
        ]
        for store in stores:
            store.start()
        values = jnp.dot(grouped_ref[...], whole[...], preferred_element_type=jnp.float32)
        gate_value = values[:, :width] * factor
        up_value = values[:, width:] * factor
        hidden = (gate_value / (1.0 + jnp.exp(-gate_value)) * up_value).astype(jnp.bfloat16)
        hidden_ref[...] = hidden.reshape(devices, each, width)
        for store in stores:
            store.wait()

    weights = jax.ShapeDtypeStruct((1, depth, full), jnp.bfloat16)
    return step_call(
        kernel,
        token,
        (info, grouped, own, partner, *outputs),
        [SMEM, VMEM, ANY, ANY] + [ANY] * len(outputs),
        [weights, weights, jax.ShapeDtypeStruct((devices, each, width), jnp.bfloat16)],
        [ANY, ANY, VMEM],
        scratch_shapes=[
            pltpu.VMEM((depth, 2 * width), jnp.bfloat16),
            pltpu.SemaphoreType.DMA((2,)),
            pltpu.SemaphoreType.DMA((2,)),
        ],
        input_output_aliases={4 + index: index for index in range(len(outputs))},
        name="run_chunk",
    )


def plan(count):
    order = [("pack", 0), ("raw", 0), ("pack", 1), ("raw", 1), ("sum", 0)]
    for chunk in range(count):
        if chunk + 2 < count:
            order.append(("pack", chunk + 2))
        order.append(("back", chunk))
        if chunk + 1 < count:
            order.append(("sum", chunk + 1))
        if chunk >= 1:
            order.append(("run", chunk - 1))
        order.append(("trade", chunk))
        if chunk + 2 < count:
            order.append(("raw", chunk + 2))
    order.extend([("give", 0), ("run", count - 1), ("give", 1)])
    return order


def route_slots(routes, merged_count, tok_dev):
    experts = jnp.arange(merged_count, dtype=jnp.int32)
    hit_table = jnp.sum((routes[:, :, None] == experts).astype(jnp.int32), axis=1)
    hit_table = hit_table.reshape(-1, tok_dev, merged_count)
    position_lookup = jnp.cumsum(hit_table, axis=1) - hit_table
    return (hit_table, position_lookup)


def chunk_widths(blocks):
    widths = []
    while blocks > 0:
        widths.append(max(1, (blocks + 1) // 2 if blocks > 3 else blocks - 1))
        blocks -= widths[-1]
    return widths


def shards(tokens, routes, quant_gate, quant_up, gate_scales, up_scales, cluster_ids, frequency):
    expert_count = lax.axis_size("expert")
    own_index = lax.axis_index("expert")
    group_count = lax.axis_size("groups")
    half = lax.axis_index("groups") % 2
    depth, full = quant_gate.shape[1:]
    tok_dev = tokens.shape[0]
    top_count = routes.shape[1]
    capacity = min(tok_dev, 2 * tok_dev * top_count // expert_count)

    partners = [(g, g ^ 1) for g in range(group_count)]

    def exchange(pieces):
        return lax.all_to_all(pieces, "expert", 0, 0, tiled=True)

    info = jnp.stack([half]).astype(jnp.int32)
    rows = depth // expert_count
    step = math.gcd(rows, BLOCK)
    slots = cluster_ids[:, 0]
    weights = cluster_weights(cluster_ids, frequency)
    scales = jnp.where(half == 0, gate_scales, up_scales)
    row_blocks = (own_index * rows + step * jnp.arange(rows // step, dtype=jnp.int32)) // BLOCK
    factors = jnp.take(scales, row_blocks, axis=1) * weights[:, None, None]
    blocks_of_rows = factors.shape[1:]
    factors = factors.reshape(-1)

    hit_table, position_lookup = route_slots(routes, expert_count, tok_dev)
    positions = jnp.arange(capacity, dtype=jnp.int32)

    def in_blocks(table):
        column = lax.dynamic_index_in_dim(table, own_index, 2, keepdims=False)
        return column.reshape(expert_count, 1, tok_dev)

    placing = (
        (in_blocks(hit_table) == 1) & (in_blocks(position_lookup) == positions[None, :, None])
    ).astype(jnp.bfloat16)

    experts = jnp.arange(expert_count, dtype=jnp.int32)
    local_routes = lax.dynamic_slice_in_dim(routes, own_index * tok_dev, tok_dev, 0)
    own_slots = lax.dynamic_index_in_dim(position_lookup, own_index, 0, keepdims=False)
    chosen = local_routes[:, :, None] == experts
    slot_of = jnp.sum(jnp.where(chosen, own_slots[:, None, :], 0), axis=2)
    picking = (chosen[:, :, :, None] & (slot_of[:, :, None, None] == positions)).astype(
        jnp.bfloat16
    )
    picking = picking.reshape(tok_dev * top_count, expert_count * capacity)

    widths = chunk_widths(full // BLOCK)
    starts = [BLOCK * sum(widths[:chunk]) for chunk in range(len(widths))]
    token = jnp.zeros(TOKEN.shape, TOKEN.dtype)
    everyone = lax.all_gather(tokens, "expert", axis=0, tiled=True)
    arrived = jnp.einsum(
        "jct,jtd->jcd",
        placing,
        everyone.reshape(expert_count, tok_dev, everyone.shape[1]),
        preferred_element_type=jnp.float32,
    ).astype(jnp.bfloat16)
    arrived = lax.all_gather(arrived, "mp", axis=2, tiled=True)
    grouped = arrived.reshape(expert_count * capacity, depth)
    pieces, gathered, merged, own, partner, hiddens = ({} for _ in range(6))
    outputs, returned, last = (), [], len(widths) - 1
    for name, c in plan(len(widths)):
        start, width = starts[c], widths[c] * BLOCK
        if name == "pack":
            (pieces[c],), token = pack(
                token, info, quant_gate, quant_up, start, width, expert_count
            )
        elif name == "raw":
            if c >= 2:
                pieces[c], token = hold(token, pieces[c], [])
            gathered[c] = exchange(pieces[c])
        elif name == "sum":
            merged[c], token = merge(token, slots, factors, gathered[c], start, blocks_of_rows)
        elif name == "back":
            earlier = [gathered[c + 1]] if c + 1 in gathered else []
            earlier += [placing, picking] if c == 0 else [grouped] if c == 1 else []
            merged[c], token = hold(token, merged[c], earlier)
            own[c] = exchange(merged[c])
        elif name == "trade":
            own[c], token = hold(token, own[c].reshape(depth, width), [])
            partner[c] = lax.ppermute(own[c], "groups", partners)
        elif name == "run":
            (*outputs, hiddens[c]), token = run_chunk(
                token, info, grouped, own[c], partner[c], outputs, start, full, expert_count
            )
        else:
            batch = [hiddens[i] for i in (range(last) if c == 0 else range(last, last + 1))]
            hidden, token = hold(token, jnp.concatenate(batch, axis=2), returned[:c])
            returned.append(exchange(hidden))

    finished = [
        jnp.dot(
            picking,
            part.reshape(expert_count * capacity, part.shape[2]),
            preferred_element_type=jnp.float32,
        ).astype(jnp.bfloat16)
        for part in returned
    ]
    output = jnp.concatenate(finished, axis=1)
    merged_gate, merged_up = outputs
    return (merged_gate, merged_up, output.reshape(tok_dev, top_count, full))


def solution(mesh):
    return jax.shard_map(
        shards,
        mesh=mesh,
        in_specs=(
            P(("groups", "expert"), "mp"),
            P("groups", None),
            P("expert", None, "mp"),
            P("expert", None, "mp"),
            P(None, None, "mp"),
            P(None, None, "mp"),
            P(),
            P(),
        ),
        out_specs=(
            P(("groups", "expert"), None, "mp"),
            P(("groups", "expert"), None, "mp"),
            P(("groups", "expert"), None, "mp"),
        ),
        check_vma=False,
    )
```

```python
import math

import jax
import jax.numpy as jnp
from jax import lax
from jax.experimental import pallas as pl
from jax.experimental.pallas import tpu as pltpu
from jax.sharding import PartitionSpec as P

D = 2560
BLOCK = 128
PLANES = 4
TOKEN = jax.ShapeDtypeStruct((8, 128), jnp.float32)
ANY = pl.BlockSpec(memory_space=pl.ANY)
SMEM = pl.BlockSpec(memory_space=pltpu.SMEM)
VMEM = pl.BlockSpec(memory_space=pltpu.VMEM)
VMEM_LIMIT = 60 * 1024 * 1024


def cluster_weights(cluster_ids, frequency):
    ids = cluster_ids[:, 0]
    same = (ids[:, None] == ids[None, :]).astype(jnp.float32)
    return frequency / jnp.sum(same * frequency[None, :], axis=1)


def step_call(kernel, token, operands, in_specs, out_shape, out_specs, **options):
    count = len(operands)

    def ordered(*refs):
        kernel(*refs[:count], *refs[count + 1 : count + 1 + len(out_shape)], *refs[count + 2 + len(out_shape) :])

    *results, token = pl.pallas_call(
        ordered,
        out_shape=[*out_shape, TOKEN],
        in_specs=[*in_specs, ANY],
        out_specs=[*out_specs, ANY],
        compiler_params=pltpu.CompilerParams(vmem_limit_bytes=VMEM_LIMIT),
        cost_estimate=pl.CostEstimate(flops=0, bytes_accessed=0, transcendentals=0),
        **options,
    )(*operands, token)
    return results, token


def pack(token, info, gate, up, start, width, devices):
    sources, depth, _ = gate.shape
    rows = depth // devices

    def kernel(info_ref, gate_ref, up_ref, *rest):
        out, held, in_sems, out_sems = rest

        def move(source):
            loads = [
                pltpu.make_async_copy(
                    source.at[
                        :,
                        pl.ds(part * rows, rows),
                        pl.ds(start, width),
                    ],
                    held.at[part],
                    in_sems.at[part],
                )
                for part in range(devices)
            ]
            stores = [
                pltpu.make_async_copy(held.at[part], out.at[part], out_sems.at[part])
                for part in range(devices)
            ]
            for load in loads:
                load.start()
            for load, store in zip(loads, stores):
                load.wait()
                store.start()
            for store in stores:
                store.wait()

        @pl.when(info_ref[0] == 0)
        def _():
            move(gate_ref)

        @pl.when(info_ref[0] != 0)
        def _():
            move(up_ref)

    return step_call(
        kernel,
        token,
        (info, gate, up),
        [SMEM, ANY, ANY],
        [jax.ShapeDtypeStruct((devices, sources, rows, width), gate.dtype)],
        [ANY],
        scratch_shapes=[
            pltpu.VMEM((devices, sources, rows, width), gate.dtype),
            pltpu.SemaphoreType.DMA((devices,)),
            pltpu.SemaphoreType.DMA((devices,)),
        ],
        name="pack",
    )


def hold(token, value, earlier):
    def kernel(*refs):
        pass

    (value,), token = step_call(
        kernel,
        token,
        (value, *earlier),
        [ANY] * (1 + len(earlier)),
        [jax.ShapeDtypeStruct(value.shape, value.dtype)],
        [ANY],
        input_output_aliases={0: 0},
        name="hold",
    )
    return value, token


def merge(token, slots, factors, rows_of, start, blocks):
    devices, sources, rows, width = rows_of.shape
    steps, column_blocks = blocks
    step = rows // steps
    first = start // BLOCK

    def kernel(slots_ref, factors_ref, rows_ref, out_ref, total):
        piece = pl.program_id(0)

        @pl.when(piece == 0)
        def _():
            total[...] = jnp.zeros_like(total)

        for number in range(sources):
            source = piece * sources + number
            slot = slots_ref[source]
            for index in range(steps):
                for part in range(width // BLOCK):
                    base = (source * steps + index) * column_blocks + first
                    lanes = slice(part * BLOCK, (part + 1) * BLOCK)
                    place = slice(index * step, (index + 1) * step)
                    total[slot, place, lanes] += (
                        rows_ref[0, number, place, lanes].astype(jnp.float32)
                        * factors_ref[base + part]
                    )

        @pl.when(piece == devices - 1)
        def _():
            out_ref[...] = total[...].astype(jnp.bfloat16)

    (merged,), token = step_call(
        kernel,
        token,
        (slots, factors, rows_of),
        [SMEM, SMEM, pl.BlockSpec((1, sources, rows, width), lambda i: (i, 0, 0, 0))],
        [jax.ShapeDtypeStruct((devices, rows, width), jnp.bfloat16)],
        [pl.BlockSpec((devices, rows, width), lambda i: (0, 0, 0))],
        grid=(devices,),
        scratch_shapes=[pltpu.VMEM((devices, rows, width), jnp.float32)],
        name="merge",
    )
    return merged, token


def pair(token, tokens, other):
    def kernel(tokens_ref, other_ref, out_ref):
        out_ref[0] = tokens_ref[...]
        out_ref[1] = other_ref[...]

    (both,), token = step_call(
        kernel,
        token,
        (tokens, other),
        [VMEM, VMEM],
        [jax.ShapeDtypeStruct((2,) + tokens.shape, tokens.dtype)],
        [VMEM],
        name="pair",
    )
    return both, token


def line(token, info, both, nearby):
    _, tok_dev, width = both.shape

    def kernel(info_ref, both_ref, nearby_ref, out_ref):
        level = info_ref[1]
        for index, other in enumerate((both_ref, nearby_ref)):
            out_ref[level ^ index] = other[0]
            out_ref[level ^ index ^ (PLANES // 2)] = other[1]

    (whole,), token = step_call(
        kernel,
        token,
        (info, both, nearby),
        [SMEM, VMEM, VMEM],
        [jax.ShapeDtypeStruct((PLANES, tok_dev, width), both.dtype)],
        [VMEM],
        name="line",
    )
    return whole, token


def run_chunk(token, info, grouped, own, partner, outputs, start, full, blocks):
    depth, width = own.shape
    count = grouped.shape[0]
    each = count // len(blocks)
    factor = 1.0 / math.sqrt(D)

    def kernel(info_ref, grouped_ref, own_ref, partner_ref, *rest):
        gate_out, up_out, hidden_ref, whole, in_sems, out_sems = rest[len(outputs) :]
        halves = [whole.at[:, pl.ds(index * width, width)] for index in range(2)]

        def fill(*sources):
            loads = [
                pltpu.make_async_copy(source, half, in_sems.at[index])
                for index, (source, half) in enumerate(zip(sources, halves))
            ]
            for load in loads:
                load.start()
            for load in loads:
                load.wait()

        @pl.when(info_ref[0] == 0)
        def _():
            fill(own_ref, partner_ref)

        @pl.when(info_ref[0] != 0)
        def _():
            fill(partner_ref, own_ref)

        stores = [
            pltpu.make_async_copy(half, out.at[0, :, pl.ds(start, width)], out_sems.at[index])
            for index, (half, out) in enumerate(zip(halves, (gate_out, up_out)))
        ]
        for store in stores:
            store.start()
        values = jnp.dot(grouped_ref[...], whole[...], preferred_element_type=jnp.float32)
        gate_value = values[:, :width] * factor
        up_value = values[:, width:] * factor
        hidden = (gate_value / (1.0 + jnp.exp(-gate_value)) * up_value).astype(jnp.bfloat16)
        for index, block in enumerate(blocks):
            hidden_ref[block] = hidden[index * each : (index + 1) * each]
        for store in stores:
            store.wait()

    weights = jax.ShapeDtypeStruct((1, depth, full), jnp.bfloat16)
    return step_call(
        kernel,
        token,
        (info, grouped, own, partner, *outputs),
        [SMEM, VMEM, ANY, ANY] + [ANY] * len(outputs),
        [weights, weights, jax.ShapeDtypeStruct((len(blocks), each, width), jnp.bfloat16)],
        [ANY, ANY, VMEM],
        scratch_shapes=[
            pltpu.VMEM((depth, 2 * width), jnp.bfloat16),
            pltpu.SemaphoreType.DMA((2,)),
            pltpu.SemaphoreType.DMA((2,)),
        ],
        input_output_aliases={4 + index: index for index in range(len(outputs))},
        name="run_chunk",
    )


def first_runs(count):
    return max(1, count - 2)


def plan(count):
    cut = first_runs(count)
    order = [("pack", 0), ("raw", 0), ("pack", 1), ("pair", 0), ("line", 0), ("raw", 1), ("sum", 0)]
    for chunk in range(count):
        if chunk + 2 < count:
            order.append(("pack", chunk + 2))
        order.append(("back", chunk))
        if chunk + 1 < count:
            order.append(("sum", chunk + 1))
        if chunk + 1 == count:
            order.extend(("run", earlier) for earlier in range(cut))
        order.append(("trade", chunk))
        if chunk + 2 < count:
            order.append(("raw", chunk + 2))
    order.append(("give", 0))
    order.extend(("run", later) for later in range(cut, count))
    order.append(("give", 1))
    return order


def route_slots(routes, merged_count, tok_dev):
    experts = jnp.arange(merged_count, dtype=jnp.int32)
    hit_table = jnp.sum((routes[:, :, None] == experts).astype(jnp.int32), axis=1)
    hit_table = hit_table.reshape(-1, tok_dev, merged_count)
    position_lookup = jnp.cumsum(hit_table, axis=1) - hit_table
    return (hit_table, position_lookup)


def chunk_widths(blocks):
    widths = []
    while blocks > 0:
        widths.append(max(1, (blocks + 1) // 2 if blocks > 3 else blocks - 1))
        blocks -= widths[-1]
    return widths


def shards(tokens, routes, quant_gate, quant_up, gate_scales, up_scales, cluster_ids, frequency):
    expert_count = lax.axis_size("expert")
    own_index = lax.axis_index("expert")
    group_count = lax.axis_size("groups")
    half = lax.axis_index("groups") % 2
    depth, full = quant_gate.shape[1:]
    tok_dev = tokens.shape[0]
    top_count = routes.shape[1]
    capacity = min(tok_dev, 2 * tok_dev * top_count // expert_count)

    plane = expert_count // PLANES
    by_plane = [[z * plane + p for p in range(plane)] for z in range(PLANES)]
    across = [(i, (i + expert_count // 2) % expert_count) for i in range(expert_count)]
    beside = [(i, (i // plane ^ 1) * plane + i % plane) for i in range(expert_count)]
    partners = [(g, g ^ 1) for g in range(group_count)]

    def exchange(pieces):
        return lax.all_to_all(pieces, "expert", 0, 0, tiled=True)

    info = jnp.stack([half, own_index // plane]).astype(jnp.int32)
    rows = depth // expert_count
    step = math.gcd(rows, BLOCK)
    slots = cluster_ids[:, 0]
    weights = cluster_weights(cluster_ids, frequency)
    scales = jnp.where(half == 0, gate_scales, up_scales)
    row_blocks = (own_index * rows + step * jnp.arange(rows // step, dtype=jnp.int32)) // BLOCK
    factors = jnp.take(scales, row_blocks, axis=1) * weights[:, None, None]
    blocks_of_rows = factors.shape[1:]
    factors = factors.reshape(-1)

    hit_table, position_lookup = route_slots(routes, expert_count, tok_dev)
    positions = jnp.arange(capacity, dtype=jnp.int32)

    blocks = [z * plane + p for p in range(plane) for z in range(PLANES)]

    def in_blocks(table):
        column = lax.dynamic_index_in_dim(table, own_index, 2, keepdims=False)
        column = column.reshape(PLANES, plane, tok_dev).transpose(1, 0, 2)
        return column.reshape(expert_count, 1, tok_dev)

    placing = (
        (in_blocks(hit_table) == 1) & (in_blocks(position_lookup) == positions[None, :, None])
    ).astype(jnp.bfloat16)

    experts = jnp.arange(expert_count, dtype=jnp.int32)
    local_routes = lax.dynamic_slice_in_dim(routes, own_index * tok_dev, tok_dev, 0)
    own_slots = lax.dynamic_index_in_dim(position_lookup, own_index, 0, keepdims=False)
    chosen = local_routes[:, :, None] == experts
    slot_of = jnp.sum(jnp.where(chosen, own_slots[:, None, :], 0), axis=2)
    picking = (chosen[:, :, :, None] & (slot_of[:, :, None, None] == positions)).astype(
        jnp.bfloat16
    )
    picking = picking.reshape(tok_dev * top_count, expert_count * capacity)

    widths = chunk_widths(full // BLOCK)
    starts = [BLOCK * sum(widths[:chunk]) for chunk in range(len(widths))]
    token = jnp.zeros(TOKEN.shape, TOKEN.dtype)
    opposite = lax.ppermute(tokens, "expert", across)
    pieces, gathered, merged, own, partner, hiddens = ({} for _ in range(6))
    outputs, returned, last = (), [], len(widths) - 1
    cut = first_runs(len(widths))
    for name, c in plan(len(widths)):
        start, width = starts[c], widths[c] * BLOCK
        if name == "pack":
            (pieces[c],), token = pack(
                token, info, quant_gate, quant_up, start, width, expert_count
            )
        elif name == "pair":
            both, token = pair(token, tokens, opposite)
            nearby = lax.ppermute(both, "expert", beside)
        elif name == "line":
            whole, token = line(token, info, both, nearby)
            everyone = lax.all_gather(whole, "expert", axis=0, tiled=True, axis_index_groups=by_plane)
            arrived = jnp.einsum(
                "jct,jtd->jcd", placing, everyone, preferred_element_type=jnp.float32
            ).astype(jnp.bfloat16)
            arrived = lax.all_gather(arrived, "mp", axis=2, tiled=True)
            grouped = arrived.reshape(expert_count * capacity, depth)
        elif name == "raw":
            if c >= 1:
                pieces[c], token = hold(token, pieces[c], [gathered[0]] if c == 1 else [])
            gathered[c] = exchange(pieces[c])
        elif name == "sum":
            merged[c], token = merge(token, slots, factors, gathered[c], start, blocks_of_rows)
        elif name == "back":
            earlier = [gathered[c + 1]] if c + 1 in gathered else []
            earlier += [placing, picking] if c == 0 else [grouped] if c == 1 else []
            earlier += [partner[c - 1]] if 0 < c < last else []
            merged[c], token = hold(token, merged[c], earlier)
            own[c] = exchange(merged[c])
        elif name == "trade":
            own[c], token = hold(token, own[c].reshape(depth, width), [])
            partner[c] = lax.ppermute(own[c], "groups", partners)
        elif name == "run":
            (*outputs, hiddens[c]), token = run_chunk(
                token, info, grouped, own[c], partner[c], outputs, start, full, blocks
            )
        else:
            batch = [hiddens[i] for i in (range(cut) if c == 0 else range(cut, last + 1))]
            hidden, token = hold(token, jnp.concatenate(batch, axis=2), returned[:c])
            returned.append(exchange(hidden))

    finished = [
        jnp.dot(
            picking,
            part.reshape(expert_count * capacity, part.shape[2]),
            preferred_element_type=jnp.float32,
        ).astype(jnp.bfloat16)
        for part in returned
    ]
    output = jnp.concatenate(finished, axis=1)
    merged_gate, merged_up = outputs
    return (merged_gate, merged_up, output.reshape(tok_dev, top_count, full))


def solution(mesh):
    return jax.shard_map(
        shards,
        mesh=mesh,
        in_specs=(
            P(("groups", "expert"), "mp"),
            P("groups", None),
            P("expert", None, "mp"),
            P("expert", None, "mp"),
            P(None, None, "mp"),
            P(None, None, "mp"),
            P(),
            P(),
        ),
        out_specs=(
            P(("groups", "expert"), None, "mp"),
            P(("groups", "expert"), None, "mp"),
            P(("groups", "expert"), None, "mp"),
        ),
        check_vma=False,
    )
```

```python
import math

import jax
import jax.numpy as jnp
from jax import lax
from jax.experimental import pallas as pl
from jax.experimental.pallas import tpu as pltpu
from jax.sharding import PartitionSpec as P

D = 2560
BLOCK = 128
PLANES = 4
TOKEN = jax.ShapeDtypeStruct((8, 128), jnp.float32)
ANY = pl.BlockSpec(memory_space=pl.ANY)
SMEM = pl.BlockSpec(memory_space=pltpu.SMEM)
VMEM = pl.BlockSpec(memory_space=pltpu.VMEM)
VMEM_LIMIT = 60 * 1024 * 1024


def cluster_weights(cluster_ids, frequency):
    ids = cluster_ids[:, 0]
    same = (ids[:, None] == ids[None, :]).astype(jnp.float32)
    return frequency / jnp.sum(same * frequency[None, :], axis=1)


def step_call(kernel, token, operands, in_specs, out_shape, out_specs, **options):
    count = len(operands)

    def ordered(*refs):
        kernel(*refs[:count], *refs[count + 1 : count + 1 + len(out_shape)], *refs[count + 2 + len(out_shape) :])

    *results, token = pl.pallas_call(
        ordered,
        out_shape=[*out_shape, TOKEN],
        in_specs=[*in_specs, ANY],
        out_specs=[*out_specs, ANY],
        compiler_params=pltpu.CompilerParams(vmem_limit_bytes=VMEM_LIMIT),
        cost_estimate=pl.CostEstimate(flops=0, bytes_accessed=0, transcendentals=0),
        **options,
    )(*operands, token)
    return results, token


def pack(token, info, gate, up, start, width, devices):
    sources, depth, _ = gate.shape
    rows = depth // devices

    def kernel(info_ref, gate_ref, up_ref, *rest):
        out, held, in_sems, out_sems = rest

        def move(source):
            loads = [
                pltpu.make_async_copy(
                    source.at[
                        :,
                        pl.ds(part * rows, rows),
                        pl.ds(start, width),
                    ],
                    held.at[part],
                    in_sems.at[part],
                )
                for part in range(devices)
            ]
            stores = [
                pltpu.make_async_copy(held.at[part], out.at[part], out_sems.at[part])
                for part in range(devices)
            ]
            for load in loads:
                load.start()
            for load, store in zip(loads, stores):
                load.wait()
                store.start()
            for store in stores:
                store.wait()

        @pl.when(info_ref[0] == 0)
        def _():
            move(gate_ref)

        @pl.when(info_ref[0] != 0)
        def _():
            move(up_ref)

    return step_call(
        kernel,
        token,
        (info, gate, up),
        [SMEM, ANY, ANY],
        [jax.ShapeDtypeStruct((devices, sources, rows, width), gate.dtype)],
        [ANY],
        scratch_shapes=[
            pltpu.VMEM((devices, sources, rows, width), gate.dtype),
            pltpu.SemaphoreType.DMA((devices,)),
            pltpu.SemaphoreType.DMA((devices,)),
        ],
        name="pack",
    )


def hold(token, value, earlier):
    def kernel(*refs):
        pass

    (value,), token = step_call(
        kernel,
        token,
        (value, *earlier),
        [ANY] * (1 + len(earlier)),
        [jax.ShapeDtypeStruct(value.shape, value.dtype)],
        [ANY],
        input_output_aliases={0: 0},
        name="hold",
    )
    return value, token


def merge(token, slots, factors, rows_of, start, blocks):
    devices, sources, rows, width = rows_of.shape
    steps, column_blocks = blocks
    step = rows // steps
    first = start // BLOCK

    def kernel(slots_ref, factors_ref, rows_ref, out_ref, total):
        piece = pl.program_id(0)

        @pl.when(piece == 0)
        def _():
            total[...] = jnp.zeros_like(total)

        for number in range(sources):
            source = piece * sources + number
            slot = slots_ref[source]
            for index in range(steps):
                for part in range(width // BLOCK):
                    base = (source * steps + index) * column_blocks + first
                    lanes = slice(part * BLOCK, (part + 1) * BLOCK)
                    place = slice(index * step, (index + 1) * step)
                    total[slot, place, lanes] += (
                        rows_ref[0, number, place, lanes].astype(jnp.float32)
                        * factors_ref[base + part]
                    )

        @pl.when(piece == devices - 1)
        def _():
            out_ref[...] = total[...].astype(jnp.bfloat16)

    (merged,), token = step_call(
        kernel,
        token,
        (slots, factors, rows_of),
        [SMEM, SMEM, pl.BlockSpec((1, sources, rows, width), lambda i: (i, 0, 0, 0))],
        [jax.ShapeDtypeStruct((devices, rows, width), jnp.bfloat16)],
        [pl.BlockSpec((devices, rows, width), lambda i: (0, 0, 0))],
        grid=(devices,),
        scratch_shapes=[pltpu.VMEM((devices, rows, width), jnp.float32)],
        name="merge",
    )
    return merged, token


def pair(token, tokens, other):
    def kernel(tokens_ref, other_ref, out_ref):
        out_ref[0] = tokens_ref[...]
        out_ref[1] = other_ref[...]

    (both,), token = step_call(
        kernel,
        token,
        (tokens, other),
        [VMEM, VMEM],
        [jax.ShapeDtypeStruct((2,) + tokens.shape, tokens.dtype)],
        [VMEM],
        name="pair",
    )
    return both, token


def line(token, info, both, nearby):
    _, tok_dev, width = both.shape

    def kernel(info_ref, both_ref, nearby_ref, out_ref):
        level = info_ref[1]
        for index, other in enumerate((both_ref, nearby_ref)):
            out_ref[level ^ index] = other[0]
            out_ref[level ^ index ^ (PLANES // 2)] = other[1]

    (whole,), token = step_call(
        kernel,
        token,
        (info, both, nearby),
        [SMEM, VMEM, VMEM],
        [jax.ShapeDtypeStruct((PLANES, tok_dev, width), both.dtype)],
        [VMEM],
        name="line",
    )
    return whole, token


def run_chunk(token, info, grouped, own, partner, outputs, start, full, blocks):
    depth, width = own.shape
    count = grouped.shape[0]
    each = count // len(blocks)
    factor = 1.0 / math.sqrt(D)

    def kernel(info_ref, grouped_ref, own_ref, partner_ref, *rest):
        gate_out, up_out, hidden_ref, whole, in_sems, out_sems = rest[len(outputs) :]
        halves = [whole.at[:, pl.ds(index * width, width)] for index in range(2)]

        def fill(*sources):
            loads = [
                pltpu.make_async_copy(source, half, in_sems.at[index])
                for index, (source, half) in enumerate(zip(sources, halves))
            ]
            for load in loads:
                load.start()
            for load in loads:
                load.wait()

        @pl.when(info_ref[0] == 0)
        def _():
            fill(own_ref, partner_ref)

        @pl.when(info_ref[0] != 0)
        def _():
            fill(partner_ref, own_ref)

        stores = [
            pltpu.make_async_copy(half, out.at[0, :, pl.ds(start, width)], out_sems.at[index])
            for index, (half, out) in enumerate(zip(halves, (gate_out, up_out)))
        ]
        for store in stores:
            store.start()
        values = jnp.dot(grouped_ref[...], whole[...], preferred_element_type=jnp.float32)
        gate_value = values[:, :width] * factor
        up_value = values[:, width:] * factor
        hidden = (gate_value / (1.0 + jnp.exp(-gate_value)) * up_value).astype(jnp.bfloat16)
        for index, block in enumerate(blocks):
            hidden_ref[block] = hidden[index * each : (index + 1) * each]
        for store in stores:
            store.wait()

    weights = jax.ShapeDtypeStruct((1, depth, full), jnp.bfloat16)
    return step_call(
        kernel,
        token,
        (info, grouped, own, partner, *outputs),
        [SMEM, VMEM, ANY, ANY] + [ANY] * len(outputs),
        [weights, weights, jax.ShapeDtypeStruct((len(blocks), each, width), jnp.bfloat16)],
        [ANY, ANY, VMEM],
        scratch_shapes=[
            pltpu.VMEM((depth, 2 * width), jnp.bfloat16),
            pltpu.SemaphoreType.DMA((2,)),
            pltpu.SemaphoreType.DMA((2,)),
        ],
        input_output_aliases={4 + index: index for index in range(len(outputs))},
        name="run_chunk",
    )


def first_runs(count):
    return max(1, count - 1)


def plan(count):
    cut = first_runs(count)
    order = [("pack", 0), ("raw", 0), ("pack", 1), ("raw", 1), ("sum", 0)]
    for chunk in range(count):
        if chunk + 2 < count:
            order.append(("pack", chunk + 2))
        if chunk == 0:
            order.append(("pair", 0))
        order.append(("back", chunk))
        if chunk + 1 < count:
            order.append(("sum", chunk + 1))
        if chunk == 0:
            order.append(("line", 0))
        if chunk + 1 == count:
            order.extend(("run", earlier) for earlier in range(cut))
        order.append(("trade", chunk))
        if chunk + 2 < count:
            order.append(("raw", chunk + 2))
    order.append(("give", 0))
    order.extend(("run", later) for later in range(cut, count))
    order.append(("give", 1))
    return order


def route_slots(routes, merged_count, tok_dev):
    experts = jnp.arange(merged_count, dtype=jnp.int32)
    hit_table = jnp.sum((routes[:, :, None] == experts).astype(jnp.int32), axis=1)
    hit_table = hit_table.reshape(-1, tok_dev, merged_count)
    position_lookup = jnp.cumsum(hit_table, axis=1) - hit_table
    return (hit_table, position_lookup)


def chunk_widths(blocks):
    first = max(1, blocks // 2)
    second = max(1, blocks // 6)
    return [width for width in (first, second, blocks - first - second) if width > 0]


def shards(tokens, routes, quant_gate, quant_up, gate_scales, up_scales, cluster_ids, frequency):
    expert_count = lax.axis_size("expert")
    own_index = lax.axis_index("expert")
    group_count = lax.axis_size("groups")
    half = lax.axis_index("groups") % 2
    depth, full = quant_gate.shape[1:]
    tok_dev = tokens.shape[0]
    top_count = routes.shape[1]
    capacity = min(tok_dev, 2 * tok_dev * top_count // expert_count)

    plane = expert_count // PLANES
    by_plane = [[z * plane + p for p in range(plane)] for z in range(PLANES)]
    across = [(i, (i + expert_count // 2) % expert_count) for i in range(expert_count)]
    beside = [(i, (i // plane ^ 1) * plane + i % plane) for i in range(expert_count)]
    partners = [(g, g ^ 1) for g in range(group_count)]

    def exchange(pieces):
        return lax.all_to_all(pieces, "expert", 0, 0, tiled=True)

    info = jnp.stack([half, own_index // plane]).astype(jnp.int32)
    rows = depth // expert_count
    step = math.gcd(rows, BLOCK)
    slots = cluster_ids[:, 0]
    weights = cluster_weights(cluster_ids, frequency)
    scales = jnp.where(half == 0, gate_scales, up_scales)
    row_blocks = (own_index * rows + step * jnp.arange(rows // step, dtype=jnp.int32)) // BLOCK
    factors = jnp.take(scales, row_blocks, axis=1) * weights[:, None, None]
    blocks_of_rows = factors.shape[1:]
    factors = factors.reshape(-1)

    hit_table, position_lookup = route_slots(routes, expert_count, tok_dev)
    positions = jnp.arange(capacity, dtype=jnp.int32)

    blocks = [z * plane + p for p in range(plane) for z in range(PLANES)]

    def in_blocks(table):
        column = lax.dynamic_index_in_dim(table, own_index, 2, keepdims=False)
        column = column.reshape(PLANES, plane, tok_dev).transpose(1, 0, 2)
        return column.reshape(expert_count, 1, tok_dev)

    placing = (
        (in_blocks(hit_table) == 1) & (in_blocks(position_lookup) == positions[None, :, None])
    ).astype(jnp.bfloat16)

    experts = jnp.arange(expert_count, dtype=jnp.int32)
    local_routes = lax.dynamic_slice_in_dim(routes, own_index * tok_dev, tok_dev, 0)
    own_slots = lax.dynamic_index_in_dim(position_lookup, own_index, 0, keepdims=False)
    chosen = local_routes[:, :, None] == experts
    slot_of = jnp.sum(jnp.where(chosen, own_slots[:, None, :], 0), axis=2)
    picking = (chosen[:, :, :, None] & (slot_of[:, :, None, None] == positions)).astype(
        jnp.bfloat16
    )
    picking = picking.reshape(tok_dev * top_count, expert_count * capacity)

    widths = chunk_widths(full // BLOCK)
    starts = [BLOCK * sum(widths[:chunk]) for chunk in range(len(widths))]
    token = jnp.zeros(TOKEN.shape, TOKEN.dtype)
    opposite = lax.ppermute(tokens, "expert", across)
    pieces, gathered, merged, own, partner, hiddens = ({} for _ in range(6))
    outputs, returned, last = (), [], len(widths) - 1
    cut = first_runs(len(widths))
    for name, c in plan(len(widths)):
        start, width = starts[c], widths[c] * BLOCK
        if name == "pack":
            (pieces[c],), token = pack(
                token, info, quant_gate, quant_up, start, width, expert_count
            )
        elif name == "pair":
            both, token = pair(token, tokens, opposite)
            nearby = lax.ppermute(both, "expert", beside)
        elif name == "line":
            whole, token = line(token, info, both, nearby)
            everyone = lax.all_gather(whole, "expert", axis=0, tiled=True, axis_index_groups=by_plane)
            arrived = jnp.einsum(
                "jct,jtd->jcd", placing, everyone, preferred_element_type=jnp.float32
            ).astype(jnp.bfloat16)
            arrived = lax.all_gather(arrived, "mp", axis=2, tiled=True)
            grouped = arrived.reshape(expert_count * capacity, depth)
        elif name == "raw":
            if c >= 1:
                pieces[c], token = hold(token, pieces[c], [gathered[0]] if c == 1 else [])
            gathered[c] = exchange(pieces[c])
        elif name == "sum":
            merged[c], token = merge(token, slots, factors, gathered[c], start, blocks_of_rows)
        elif name == "back":
            earlier = [gathered[c + 1]] if c + 1 in gathered else []
            earlier += [placing, picking] if c == 0 else [grouped] if c == last else []
            earlier += [partner[c - 1]] if 0 < c < last else []
            merged[c], token = hold(token, merged[c], earlier)
            own[c] = exchange(merged[c])
        elif name == "trade":
            own[c], token = hold(token, own[c].reshape(depth, width), [])
            partner[c] = lax.ppermute(own[c], "groups", partners)
        elif name == "run":
            (*outputs, hiddens[c]), token = run_chunk(
                token, info, grouped, own[c], partner[c], outputs, start, full, blocks
            )
        else:
            batch = [hiddens[i] for i in (range(cut) if c == 0 else range(cut, last + 1))]
            hidden, token = hold(token, jnp.concatenate(batch, axis=2), returned[:c])
            returned.append(exchange(hidden))

    finished = [
        jnp.dot(
            picking,
            part.reshape(expert_count * capacity, part.shape[2]),
            preferred_element_type=jnp.float32,
        ).astype(jnp.bfloat16)
        for part in returned
    ]
    output = jnp.concatenate(finished, axis=1)
    merged_gate, merged_up = outputs
    return (merged_gate, merged_up, output.reshape(tok_dev, top_count, full))


def solution(mesh):
    return jax.shard_map(
        shards,
        mesh=mesh,
        in_specs=(
            P(("groups", "expert"), "mp"),
            P("groups", None),
            P("expert", None, "mp"),
            P("expert", None, "mp"),
            P(None, None, "mp"),
            P(None, None, "mp"),
            P(),
            P(),
        ),
        out_specs=(
            P(("groups", "expert"), None, "mp"),
            P(("groups", "expert"), None, "mp"),
            P(("groups", "expert"), None, "mp"),
        ),
        check_vma=False,
    )
```

```python
import math

import jax
import jax.numpy as jnp
from jax import lax
from jax.experimental import pallas as pl
from jax.experimental.pallas import tpu as pltpu
from jax.sharding import PartitionSpec as P

D = 2560
BLOCK = 128
PLANES = 4
TOKEN = jax.ShapeDtypeStruct((8, 128), jnp.float32)
ANY = pl.BlockSpec(memory_space=pl.ANY)
SMEM = pl.BlockSpec(memory_space=pltpu.SMEM)
VMEM = pl.BlockSpec(memory_space=pltpu.VMEM)
VMEM_LIMIT = 60 * 1024 * 1024


def cluster_weights(cluster_ids, frequency):
    ids = cluster_ids[:, 0]
    same = (ids[:, None] == ids[None, :]).astype(jnp.float32)
    return frequency / jnp.sum(same * frequency[None, :], axis=1)


def step_call(kernel, token, operands, in_specs, out_shape, out_specs, **options):
    count = len(operands)

    def ordered(*refs):
        kernel(*refs[:count], *refs[count + 1 : count + 1 + len(out_shape)], *refs[count + 2 + len(out_shape) :])

    *results, token = pl.pallas_call(
        ordered,
        out_shape=[*out_shape, TOKEN],
        in_specs=[*in_specs, ANY],
        out_specs=[*out_specs, ANY],
        compiler_params=pltpu.CompilerParams(vmem_limit_bytes=VMEM_LIMIT),
        cost_estimate=pl.CostEstimate(flops=0, bytes_accessed=0, transcendentals=0),
        **options,
    )(*operands, token)
    return results, token


def pack(token, info, gate, up, start, width, devices):
    sources, depth, _ = gate.shape
    rows = depth // devices

    def kernel(info_ref, gate_ref, up_ref, *rest):
        out, held, in_sems, out_sems = rest

        def move(source):
            loads = [
                pltpu.make_async_copy(
                    source.at[
                        :,
                        pl.ds(part * rows, rows),
                        pl.ds(start, width),
                    ],
                    held.at[part],
                    in_sems.at[part],
                )
                for part in range(devices)
            ]
            stores = [
                pltpu.make_async_copy(held.at[part], out.at[part], out_sems.at[part])
                for part in range(devices)
            ]
            for load in loads:
                load.start()
            for load, store in zip(loads, stores):
                load.wait()
                store.start()
            for store in stores:
                store.wait()

        @pl.when(info_ref[0] == 0)
        def _():
            move(gate_ref)

        @pl.when(info_ref[0] != 0)
        def _():
            move(up_ref)

    return step_call(
        kernel,
        token,
        (info, gate, up),
        [SMEM, ANY, ANY],
        [jax.ShapeDtypeStruct((devices, sources, rows, width), gate.dtype)],
        [ANY],
        scratch_shapes=[
            pltpu.VMEM((devices, sources, rows, width), gate.dtype),
            pltpu.SemaphoreType.DMA((devices,)),
            pltpu.SemaphoreType.DMA((devices,)),
        ],
        name="pack",
    )


def hold(token, value, earlier):
    def kernel(*refs):
        pass

    (value,), token = step_call(
        kernel,
        token,
        (value, *earlier),
        [ANY] * (1 + len(earlier)),
        [jax.ShapeDtypeStruct(value.shape, value.dtype)],
        [ANY],
        input_output_aliases={0: 0},
        name="hold",
    )
    return value, token


def merge(token, slots, factors, rows_of, start, blocks):
    devices, sources, rows, width = rows_of.shape
    steps, column_blocks = blocks
    step = rows // steps
    first = start // BLOCK

    def kernel(slots_ref, factors_ref, rows_ref, out_ref, total):
        piece = pl.program_id(0)

        @pl.when(piece == 0)
        def _():
            total[...] = jnp.zeros_like(total)

        for number in range(sources):
            source = piece * sources + number
            slot = slots_ref[source]
            for index in range(steps):
                for part in range(width // BLOCK):
                    base = (source * steps + index) * column_blocks + first
                    lanes = slice(part * BLOCK, (part + 1) * BLOCK)
                    place = slice(index * step, (index + 1) * step)
                    total[slot, place, lanes] += (
                        rows_ref[0, number, place, lanes].astype(jnp.float32)
                        * factors_ref[base + part]
                    )

        @pl.when(piece == devices - 1)
        def _():
            out_ref[...] = total[...].astype(jnp.bfloat16)

    (merged,), token = step_call(
        kernel,
        token,
        (slots, factors, rows_of),
        [SMEM, SMEM, pl.BlockSpec((1, sources, rows, width), lambda i: (i, 0, 0, 0))],
        [jax.ShapeDtypeStruct((devices, rows, width), jnp.bfloat16)],
        [pl.BlockSpec((devices, rows, width), lambda i: (0, 0, 0))],
        grid=(devices,),
        scratch_shapes=[pltpu.VMEM((devices, rows, width), jnp.float32)],
        name="merge",
    )
    return merged, token


def pair(token, tokens, other):
    def kernel(tokens_ref, other_ref, out_ref):
        out_ref[0] = tokens_ref[...]
        out_ref[1] = other_ref[...]

    (both,), token = step_call(
        kernel,
        token,
        (tokens, other),
        [VMEM, VMEM],
        [jax.ShapeDtypeStruct((2,) + tokens.shape, tokens.dtype)],
        [VMEM],
        name="pair",
    )
    return both, token


def line(token, info, both, nearby):
    _, tok_dev, width = both.shape

    def kernel(info_ref, both_ref, nearby_ref, out_ref):
        level = info_ref[1]
        for index, other in enumerate((both_ref, nearby_ref)):
            out_ref[level ^ index] = other[0]
            out_ref[level ^ index ^ (PLANES // 2)] = other[1]

    (whole,), token = step_call(
        kernel,
        token,
        (info, both, nearby),
        [SMEM, VMEM, VMEM],
        [jax.ShapeDtypeStruct((PLANES, tok_dev, width), both.dtype)],
        [VMEM],
        name="line",
    )
    return whole, token


def run_chunk(token, info, grouped, own, partner, outputs, start, full, blocks):
    depth, width = own.shape
    count = grouped.shape[0]
    each = count // len(blocks)
    factor = 1.0 / math.sqrt(D)

    def kernel(info_ref, grouped_ref, own_ref, partner_ref, *rest):
        gate_out, up_out, hidden_ref, whole, in_sems, out_sems = rest[len(outputs) :]
        halves = [whole.at[:, pl.ds(index * width, width)] for index in range(2)]

        def fill(*sources):
            loads = [
                pltpu.make_async_copy(source, half, in_sems.at[index])
                for index, (source, half) in enumerate(zip(sources, halves))
            ]
            for load in loads:
                load.start()
            for load in loads:
                load.wait()

        @pl.when(info_ref[0] == 0)
        def _():
            fill(own_ref, partner_ref)

        @pl.when(info_ref[0] != 0)
        def _():
            fill(partner_ref, own_ref)

        stores = [
            pltpu.make_async_copy(half, out.at[0, :, pl.ds(start, width)], out_sems.at[index])
            for index, (half, out) in enumerate(zip(halves, (gate_out, up_out)))
        ]
        for store in stores:
            store.start()
        values = jnp.dot(grouped_ref[...], whole[...], preferred_element_type=jnp.float32)
        gate_value = values[:, :width] * factor
        up_value = values[:, width:] * factor
        hidden = (gate_value / (1.0 + jnp.exp(-gate_value)) * up_value).astype(jnp.bfloat16)
        for index, block in enumerate(blocks):
            hidden_ref[block] = hidden[index * each : (index + 1) * each]
        for store in stores:
            store.wait()

    weights = jax.ShapeDtypeStruct((1, depth, full), jnp.bfloat16)
    return step_call(
        kernel,
        token,
        (info, grouped, own, partner, *outputs),
        [SMEM, VMEM, ANY, ANY] + [ANY] * len(outputs),
        [weights, weights, jax.ShapeDtypeStruct((len(blocks), each, width), jnp.bfloat16)],
        [ANY, ANY, VMEM],
        scratch_shapes=[
            pltpu.VMEM((depth, 2 * width), jnp.bfloat16),
            pltpu.SemaphoreType.DMA((2,)),
            pltpu.SemaphoreType.DMA((2,)),
        ],
        input_output_aliases={4 + index: index for index in range(len(outputs))},
        name="run_chunk",
    )


def first_runs(count):
    return max(1, count - 1)


def plan(count):
    cut = first_runs(count)
    order = [("pack", 0), ("raw", 0), ("pack", 1), ("raw", 1), ("sum", 0)]
    for chunk in range(count):
        if chunk + 2 < count:
            order.append(("pack", chunk + 2))
        if chunk == 0:
            order.append(("pair", 0))
        order.append(("back", chunk))
        if chunk + 1 < count:
            order.append(("sum", chunk + 1))
        if chunk == 0:
            order.append(("line", 0))
        if chunk + 1 == count:
            order.extend(("run", earlier) for earlier in range(cut))
        if chunk + 2 < count:
            order.append(("raw", chunk + 2))
    order.append(("give", 0))
    order.extend(("run", later) for later in range(cut, count))
    order.append(("give", 1))
    return order


def route_slots(routes, merged_count, tok_dev):
    experts = jnp.arange(merged_count, dtype=jnp.int32)
    hit_table = jnp.sum((routes[:, :, None] == experts).astype(jnp.int32), axis=1)
    hit_table = hit_table.reshape(-1, tok_dev, merged_count)
    position_lookup = jnp.cumsum(hit_table, axis=1) - hit_table
    return (hit_table, position_lookup)


def chunk_widths(blocks):
    return [max(1, blocks - 2)] + [1] * min(2, blocks - 1)


def shards(tokens, routes, quant_gate, quant_up, gate_scales, up_scales, cluster_ids, frequency):
    expert_count = lax.axis_size("expert")
    own_index = lax.axis_index("expert")
    group_count = lax.axis_size("groups")
    half = lax.axis_index("groups") % 2
    depth, full = quant_gate.shape[1:]
    tok_dev = tokens.shape[0]
    top_count = routes.shape[1]
    capacity = min(tok_dev, 2 * tok_dev * top_count // expert_count)

    plane = expert_count // PLANES
    by_plane = [[z * plane + p for p in range(plane)] for z in range(PLANES)]
    across = [(i, (i + expert_count // 2) % expert_count) for i in range(expert_count)]
    beside = [(i, (i // plane ^ 1) * plane + i % plane) for i in range(expert_count)]
    partners = [(g, g ^ 1) for g in range(group_count)]

    def exchange(pieces):
        return lax.all_to_all(pieces, "expert", 0, 0, tiled=True)

    info = jnp.stack([half, own_index // plane]).astype(jnp.int32)
    rows = depth // expert_count
    step = math.gcd(rows, BLOCK)
    slots = cluster_ids[:, 0]
    weights = cluster_weights(cluster_ids, frequency)
    scales = jnp.where(half == 0, gate_scales, up_scales)
    row_blocks = (own_index * rows + step * jnp.arange(rows // step, dtype=jnp.int32)) // BLOCK
    factors = jnp.take(scales, row_blocks, axis=1) * weights[:, None, None]
    blocks_of_rows = factors.shape[1:]
    factors = factors.reshape(-1)

    hit_table, position_lookup = route_slots(routes, expert_count, tok_dev)
    positions = jnp.arange(capacity, dtype=jnp.int32)

    blocks = [z * plane + p for p in range(plane) for z in range(PLANES)]

    def in_blocks(table):
        column = lax.dynamic_index_in_dim(table, own_index, 2, keepdims=False)
        column = column.reshape(PLANES, plane, tok_dev).transpose(1, 0, 2)
        return column.reshape(expert_count, 1, tok_dev)

    placing = (
        (in_blocks(hit_table) == 1) & (in_blocks(position_lookup) == positions[None, :, None])
    ).astype(jnp.bfloat16)

    experts = jnp.arange(expert_count, dtype=jnp.int32)
    local_routes = lax.dynamic_slice_in_dim(routes, own_index * tok_dev, tok_dev, 0)
    own_slots = lax.dynamic_index_in_dim(position_lookup, own_index, 0, keepdims=False)
    chosen = local_routes[:, :, None] == experts
    slot_of = jnp.sum(jnp.where(chosen, own_slots[:, None, :], 0), axis=2)
    picking = (chosen[:, :, :, None] & (slot_of[:, :, None, None] == positions)).astype(
        jnp.bfloat16
    )
    picking = picking.reshape(tok_dev * top_count, expert_count * capacity)

    widths = chunk_widths(full // BLOCK)
    starts = [BLOCK * sum(widths[:chunk]) for chunk in range(len(widths))]
    token = jnp.zeros(TOKEN.shape, TOKEN.dtype)
    opposite = lax.ppermute(tokens, "expert", across)
    pieces, gathered, merged, own, partner, hiddens = ({} for _ in range(6))
    outputs, returned, last = (), [], len(widths) - 1
    cut = first_runs(len(widths))
    for name, c in plan(len(widths)):
        start, width = starts[c], widths[c] * BLOCK
        if name == "pack":
            (pieces[c],), token = pack(
                token, info, quant_gate, quant_up, start, width, expert_count
            )
        elif name == "pair":
            both, token = pair(token, tokens, opposite)
            nearby = lax.ppermute(both, "expert", beside)
        elif name == "line":
            whole, token = line(token, info, both, nearby)
            everyone = lax.all_gather(whole, "expert", axis=0, tiled=True, axis_index_groups=by_plane)
            arrived = jnp.einsum(
                "jct,jtd->jcd", placing, everyone, preferred_element_type=jnp.float32
            ).astype(jnp.bfloat16)
            arrived = lax.all_gather(arrived, "mp", axis=2, tiled=True)
            grouped = arrived.reshape(expert_count * capacity, depth)
        elif name == "raw":
            if c == 1:
                pieces[c], token = hold(token, pieces[c], [gathered[0], placing, picking])
            elif c >= 2:
                pieces[c], token = hold(token, pieces[c], [own[c - 2]])
            gathered[c] = exchange(pieces[c])
        elif name == "sum":
            merged[c], token = merge(token, slots, factors, gathered[c], start, blocks_of_rows)
        elif name == "back":
            if 0 < c < last:
                merged[c], token = hold(token, merged[c], [gathered[c + 1]])
            own[c] = exchange(merged[c]).reshape(depth, width)
            partner[c] = lax.ppermute(own[c], "groups", partners)
        elif name == "run":
            (*outputs, hiddens[c]), token = run_chunk(
                token, info, grouped, own[c], partner[c], outputs, start, full, blocks
            )
        else:
            batch = [hiddens[i] for i in (range(cut) if c == 0 else range(cut, last + 1))]
            hidden, token = hold(token, jnp.concatenate(batch, axis=2), returned[:c])
            returned.append(exchange(hidden))

    finished = [
        jnp.dot(
            picking,
            part.reshape(expert_count * capacity, part.shape[2]),
            preferred_element_type=jnp.float32,
        ).astype(jnp.bfloat16)
        for part in returned
    ]
    output = jnp.concatenate(finished, axis=1)
    merged_gate, merged_up = outputs
    return (merged_gate, merged_up, output.reshape(tok_dev, top_count, full))


def solution(mesh):
    return jax.shard_map(
        shards,
        mesh=mesh,
        in_specs=(
            P(("groups", "expert"), "mp"),
            P("groups", None),
            P("expert", None, "mp"),
            P("expert", None, "mp"),
            P(None, None, "mp"),
            P(None, None, "mp"),
            P(),
            P(),
        ),
        out_specs=(
            P(("groups", "expert"), None, "mp"),
            P(("groups", "expert"), None, "mp"),
            P(("groups", "expert"), None, "mp"),
        ),
        check_vma=False,
    )
```

```python
import math

import jax
import jax.numpy as jnp
from jax import lax
from jax.experimental import pallas as pl
from jax.experimental.pallas import tpu as pltpu
from jax.sharding import PartitionSpec as P

D = 2560
BLOCK = 128
PLANES = 4
TOKEN = jax.ShapeDtypeStruct((8, 128), jnp.float32)
ANY = pl.BlockSpec(memory_space=pl.ANY)
SMEM = pl.BlockSpec(memory_space=pltpu.SMEM)
VMEM = pl.BlockSpec(memory_space=pltpu.VMEM)
VMEM_LIMIT = 60 * 1024 * 1024


def cluster_weights(cluster_ids, frequency):
    ids = cluster_ids[:, 0]
    same = (ids[:, None] == ids[None, :]).astype(jnp.float32)
    return frequency / jnp.sum(same * frequency[None, :], axis=1)


def step_call(kernel, token, operands, in_specs, out_shape, out_specs, **options):
    count = len(operands)

    def ordered(*refs):
        kernel(*refs[:count], *refs[count + 1 : count + 1 + len(out_shape)], *refs[count + 2 + len(out_shape) :])

    *results, token = pl.pallas_call(
        ordered,
        out_shape=[*out_shape, TOKEN],
        in_specs=[*in_specs, ANY],
        out_specs=[*out_specs, ANY],
        compiler_params=pltpu.CompilerParams(vmem_limit_bytes=VMEM_LIMIT),
        cost_estimate=pl.CostEstimate(flops=0, bytes_accessed=0, transcendentals=0),
        **options,
    )(*operands, token)
    return results, token


def pack(token, info, gate, up, start, width, devices):
    sources, depth, _ = gate.shape
    rows = depth // devices

    def kernel(info_ref, gate_ref, up_ref, *rest):
        out, held, in_sems, out_sems = rest

        def move(source):
            loads = [
                pltpu.make_async_copy(
                    source.at[
                        :,
                        pl.ds(part * rows, rows),
                        pl.ds(start, width),
                    ],
                    held.at[part],
                    in_sems.at[part],
                )
                for part in range(devices)
            ]
            stores = [
                pltpu.make_async_copy(held.at[part], out.at[part], out_sems.at[part])
                for part in range(devices)
            ]
            for load in loads:
                load.start()
            for load, store in zip(loads, stores):
                load.wait()
                store.start()
            for store in stores:
                store.wait()

        @pl.when(info_ref[0] == 0)
        def _():
            move(gate_ref)

        @pl.when(info_ref[0] != 0)
        def _():
            move(up_ref)

    return step_call(
        kernel,
        token,
        (info, gate, up),
        [SMEM, ANY, ANY],
        [jax.ShapeDtypeStruct((devices, sources, rows, width), gate.dtype)],
        [ANY],
        scratch_shapes=[
            pltpu.VMEM((devices, sources, rows, width), gate.dtype),
            pltpu.SemaphoreType.DMA((devices,)),
            pltpu.SemaphoreType.DMA((devices,)),
        ],
        name="pack",
    )


def hold(token, value, earlier):
    def kernel(*refs):
        pass

    (value,), token = step_call(
        kernel,
        token,
        (value, *earlier),
        [ANY] * (1 + len(earlier)),
        [jax.ShapeDtypeStruct(value.shape, value.dtype)],
        [ANY],
        input_output_aliases={0: 0},
        name="hold",
    )
    return value, token


def merge(token, slots, factors, rows_of, start, blocks):
    devices, sources, rows, width = rows_of.shape
    steps, column_blocks = blocks
    step = rows // steps
    first = start // BLOCK

    def kernel(slots_ref, factors_ref, rows_ref, out_ref, total):
        piece = pl.program_id(0)

        @pl.when(piece == 0)
        def _():
            total[...] = jnp.zeros_like(total)

        for number in range(sources):
            source = piece * sources + number
            slot = slots_ref[source]
            for index in range(steps):
                for part in range(width // BLOCK):
                    base = (source * steps + index) * column_blocks + first
                    lanes = slice(part * BLOCK, (part + 1) * BLOCK)
                    place = slice(index * step, (index + 1) * step)
                    total[slot, place, lanes] += (
                        rows_ref[0, number, place, lanes].astype(jnp.float32)
                        * factors_ref[base + part]
                    )

        @pl.when(piece == devices - 1)
        def _():
            out_ref[...] = total[...].astype(jnp.bfloat16)

    (merged,), token = step_call(
        kernel,
        token,
        (slots, factors, rows_of),
        [SMEM, SMEM, pl.BlockSpec((1, sources, rows, width), lambda i: (i, 0, 0, 0))],
        [jax.ShapeDtypeStruct((devices, rows, width), jnp.bfloat16)],
        [pl.BlockSpec((devices, rows, width), lambda i: (0, 0, 0))],
        grid=(devices,),
        scratch_shapes=[pltpu.VMEM((devices, rows, width), jnp.float32)],
        name="merge",
    )
    return merged, token


def pair(token, tokens, other):
    def kernel(tokens_ref, other_ref, out_ref):
        out_ref[0] = tokens_ref[...]
        out_ref[1] = other_ref[...]

    (both,), token = step_call(
        kernel,
        token,
        (tokens, other),
        [VMEM, VMEM],
        [jax.ShapeDtypeStruct((2,) + tokens.shape, tokens.dtype)],
        [VMEM],
        name="pair",
    )
    return both, token


def line(token, info, both, nearby):
    _, tok_dev, width = both.shape

    def kernel(info_ref, both_ref, nearby_ref, out_ref):
        level = info_ref[1]
        for index, other in enumerate((both_ref, nearby_ref)):
            out_ref[level ^ index] = other[0]
            out_ref[level ^ index ^ (PLANES // 2)] = other[1]

    (whole,), token = step_call(
        kernel,
        token,
        (info, both, nearby),
        [SMEM, VMEM, VMEM],
        [jax.ShapeDtypeStruct((PLANES, tok_dev, width), both.dtype)],
        [VMEM],
        name="line",
    )
    return whole, token


def run_chunk(token, info, grouped, own, partner, outputs, start, full, blocks):
    depth, width = own.shape
    count = grouped.shape[0]
    each = count // len(blocks)
    factor = 1.0 / math.sqrt(D)

    def kernel(info_ref, grouped_ref, own_ref, partner_ref, *rest):
        gate_out, up_out, hidden_ref, whole, in_sems, out_sems = rest[len(outputs) :]
        halves = [whole.at[:, pl.ds(index * width, width)] for index in range(2)]

        def fill(*sources):
            loads = [
                pltpu.make_async_copy(source, half, in_sems.at[index])
                for index, (source, half) in enumerate(zip(sources, halves))
            ]
            for load in loads:
                load.start()
            for load in loads:
                load.wait()

        @pl.when(info_ref[0] == 0)
        def _():
            fill(own_ref, partner_ref)

        @pl.when(info_ref[0] != 0)
        def _():
            fill(partner_ref, own_ref)

        stores = [
            pltpu.make_async_copy(half, out.at[0, :, pl.ds(start, width)], out_sems.at[index])
            for index, (half, out) in enumerate(zip(halves, (gate_out, up_out)))
        ]
        for store in stores:
            store.start()
        values = jnp.dot(grouped_ref[...], whole[...], preferred_element_type=jnp.float32)
        gate_value = values[:, :width] * factor
        up_value = values[:, width:] * factor
        hidden = (gate_value / (1.0 + jnp.exp(-gate_value)) * up_value).astype(jnp.bfloat16)
        for index, block in enumerate(blocks):
            hidden_ref[block] = hidden[index * each : (index + 1) * each]
        for store in stores:
            store.wait()

    weights = jax.ShapeDtypeStruct((1, depth, full), jnp.bfloat16)
    return step_call(
        kernel,
        token,
        (info, grouped, own, partner, *outputs),
        [SMEM, VMEM, ANY, ANY] + [ANY] * len(outputs),
        [weights, weights, jax.ShapeDtypeStruct((len(blocks), each, width), jnp.bfloat16)],
        [ANY, ANY, VMEM],
        scratch_shapes=[
            pltpu.VMEM((depth, 2 * width), jnp.bfloat16),
            pltpu.SemaphoreType.DMA((2,)),
            pltpu.SemaphoreType.DMA((2,)),
        ],
        input_output_aliases={4 + index: index for index in range(len(outputs))},
        name="run_chunk",
    )


def first_runs(count):
    return max(1, count - 1)


def plan(count):
    cut = first_runs(count)
    order = [("pack", 0), ("raw", 0), ("pack", 1), ("raw", 1), ("pair", 0), ("sum", 0)]
    for chunk in range(count):
        if chunk + 2 < count:
            order.append(("pack", chunk + 2))
        if chunk == 0:
            order.append(("line", 0))
        order.append(("back", chunk))
        if chunk + 1 < count:
            order.append(("sum", chunk + 1))
        if chunk + 1 == count:
            order.extend(("run", earlier) for earlier in range(cut))
        if chunk + 2 < count:
            order.append(("raw", chunk + 2))
    order.append(("give", 0))
    order.extend(("run", later) for later in range(cut, count))
    order.append(("give", 1))
    return order


def route_slots(routes, merged_count, tok_dev):
    experts = jnp.arange(merged_count, dtype=jnp.int32)
    hit_table = jnp.sum((routes[:, :, None] == experts).astype(jnp.int32), axis=1)
    hit_table = hit_table.reshape(-1, tok_dev, merged_count)
    position_lookup = jnp.cumsum(hit_table, axis=1) - hit_table
    return (hit_table, position_lookup)


def chunk_widths(blocks):
    return [max(1, blocks - 2)] + [1] * min(2, blocks - 1)


def shards(tokens, routes, quant_gate, quant_up, gate_scales, up_scales, cluster_ids, frequency):
    expert_count = lax.axis_size("expert")
    own_index = lax.axis_index("expert")
    group_count = lax.axis_size("groups")
    half = lax.axis_index("groups") % 2
    depth, full = quant_gate.shape[1:]
    tok_dev = tokens.shape[0]
    top_count = routes.shape[1]
    capacity = min(tok_dev, 2 * tok_dev * top_count // expert_count)

    plane = expert_count // PLANES
    by_plane = [[z * plane + p for p in range(plane)] for z in range(PLANES)]
    across = [(i, (i + expert_count // 2) % expert_count) for i in range(expert_count)]
    beside = [(i, (i // plane ^ 1) * plane + i % plane) for i in range(expert_count)]
    partners = [(g, g ^ 1) for g in range(group_count)]

    def exchange(pieces):
        return lax.all_to_all(pieces, "expert", 0, 0, tiled=True)

    info = jnp.stack([half, own_index // plane]).astype(jnp.int32)
    rows = depth // expert_count
    step = math.gcd(rows, BLOCK)
    slots = cluster_ids[:, 0]
    weights = cluster_weights(cluster_ids, frequency)
    scales = jnp.where(half == 0, gate_scales, up_scales)
    row_blocks = (own_index * rows + step * jnp.arange(rows // step, dtype=jnp.int32)) // BLOCK
    factors = jnp.take(scales, row_blocks, axis=1) * weights[:, None, None]
    blocks_of_rows = factors.shape[1:]
    factors = factors.reshape(-1)

    hit_table, position_lookup = route_slots(routes, expert_count, tok_dev)
    positions = jnp.arange(capacity, dtype=jnp.int32)

    blocks = [z * plane + p for p in range(plane) for z in range(PLANES)]

    def in_blocks(table):
        column = lax.dynamic_index_in_dim(table, own_index, 2, keepdims=False)
        column = column.reshape(PLANES, plane, tok_dev).transpose(1, 0, 2)
        return column.reshape(expert_count, 1, tok_dev)

    placing = (
        (in_blocks(hit_table) == 1) & (in_blocks(position_lookup) == positions[None, :, None])
    ).astype(jnp.bfloat16)

    experts = jnp.arange(expert_count, dtype=jnp.int32)
    local_routes = lax.dynamic_slice_in_dim(routes, own_index * tok_dev, tok_dev, 0)
    own_slots = lax.dynamic_index_in_dim(position_lookup, own_index, 0, keepdims=False)
    chosen = local_routes[:, :, None] == experts
    slot_of = jnp.sum(jnp.where(chosen, own_slots[:, None, :], 0), axis=2)
    picking = (chosen[:, :, :, None] & (slot_of[:, :, None, None] == positions)).astype(
        jnp.bfloat16
    )
    picking = picking.reshape(tok_dev * top_count, expert_count * capacity)

    widths = chunk_widths(full // BLOCK)
    starts = [BLOCK * sum(widths[:chunk]) for chunk in range(len(widths))]
    token = jnp.zeros(TOKEN.shape, TOKEN.dtype)
    opposite = lax.ppermute(tokens, "expert", across)
    pieces, gathered, merged, own, partner, hiddens = ({} for _ in range(6))
    outputs, returned, last = (), [], len(widths) - 1
    cut = first_runs(len(widths))
    for name, c in plan(len(widths)):
        start, width = starts[c], widths[c] * BLOCK
        if name == "pack":
            (pieces[c],), token = pack(
                token, info, quant_gate, quant_up, start, width, expert_count
            )
        elif name == "pair":
            both, token = pair(token, tokens, opposite)
            nearby = lax.ppermute(both, "expert", beside)
        elif name == "line":
            whole, token = line(token, info, both, nearby)
            everyone = lax.all_gather(whole, "expert", axis=0, tiled=True, axis_index_groups=by_plane)
            arrived = jnp.einsum(
                "jct,jtd->jcd", placing, everyone, preferred_element_type=jnp.float32
            ).astype(jnp.bfloat16)
            arrived = lax.all_gather(arrived, "mp", axis=2, tiled=True)
            grouped = arrived.reshape(expert_count * capacity, depth)
        elif name == "raw":
            if c == 1:
                pieces[c], token = hold(token, pieces[c], [gathered[0], placing, picking])
            elif c >= 2:
                pieces[c], token = hold(token, pieces[c], [own[c - 2], grouped])
            gathered[c] = exchange(pieces[c])
        elif name == "sum":
            merged[c], token = merge(token, slots, factors, gathered[c], start, blocks_of_rows)
        elif name == "back":
            if c < last:
                merged[c], token = hold(token, merged[c], [gathered[c + 1]])
            own[c] = exchange(merged[c]).reshape(depth, width)
            partner[c] = lax.ppermute(own[c], "groups", partners)
        elif name == "run":
            (*outputs, hiddens[c]), token = run_chunk(
                token, info, grouped, own[c], partner[c], outputs, start, full, blocks
            )
        else:
            batch = [hiddens[i] for i in (range(cut) if c == 0 else range(cut, last + 1))]
            hidden, token = hold(token, jnp.concatenate(batch, axis=2), returned[:c])
            returned.append(exchange(hidden))

    finished = [
        jnp.dot(
            picking,
            part.reshape(expert_count * capacity, part.shape[2]),
            preferred_element_type=jnp.float32,
        ).astype(jnp.bfloat16)
        for part in returned
    ]
    output = jnp.concatenate(finished, axis=1)
    merged_gate, merged_up = outputs
    return (merged_gate, merged_up, output.reshape(tok_dev, top_count, full))


def solution(mesh):
    return jax.shard_map(
        shards,
        mesh=mesh,
        in_specs=(
            P(("groups", "expert"), "mp"),
            P("groups", None),
            P("expert", None, "mp"),
            P("expert", None, "mp"),
            P(None, None, "mp"),
            P(None, None, "mp"),
            P(),
            P(),
        ),
        out_specs=(
            P(("groups", "expert"), None, "mp"),
            P(("groups", "expert"), None, "mp"),
            P(("groups", "expert"), None, "mp"),
        ),
        check_vma=False,
    )
```

```python
import math

import jax
import jax.numpy as jnp
from jax import lax
from jax.experimental import pallas as pl
from jax.experimental.pallas import tpu as pltpu
from jax.sharding import PartitionSpec as P

D = 2560
BLOCK = 128
PLANES = 4
TOKEN = jax.ShapeDtypeStruct((8, 128), jnp.float32)
ANY = pl.BlockSpec(memory_space=pl.ANY)
SMEM = pl.BlockSpec(memory_space=pltpu.SMEM)
VMEM = pl.BlockSpec(memory_space=pltpu.VMEM)
VMEM_LIMIT = 60 * 1024 * 1024


def cluster_weights(cluster_ids, frequency):
    ids = cluster_ids[:, 0]
    same = (ids[:, None] == ids[None, :]).astype(jnp.float32)
    return frequency / jnp.sum(same * frequency[None, :], axis=1)


def step_call(kernel, token, operands, in_specs, out_shape, out_specs, **options):
    count = len(operands)

    def ordered(*refs):
        kernel(*refs[:count], *refs[count + 1 : count + 1 + len(out_shape)], *refs[count + 2 + len(out_shape) :])

    *results, token = pl.pallas_call(
        ordered,
        out_shape=[*out_shape, TOKEN],
        in_specs=[*in_specs, ANY],
        out_specs=[*out_specs, ANY],
        compiler_params=pltpu.CompilerParams(vmem_limit_bytes=VMEM_LIMIT),
        cost_estimate=pl.CostEstimate(flops=0, bytes_accessed=0, transcendentals=0),
        **options,
    )(*operands, token)
    return results, token


def pack(token, info, gate, up, start, width, devices):
    sources, depth, _ = gate.shape
    rows = depth // devices

    def kernel(info_ref, gate_ref, up_ref, *rest):
        out, held, in_sems, out_sems = rest

        def move(source):
            loads = [
                pltpu.make_async_copy(
                    source.at[
                        :,
                        pl.ds(part * rows, rows),
                        pl.ds(start, width),
                    ],
                    held.at[part],
                    in_sems.at[part],
                )
                for part in range(devices)
            ]
            stores = [
                pltpu.make_async_copy(held.at[part], out.at[part], out_sems.at[part])
                for part in range(devices)
            ]
            for load in loads:
                load.start()
            for load, store in zip(loads, stores):
                load.wait()
                store.start()
            for store in stores:
                store.wait()

        @pl.when(info_ref[0] == 0)
        def _():
            move(gate_ref)

        @pl.when(info_ref[0] != 0)
        def _():
            move(up_ref)

    return step_call(
        kernel,
        token,
        (info, gate, up),
        [SMEM, ANY, ANY],
        [jax.ShapeDtypeStruct((devices, sources, rows, width), gate.dtype)],
        [ANY],
        scratch_shapes=[
            pltpu.VMEM((devices, sources, rows, width), gate.dtype),
            pltpu.SemaphoreType.DMA((devices,)),
            pltpu.SemaphoreType.DMA((devices,)),
        ],
        name="pack",
    )


def hold(token, value, earlier):
    def kernel(*refs):
        pass

    (value,), token = step_call(
        kernel,
        token,
        (value, *earlier),
        [ANY] * (1 + len(earlier)),
        [jax.ShapeDtypeStruct(value.shape, value.dtype)],
        [ANY],
        input_output_aliases={0: 0},
        name="hold",
    )
    return value, token


def merge(token, slots, factors, rows_of, start, blocks):
    devices, sources, rows, width = rows_of.shape
    steps, column_blocks = blocks
    step = rows // steps
    first = start // BLOCK

    def kernel(slots_ref, factors_ref, rows_ref, out_ref, total):
        piece = pl.program_id(0)

        @pl.when(piece == 0)
        def _():
            total[...] = jnp.zeros_like(total)

        for number in range(sources):
            source = piece * sources + number
            slot = slots_ref[source]
            for index in range(steps):
                for part in range(width // BLOCK):
                    base = (source * steps + index) * column_blocks + first
                    lanes = slice(part * BLOCK, (part + 1) * BLOCK)
                    place = slice(index * step, (index + 1) * step)
                    total[slot, place, lanes] += (
                        rows_ref[0, number, place, lanes].astype(jnp.float32)
                        * factors_ref[base + part]
                    )

        @pl.when(piece == devices - 1)
        def _():
            out_ref[...] = total[...].astype(jnp.bfloat16)

    (merged,), token = step_call(
        kernel,
        token,
        (slots, factors, rows_of),
        [SMEM, SMEM, pl.BlockSpec((1, sources, rows, width), lambda i: (i, 0, 0, 0))],
        [jax.ShapeDtypeStruct((devices, rows, width), jnp.bfloat16)],
        [pl.BlockSpec((devices, rows, width), lambda i: (0, 0, 0))],
        grid=(devices,),
        scratch_shapes=[pltpu.VMEM((devices, rows, width), jnp.float32)],
        name="merge",
    )
    return merged, token


def pair(token, tokens, other):
    def kernel(tokens_ref, other_ref, out_ref):
        out_ref[0] = tokens_ref[...]
        out_ref[1] = other_ref[...]

    (both,), token = step_call(
        kernel,
        token,
        (tokens, other),
        [VMEM, VMEM],
        [jax.ShapeDtypeStruct((2,) + tokens.shape, tokens.dtype)],
        [VMEM],
        name="pair",
    )
    return both, token


def line(token, info, both, nearby):
    _, tok_dev, width = both.shape

    def kernel(info_ref, both_ref, nearby_ref, out_ref):
        level = info_ref[1]
        for index, other in enumerate((both_ref, nearby_ref)):
            out_ref[level ^ index] = other[0]
            out_ref[level ^ index ^ (PLANES // 2)] = other[1]

    (whole,), token = step_call(
        kernel,
        token,
        (info, both, nearby),
        [SMEM, VMEM, VMEM],
        [jax.ShapeDtypeStruct((PLANES, tok_dev, width), both.dtype)],
        [VMEM],
        name="line",
    )
    return whole, token


def run_chunk(token, info, grouped, own, partner, outputs, start, full, blocks):
    depth, width = own.shape
    count = grouped.shape[0]
    each = count // len(blocks)
    factor = 1.0 / math.sqrt(D)

    def kernel(info_ref, grouped_ref, own_ref, partner_ref, *rest):
        gate_out, up_out, hidden_ref, whole, in_sems, out_sems = rest[len(outputs) :]
        halves = [whole.at[:, pl.ds(index * width, width)] for index in range(2)]

        def fill(*sources):
            loads = [
                pltpu.make_async_copy(source, half, in_sems.at[index])
                for index, (source, half) in enumerate(zip(sources, halves))
            ]
            for load in loads:
                load.start()
            for load in loads:
                load.wait()

        @pl.when(info_ref[0] == 0)
        def _():
            fill(own_ref, partner_ref)

        @pl.when(info_ref[0] != 0)
        def _():
            fill(partner_ref, own_ref)

        stores = [
            pltpu.make_async_copy(half, out.at[0, :, pl.ds(start, width)], out_sems.at[index])
            for index, (half, out) in enumerate(zip(halves, (gate_out, up_out)))
        ]
        for store in stores:
            store.start()
        values = jnp.dot(grouped_ref[...], whole[...], preferred_element_type=jnp.float32)
        gate_value = values[:, :width] * factor
        up_value = values[:, width:] * factor
        hidden = (gate_value / (1.0 + jnp.exp(-gate_value)) * up_value).astype(jnp.bfloat16)
        for index, block in enumerate(blocks):
            hidden_ref[block] = hidden[index * each : (index + 1) * each]
        for store in stores:
            store.wait()

    weights = jax.ShapeDtypeStruct((1, depth, full), jnp.bfloat16)
    return step_call(
        kernel,
        token,
        (info, grouped, own, partner, *outputs),
        [SMEM, VMEM, ANY, ANY] + [ANY] * len(outputs),
        [weights, weights, jax.ShapeDtypeStruct((len(blocks), each, width), jnp.bfloat16)],
        [ANY, ANY, VMEM],
        scratch_shapes=[
            pltpu.VMEM((depth, 2 * width), jnp.bfloat16),
            pltpu.SemaphoreType.DMA((2,)),
            pltpu.SemaphoreType.DMA((2,)),
        ],
        input_output_aliases={4 + index: index for index in range(len(outputs))},
        name="run_chunk",
    )


def first_runs(count):
    return max(1, count - 1)


def plan(count):
    cut = first_runs(count)
    order = [("pack", 0), ("raw", 0), ("pack", 1), ("raw", 1), ("sum", 0)]
    for chunk in range(count):
        if chunk + 2 < count:
            order.append(("pack", chunk + 2))
        if chunk == 0:
            order.append(("pair", 0))
        order.append(("back", chunk))
        if chunk + 1 < count:
            order.append(("sum", chunk + 1))
        if chunk == 0:
            order.append(("line", 0))
        if chunk + 1 == count:
            order.extend(("run", earlier) for earlier in range(cut))
        if chunk + 2 < count:
            order.append(("raw", chunk + 2))
    order.append(("give", 0))
    order.extend(("run", later) for later in range(cut, count))
    order.append(("give", 1))
    return order


def route_slots(routes, merged_count, tok_dev):
    experts = jnp.arange(merged_count, dtype=jnp.int32)
    hit_table = jnp.sum((routes[:, :, None] == experts).astype(jnp.int32), axis=1)
    hit_table = hit_table.reshape(-1, tok_dev, merged_count)
    position_lookup = jnp.cumsum(hit_table, axis=1) - hit_table
    return (hit_table, position_lookup)


def chunk_widths(blocks):
    return [max(1, blocks - 2)] + [1] * min(2, blocks - 1)


def shards(tokens, routes, quant_gate, quant_up, gate_scales, up_scales, cluster_ids, frequency):
    expert_count = lax.axis_size("expert")
    own_index = lax.axis_index("expert")
    group_count = lax.axis_size("groups")
    half = lax.axis_index("groups") % 2
    depth, full = quant_gate.shape[1:]
    tok_dev = tokens.shape[0]
    top_count = routes.shape[1]
    capacity = min(tok_dev, 2 * tok_dev * top_count // expert_count)

    plane = expert_count // PLANES
    by_plane = [[z * plane + p for p in range(plane)] for z in range(PLANES)]
    across = [(i, (i + expert_count // 2) % expert_count) for i in range(expert_count)]
    beside = [(i, (i // plane ^ 1) * plane + i % plane) for i in range(expert_count)]
    partners = [(g, g ^ 1) for g in range(group_count)]

    def exchange(pieces):
        return lax.all_to_all(pieces, "expert", 0, 0, tiled=True)

    info = jnp.stack([half, own_index // plane]).astype(jnp.int32)
    rows = depth // expert_count
    step = math.gcd(rows, BLOCK)
    slots = cluster_ids[:, 0]
    weights = cluster_weights(cluster_ids, frequency)
    scales = jnp.where(half == 0, gate_scales, up_scales)
    row_blocks = (own_index * rows + step * jnp.arange(rows // step, dtype=jnp.int32)) // BLOCK
    factors = jnp.take(scales, row_blocks, axis=1) * weights[:, None, None]
    blocks_of_rows = factors.shape[1:]
    factors = factors.reshape(-1)

    hit_table, position_lookup = route_slots(routes, expert_count, tok_dev)
    positions = jnp.arange(capacity, dtype=jnp.int32)

    blocks = [z * plane + p for p in range(plane) for z in range(PLANES)]

    def in_blocks(table):
        column = lax.dynamic_index_in_dim(table, own_index, 2, keepdims=False)
        column = column.reshape(PLANES, plane, tok_dev).transpose(1, 0, 2)
        return column.reshape(expert_count, 1, tok_dev)

    placing = (
        (in_blocks(hit_table) == 1) & (in_blocks(position_lookup) == positions[None, :, None])
    ).astype(jnp.bfloat16)

    experts = jnp.arange(expert_count, dtype=jnp.int32)
    local_routes = lax.dynamic_slice_in_dim(routes, own_index * tok_dev, tok_dev, 0)
    own_slots = lax.dynamic_index_in_dim(position_lookup, own_index, 0, keepdims=False)
    chosen = local_routes[:, :, None] == experts
    slot_of = jnp.sum(jnp.where(chosen, own_slots[:, None, :], 0), axis=2)
    picking = (chosen[:, :, :, None] & (slot_of[:, :, None, None] == positions)).astype(
        jnp.bfloat16
    )
    picking = picking.reshape(tok_dev * top_count, expert_count * capacity)

    widths = chunk_widths(full // BLOCK)
    starts = [BLOCK * sum(widths[:chunk]) for chunk in range(len(widths))]
    token = jnp.zeros(TOKEN.shape, TOKEN.dtype)
    opposite = lax.ppermute(tokens, "expert", across)
    pieces, gathered, merged, own, partner, hiddens = ({} for _ in range(6))
    outputs, returned, last = (), [], len(widths) - 1
    cut = first_runs(len(widths))
    for name, c in plan(len(widths)):
        start, width = starts[c], widths[c] * BLOCK
        if name == "pack":
            (pieces[c],), token = pack(
                token, info, quant_gate, quant_up, start, width, expert_count
            )
        elif name == "pair":
            both, token = pair(token, tokens, opposite)
            nearby = lax.ppermute(both, "expert", beside)
        elif name == "line":
            whole, token = line(token, info, both, nearby)
            everyone = lax.all_gather(whole, "expert", axis=0, tiled=True, axis_index_groups=by_plane)
            arrived = jnp.einsum(
                "jct,jtd->jcd", placing, everyone, preferred_element_type=jnp.float32
            ).astype(jnp.bfloat16)
            arrived = lax.all_gather(arrived, "mp", axis=2, tiled=True)
            grouped = arrived.reshape(expert_count * capacity, depth)
        elif name == "raw":
            if c == 1:
                pieces[c], token = hold(token, pieces[c], [gathered[0], placing, picking])
            elif c >= 2:
                pieces[c], token = hold(token, pieces[c], [own[c - 2]])
            gathered[c] = exchange(pieces[c])
        elif name == "sum":
            merged[c], token = merge(token, slots, factors, gathered[c], start, blocks_of_rows)
        elif name == "back":
            if c < last:
                merged[c], token = hold(token, merged[c], [gathered[c + 1]])
            own[c] = exchange(merged[c]).reshape(depth, width)
            partner[c] = lax.ppermute(own[c], "groups", partners)
        elif name == "run":
            (*outputs, hiddens[c]), token = run_chunk(
                token, info, grouped, own[c], partner[c], outputs, start, full, blocks
            )
        else:
            batch = [hiddens[i] for i in (range(cut) if c == 0 else range(cut, last + 1))]
            hidden, token = hold(token, jnp.concatenate(batch, axis=2), returned[:c])
            returned.append(exchange(hidden))

    finished = [
        jnp.dot(
            picking,
            part.reshape(expert_count * capacity, part.shape[2]),
            preferred_element_type=jnp.float32,
        ).astype(jnp.bfloat16)
        for part in returned
    ]
    output = jnp.concatenate(finished, axis=1)
    merged_gate, merged_up = outputs
    return (merged_gate, merged_up, output.reshape(tok_dev, top_count, full))


def solution(mesh):
    return jax.shard_map(
        shards,
        mesh=mesh,
        in_specs=(
            P(("groups", "expert"), "mp"),
            P("groups", None),
            P("expert", None, "mp"),
            P("expert", None, "mp"),
            P(None, None, "mp"),
            P(None, None, "mp"),
            P(),
            P(),
        ),
        out_specs=(
            P(("groups", "expert"), None, "mp"),
            P(("groups", "expert"), None, "mp"),
            P(("groups", "expert"), None, "mp"),
        ),
        check_vma=False,
    )
```

```python
import math

import jax
import jax.numpy as jnp
from jax import lax
from jax.experimental import pallas as pl
from jax.experimental.pallas import tpu as pltpu
from jax.sharding import PartitionSpec as P

D = 2560
BLOCK = 128
PLANES = 4
TOKEN = jax.ShapeDtypeStruct((8, 128), jnp.float32)
ANY = pl.BlockSpec(memory_space=pl.ANY)
SMEM = pl.BlockSpec(memory_space=pltpu.SMEM)
VMEM = pl.BlockSpec(memory_space=pltpu.VMEM)
VMEM_LIMIT = 60 * 1024 * 1024


def cluster_weights(cluster_ids, frequency):
    ids = cluster_ids[:, 0]
    same = (ids[:, None] == ids[None, :]).astype(jnp.float32)
    return frequency / jnp.sum(same * frequency[None, :], axis=1)


def step_call(kernel, token, operands, in_specs, out_shape, out_specs, **options):
    count = len(operands)

    def ordered(*refs):
        kernel(*refs[:count], *refs[count + 1 : count + 1 + len(out_shape)], *refs[count + 2 + len(out_shape) :])

    *results, token = pl.pallas_call(
        ordered,
        out_shape=[*out_shape, TOKEN],
        in_specs=[*in_specs, ANY],
        out_specs=[*out_specs, ANY],
        compiler_params=pltpu.CompilerParams(vmem_limit_bytes=VMEM_LIMIT),
        cost_estimate=pl.CostEstimate(flops=0, bytes_accessed=0, transcendentals=0),
        **options,
    )(*operands, token)
    return results, token


def pack(token, info, gate, up, start, width, devices):
    sources, depth, _ = gate.shape
    rows = depth // devices

    def kernel(info_ref, gate_ref, up_ref, *rest):
        out, held, in_sems, out_sems = rest

        def move(source):
            loads = [
                pltpu.make_async_copy(
                    source.at[
                        :,
                        pl.ds(part * rows, rows),
                        pl.ds(start, width),
                    ],
                    held.at[part],
                    in_sems.at[part],
                )
                for part in range(devices)
            ]
            stores = [
                pltpu.make_async_copy(held.at[part], out.at[part], out_sems.at[part])
                for part in range(devices)
            ]
            for load in loads:
                load.start()
            for load, store in zip(loads, stores):
                load.wait()
                store.start()
            for store in stores:
                store.wait()

        @pl.when(info_ref[0] == 0)
        def _():
            move(gate_ref)

        @pl.when(info_ref[0] != 0)
        def _():
            move(up_ref)

    return step_call(
        kernel,
        token,
        (info, gate, up),
        [SMEM, ANY, ANY],
        [jax.ShapeDtypeStruct((devices, sources, rows, width), gate.dtype)],
        [ANY],
        scratch_shapes=[
            pltpu.VMEM((devices, sources, rows, width), gate.dtype),
            pltpu.SemaphoreType.DMA((devices,)),
            pltpu.SemaphoreType.DMA((devices,)),
        ],
        name="pack",
    )


def hold(token, value, earlier):
    def kernel(*refs):
        pass

    (value,), token = step_call(
        kernel,
        token,
        (value, *earlier),
        [ANY] * (1 + len(earlier)),
        [jax.ShapeDtypeStruct(value.shape, value.dtype)],
        [ANY],
        input_output_aliases={0: 0},
        name="hold",
    )
    return value, token


def merge(token, slots, factors, rows_of, start, blocks):
    devices, sources, rows, width = rows_of.shape
    steps, column_blocks = blocks
    step = rows // steps
    first = start // BLOCK

    def kernel(slots_ref, factors_ref, rows_ref, out_ref, total):
        piece = pl.program_id(0)

        @pl.when(piece == 0)
        def _():
            total[...] = jnp.zeros_like(total)

        for number in range(sources):
            source = piece * sources + number
            slot = slots_ref[source]
            for index in range(steps):
                for part in range(width // BLOCK):
                    base = (source * steps + index) * column_blocks + first
                    lanes = slice(part * BLOCK, (part + 1) * BLOCK)
                    place = slice(index * step, (index + 1) * step)
                    total[slot, place, lanes] += (
                        rows_ref[0, number, place, lanes].astype(jnp.float32)
                        * factors_ref[base + part]
                    )

        @pl.when(piece == devices - 1)
        def _():
            out_ref[...] = total[...].astype(jnp.bfloat16)

    (merged,), token = step_call(
        kernel,
        token,
        (slots, factors, rows_of),
        [SMEM, SMEM, pl.BlockSpec((1, sources, rows, width), lambda i: (i, 0, 0, 0))],
        [jax.ShapeDtypeStruct((devices, rows, width), jnp.bfloat16)],
        [pl.BlockSpec((devices, rows, width), lambda i: (0, 0, 0))],
        grid=(devices,),
        scratch_shapes=[pltpu.VMEM((devices, rows, width), jnp.float32)],
        name="merge",
    )
    return merged, token


def pair(token, tokens, other):
    def kernel(tokens_ref, other_ref, out_ref):
        out_ref[0] = tokens_ref[...]
        out_ref[1] = other_ref[...]

    (both,), token = step_call(
        kernel,
        token,
        (tokens, other),
        [VMEM, VMEM],
        [jax.ShapeDtypeStruct((2,) + tokens.shape, tokens.dtype)],
        [VMEM],
        name="pair",
    )
    return both, token


def line(token, info, both, nearby):
    _, tok_dev, width = both.shape

    def kernel(info_ref, both_ref, nearby_ref, out_ref):
        level = info_ref[1]
        for index, other in enumerate((both_ref, nearby_ref)):
            out_ref[level ^ index] = other[0]
            out_ref[level ^ index ^ (PLANES // 2)] = other[1]

    (whole,), token = step_call(
        kernel,
        token,
        (info, both, nearby),
        [SMEM, VMEM, VMEM],
        [jax.ShapeDtypeStruct((PLANES, tok_dev, width), both.dtype)],
        [VMEM],
        name="line",
    )
    return whole, token


def run_chunk(token, info, grouped, own, partner, outputs, start, full, blocks):
    depth, width = own.shape
    count = grouped.shape[0]
    each = count // len(blocks)
    factor = 1.0 / math.sqrt(D)

    def kernel(info_ref, grouped_ref, own_ref, partner_ref, *rest):
        gate_out, up_out, hidden_ref, whole, in_sems, out_sems = rest[len(outputs) :]
        halves = [whole.at[:, pl.ds(index * width, width)] for index in range(2)]

        def fill(*sources):
            loads = [
                pltpu.make_async_copy(source, half, in_sems.at[index])
                for index, (source, half) in enumerate(zip(sources, halves))
            ]
            for load in loads:
                load.start()
            for load in loads:
                load.wait()

        @pl.when(info_ref[0] == 0)
        def _():
            fill(own_ref, partner_ref)

        @pl.when(info_ref[0] != 0)
        def _():
            fill(partner_ref, own_ref)

        stores = [
            pltpu.make_async_copy(half, out.at[0, :, pl.ds(start, width)], out_sems.at[index])
            for index, (half, out) in enumerate(zip(halves, (gate_out, up_out)))
        ]
        for store in stores:
            store.start()
        values = jnp.dot(grouped_ref[...], whole[...], preferred_element_type=jnp.float32)
        gate_value = values[:, :width] * factor
        up_value = values[:, width:] * factor
        hidden = (gate_value / (1.0 + jnp.exp(-gate_value)) * up_value).astype(jnp.bfloat16)
        for index, block in enumerate(blocks):
            hidden_ref[block] = hidden[index * each : (index + 1) * each]
        for store in stores:
            store.wait()

    weights = jax.ShapeDtypeStruct((1, depth, full), jnp.bfloat16)
    return step_call(
        kernel,
        token,
        (info, grouped, own, partner, *outputs),
        [SMEM, VMEM, ANY, ANY] + [ANY] * len(outputs),
        [weights, weights, jax.ShapeDtypeStruct((len(blocks), each, width), jnp.bfloat16)],
        [ANY, ANY, VMEM],
        scratch_shapes=[
            pltpu.VMEM((depth, 2 * width), jnp.bfloat16),
            pltpu.SemaphoreType.DMA((2,)),
            pltpu.SemaphoreType.DMA((2,)),
        ],
        input_output_aliases={4 + index: index for index in range(len(outputs))},
        name="run_chunk",
    )


def first_runs(count):
    return max(1, count - 1)


def plan(count):
    cut = first_runs(count)
    order = [("pack", 0), ("raw", 0), ("pack", 1), ("raw", 1), ("sum", 0)]
    for chunk in range(count):
        if chunk + 2 < count:
            order.append(("pack", chunk + 2))
        if chunk == 0:
            order.append(("pair", 0))
        order.append(("back", chunk))
        if chunk + 1 < count:
            order.append(("sum", chunk + 1))
        if chunk == 0:
            order.append(("line", 0))
        if chunk + 1 == count:
            order.extend(("run", earlier) for earlier in range(cut))
        if chunk + 2 < count:
            order.append(("raw", chunk + 2))
    order.append(("give", 0))
    order.extend(("run", later) for later in range(cut, count))
    order.append(("give", 1))
    return order


def route_slots(routes, merged_count, tok_dev):
    experts = jnp.arange(merged_count, dtype=jnp.int32)
    hit_table = jnp.sum((routes[:, :, None] == experts).astype(jnp.int32), axis=1)
    hit_table = hit_table.reshape(-1, tok_dev, merged_count)
    position_lookup = jnp.cumsum(hit_table, axis=1) - hit_table
    return (hit_table, position_lookup)


def chunk_widths(blocks):
    return [max(1, blocks - 2)] + [1] * min(2, blocks - 1)


def shards(tokens, routes, quant_gate, quant_up, gate_scales, up_scales, cluster_ids, frequency):
    expert_count = lax.axis_size("expert")
    own_index = lax.axis_index("expert")
    group_count = lax.axis_size("groups")
    half = lax.axis_index("groups") % 2
    depth, full = quant_gate.shape[1:]
    tok_dev = tokens.shape[0]
    top_count = routes.shape[1]
    capacity = min(tok_dev, 2 * tok_dev * top_count // expert_count)

    plane = expert_count // PLANES
    by_plane = [[z * plane + p for p in range(plane)] for z in range(PLANES)]
    across = [(i, (i + expert_count // 2) % expert_count) for i in range(expert_count)]
    beside = [(i, (i // plane ^ 1) * plane + i % plane) for i in range(expert_count)]
    partners = [(g, g ^ 1) for g in range(group_count)]

    def exchange(pieces):
        return lax.all_to_all(pieces, "expert", 0, 0, tiled=True)

    info = jnp.stack([half, own_index // plane]).astype(jnp.int32)
    rows = depth // expert_count
    step = math.gcd(rows, BLOCK)
    slots = cluster_ids[:, 0]
    weights = cluster_weights(cluster_ids, frequency)
    scales = jnp.where(half == 0, gate_scales, up_scales)
    row_blocks = (own_index * rows + step * jnp.arange(rows // step, dtype=jnp.int32)) // BLOCK
    factors = jnp.take(scales, row_blocks, axis=1) * weights[:, None, None]
    blocks_of_rows = factors.shape[1:]
    factors = factors.reshape(-1)

    hit_table, position_lookup = route_slots(routes, expert_count, tok_dev)
    positions = jnp.arange(capacity, dtype=jnp.int32)

    blocks = [z * plane + p for p in range(plane) for z in range(PLANES)]

    def in_blocks(table):
        column = lax.dynamic_index_in_dim(table, own_index, 2, keepdims=False)
        column = column.reshape(PLANES, plane, tok_dev).transpose(1, 0, 2)
        return column.reshape(expert_count, 1, tok_dev)

    placing = (
        (in_blocks(hit_table) == 1) & (in_blocks(position_lookup) == positions[None, :, None])
    ).astype(jnp.bfloat16)

    experts = jnp.arange(expert_count, dtype=jnp.int32)
    local_routes = lax.dynamic_slice_in_dim(routes, own_index * tok_dev, tok_dev, 0)
    own_slots = lax.dynamic_index_in_dim(position_lookup, own_index, 0, keepdims=False)
    chosen = local_routes[:, :, None] == experts
    slot_of = jnp.sum(jnp.where(chosen, own_slots[:, None, :], 0), axis=2)
    picking = (chosen[:, :, :, None] & (slot_of[:, :, None, None] == positions)).astype(
        jnp.bfloat16
    )
    picking = picking.reshape(tok_dev * top_count, expert_count * capacity)

    widths = chunk_widths(full // BLOCK)
    starts = [BLOCK * sum(widths[:chunk]) for chunk in range(len(widths))]
    token = jnp.zeros(TOKEN.shape, TOKEN.dtype)
    opposite = lax.ppermute(tokens, "expert", across)
    pieces, gathered, merged, own, partner, hiddens = ({} for _ in range(6))
    outputs, returned, last = (), [], len(widths) - 1
    cut = first_runs(len(widths))
    for name, c in plan(len(widths)):
        start, width = starts[c], widths[c] * BLOCK
        if name == "pack":
            (pieces[c],), token = pack(
                token, info, quant_gate, quant_up, start, width, expert_count
            )
        elif name == "pair":
            both, token = pair(token, tokens, opposite)
            nearby = lax.ppermute(both, "expert", beside)
        elif name == "line":
            whole, token = line(token, info, both, nearby)
            everyone = lax.all_gather(whole, "expert", axis=0, tiled=True, axis_index_groups=by_plane)
            arrived = jnp.einsum(
                "jct,jtd->jcd", placing, everyone, preferred_element_type=jnp.float32
            ).astype(jnp.bfloat16)
            arrived = lax.all_gather(arrived, "mp", axis=2, tiled=True)
            grouped = arrived.reshape(expert_count * capacity, depth)
        elif name == "raw":
            if c == 0:
                pieces[c], token = hold(token, pieces[c], [opposite])
            elif c == 1:
                pieces[c], token = hold(token, pieces[c], [gathered[0], placing, picking])
            else:
                pieces[c], token = hold(token, pieces[c], [own[c - 2]])
            gathered[c] = exchange(pieces[c])
        elif name == "sum":
            merged[c], token = merge(token, slots, factors, gathered[c], start, blocks_of_rows)
        elif name == "back":
            if c < last:
                merged[c], token = hold(token, merged[c], [gathered[c + 1]])
            own[c] = exchange(merged[c]).reshape(depth, width)
            partner[c] = lax.ppermute(own[c], "groups", partners)
        elif name == "run":
            (*outputs, hiddens[c]), token = run_chunk(
                token, info, grouped, own[c], partner[c], outputs, start, full, blocks
            )
        else:
            batch = [hiddens[i] for i in (range(cut) if c == 0 else range(cut, last + 1))]
            hidden, token = hold(token, jnp.concatenate(batch, axis=2), returned[:c])
            returned.append(exchange(hidden))

    finished = [
        jnp.dot(
            picking,
            part.reshape(expert_count * capacity, part.shape[2]),
            preferred_element_type=jnp.float32,
        ).astype(jnp.bfloat16)
        for part in returned
    ]
    output = jnp.concatenate(finished, axis=1)
    merged_gate, merged_up = outputs
    return (merged_gate, merged_up, output.reshape(tok_dev, top_count, full))


def solution(mesh):
    return jax.shard_map(
        shards,
        mesh=mesh,
        in_specs=(
            P(("groups", "expert"), "mp"),
            P("groups", None),
            P("expert", None, "mp"),
            P("expert", None, "mp"),
            P(None, None, "mp"),
            P(None, None, "mp"),
            P(),
            P(),
        ),
        out_specs=(
            P(("groups", "expert"), None, "mp"),
            P(("groups", "expert"), None, "mp"),
            P(("groups", "expert"), None, "mp"),
        ),
        check_vma=False,
    )
```

```python
import math

import jax
import jax.numpy as jnp
from jax import lax
from jax.experimental import pallas as pl
from jax.experimental.pallas import tpu as pltpu
from jax.sharding import PartitionSpec as P

D = 2560
BLOCK = 128
PLANES = 4
TOKEN = jax.ShapeDtypeStruct((8, 128), jnp.float32)
ANY = pl.BlockSpec(memory_space=pl.ANY)
SMEM = pl.BlockSpec(memory_space=pltpu.SMEM)
VMEM = pl.BlockSpec(memory_space=pltpu.VMEM)
VMEM_LIMIT = 60 * 1024 * 1024


def cluster_weights(cluster_ids, frequency):
    ids = cluster_ids[:, 0]
    same = (ids[:, None] == ids[None, :]).astype(jnp.float32)
    return frequency / jnp.sum(same * frequency[None, :], axis=1)


def step_call(kernel, token, operands, in_specs, out_shape, out_specs, **options):
    count = len(operands)

    def ordered(*refs):
        kernel(*refs[:count], *refs[count + 1 : count + 1 + len(out_shape)], *refs[count + 2 + len(out_shape) :])

    *results, token = pl.pallas_call(
        ordered,
        out_shape=[*out_shape, TOKEN],
        in_specs=[*in_specs, ANY],
        out_specs=[*out_specs, ANY],
        compiler_params=pltpu.CompilerParams(vmem_limit_bytes=VMEM_LIMIT),
        cost_estimate=pl.CostEstimate(flops=0, bytes_accessed=0, transcendentals=0),
        **options,
    )(*operands, token)
    return results, token


def pack(token, info, gate, up, start, width, devices):
    sources, depth, _ = gate.shape
    rows = depth // devices

    def kernel(info_ref, gate_ref, up_ref, *rest):
        out, held, in_sems, out_sems = rest

        def move(source):
            loads = [
                pltpu.make_async_copy(
                    source.at[
                        :,
                        pl.ds(part * rows, rows),
                        pl.ds(start, width),
                    ],
                    held.at[part],
                    in_sems.at[part],
                )
                for part in range(devices)
            ]
            stores = [
                pltpu.make_async_copy(held.at[part], out.at[part], out_sems.at[part])
                for part in range(devices)
            ]
            for load in loads:
                load.start()
            for load, store in zip(loads, stores):
                load.wait()
                store.start()
            for store in stores:
                store.wait()

        @pl.when(info_ref[0] == 0)
        def _():
            move(gate_ref)

        @pl.when(info_ref[0] != 0)
        def _():
            move(up_ref)

    return step_call(
        kernel,
        token,
        (info, gate, up),
        [SMEM, ANY, ANY],
        [jax.ShapeDtypeStruct((devices, sources, rows, width), gate.dtype)],
        [ANY],
        scratch_shapes=[
            pltpu.VMEM((devices, sources, rows, width), gate.dtype),
            pltpu.SemaphoreType.DMA((devices,)),
            pltpu.SemaphoreType.DMA((devices,)),
        ],
        name="pack",
    )


def hold(token, value, earlier):
    earlier = [
        part[(slice(0, 1),) * (part.ndim - 2) + (slice(0, 16), slice(0, 128))] for part in earlier
    ]

    def kernel(*refs):
        pass

    (value,), token = step_call(
        kernel,
        token,
        (value, *earlier),
        [ANY] * (1 + len(earlier)),
        [jax.ShapeDtypeStruct(value.shape, value.dtype)],
        [ANY],
        input_output_aliases={0: 0},
        name="hold",
    )
    return value, token


def merge(token, slots, factors, rows_of, start, blocks):
    devices, sources, rows, width = rows_of.shape
    steps, column_blocks = blocks
    step = rows // steps
    first = start // BLOCK

    def kernel(slots_ref, factors_ref, rows_ref, out_ref, total):
        piece = pl.program_id(0)

        @pl.when(piece == 0)
        def _():
            total[...] = jnp.zeros_like(total)

        for number in range(sources):
            source = piece * sources + number
            slot = slots_ref[source]
            for index in range(steps):
                for part in range(width // BLOCK):
                    base = (source * steps + index) * column_blocks + first
                    lanes = slice(part * BLOCK, (part + 1) * BLOCK)
                    place = slice(index * step, (index + 1) * step)
                    total[slot, place, lanes] += (
                        rows_ref[0, number, place, lanes].astype(jnp.float32)
                        * factors_ref[base + part]
                    )

        @pl.when(piece == devices - 1)
        def _():
            out_ref[...] = total[...].astype(jnp.bfloat16)

    (merged,), token = step_call(
        kernel,
        token,
        (slots, factors, rows_of),
        [SMEM, SMEM, pl.BlockSpec((1, sources, rows, width), lambda i: (i, 0, 0, 0))],
        [jax.ShapeDtypeStruct((devices, rows, width), jnp.bfloat16)],
        [pl.BlockSpec((devices, rows, width), lambda i: (0, 0, 0))],
        grid=(devices,),
        scratch_shapes=[pltpu.VMEM((devices, rows, width), jnp.float32)],
        name="merge",
    )
    return merged, token


def pair(token, tokens, other):
    def kernel(tokens_ref, other_ref, out_ref):
        out_ref[0] = tokens_ref[...]
        out_ref[1] = other_ref[...]

    (both,), token = step_call(
        kernel,
        token,
        (tokens, other),
        [VMEM, VMEM],
        [jax.ShapeDtypeStruct((2,) + tokens.shape, tokens.dtype)],
        [VMEM],
        name="pair",
    )
    return both, token


def line(token, info, both, nearby):
    _, tok_dev, width = both.shape

    def kernel(info_ref, both_ref, nearby_ref, out_ref):
        level = info_ref[1]
        for index, other in enumerate((both_ref, nearby_ref)):
            out_ref[level ^ index] = other[0]
            out_ref[level ^ index ^ (PLANES // 2)] = other[1]

    (whole,), token = step_call(
        kernel,
        token,
        (info, both, nearby),
        [SMEM, VMEM, VMEM],
        [jax.ShapeDtypeStruct((PLANES, tok_dev, width), both.dtype)],
        [VMEM],
        name="line",
    )
    return whole, token


def run_chunk(token, info, grouped, own, partner, outputs, start, full, blocks):
    depth, width = own.shape
    count = grouped.shape[0]
    each = count // len(blocks)
    factor = 1.0 / math.sqrt(D)

    def kernel(info_ref, grouped_ref, own_ref, partner_ref, *rest):
        gate_out, up_out, hidden_ref, whole, in_sems, out_sems = rest[len(outputs) :]
        halves = [whole.at[:, pl.ds(index * width, width)] for index in range(2)]

        def fill(*sources):
            loads = [
                pltpu.make_async_copy(source, half, in_sems.at[index])
                for index, (source, half) in enumerate(zip(sources, halves))
            ]
            for load in loads:
                load.start()
            for load in loads:
                load.wait()

        @pl.when(info_ref[0] == 0)
        def _():
            fill(own_ref, partner_ref)

        @pl.when(info_ref[0] != 0)
        def _():
            fill(partner_ref, own_ref)

        stores = [
            pltpu.make_async_copy(half, out.at[0, :, pl.ds(start, width)], out_sems.at[index])
            for index, (half, out) in enumerate(zip(halves, (gate_out, up_out)))
        ]
        for store in stores:
            store.start()
        values = jnp.dot(grouped_ref[...], whole[...], preferred_element_type=jnp.float32)
        gate_value = values[:, :width] * factor
        up_value = values[:, width:] * factor
        hidden = (gate_value / (1.0 + jnp.exp(-gate_value)) * up_value).astype(jnp.bfloat16)
        for index, block in enumerate(blocks):
            hidden_ref[block] = hidden[index * each : (index + 1) * each]
        for store in stores:
            store.wait()

    weights = jax.ShapeDtypeStruct((1, depth, full), jnp.bfloat16)
    return step_call(
        kernel,
        token,
        (info, grouped, own, partner, *outputs),
        [SMEM, VMEM, ANY, ANY] + [ANY] * len(outputs),
        [weights, weights, jax.ShapeDtypeStruct((len(blocks), each, width), jnp.bfloat16)],
        [ANY, ANY, VMEM],
        scratch_shapes=[
            pltpu.VMEM((depth, 2 * width), jnp.bfloat16),
            pltpu.SemaphoreType.DMA((2,)),
            pltpu.SemaphoreType.DMA((2,)),
        ],
        input_output_aliases={4 + index: index for index in range(len(outputs))},
        name="run_chunk",
    )


def first_runs(count):
    return max(1, count - 1)


def plan(count):
    cut = first_runs(count)
    order = [("pack", 0), ("raw", 0), ("pack", 1), ("raw", 1), ("sum", 0)]
    for chunk in range(count):
        if chunk + 2 < count:
            order.append(("pack", chunk + 2))
        if chunk == 0:
            order.append(("pair", 0))
        order.append(("back", chunk))
        if chunk + 1 < count:
            order.append(("sum", chunk + 1))
        if chunk == 0:
            order.append(("line", 0))
        if chunk + 1 == count:
            order.extend(("run", earlier) for earlier in range(cut))
        if chunk + 2 < count:
            order.append(("raw", chunk + 2))
    order.append(("give", 0))
    order.extend(("run", later) for later in range(cut, count))
    order.append(("give", 1))
    return order


def route_slots(routes, merged_count, tok_dev):
    experts = jnp.arange(merged_count, dtype=jnp.int32)
    hit_table = jnp.sum((routes[:, :, None] == experts).astype(jnp.int32), axis=1)
    hit_table = hit_table.reshape(-1, tok_dev, merged_count)
    position_lookup = jnp.cumsum(hit_table, axis=1) - hit_table
    return (hit_table, position_lookup)


def chunk_widths(blocks):
    return [max(1, blocks - 2)] + [1] * min(2, blocks - 1)


def shards(tokens, routes, quant_gate, quant_up, gate_scales, up_scales, cluster_ids, frequency):
    expert_count = lax.axis_size("expert")
    own_index = lax.axis_index("expert")
    group_count = lax.axis_size("groups")
    half = lax.axis_index("groups") % 2
    depth, full = quant_gate.shape[1:]
    tok_dev = tokens.shape[0]
    top_count = routes.shape[1]
    capacity = min(tok_dev, 2 * tok_dev * top_count // expert_count)

    plane = expert_count // PLANES
    by_plane = [[z * plane + p for p in range(plane)] for z in range(PLANES)]
    across = [(i, (i + expert_count // 2) % expert_count) for i in range(expert_count)]
    beside = [(i, (i // plane ^ 1) * plane + i % plane) for i in range(expert_count)]
    partners = [(g, g ^ 1) for g in range(group_count)]

    def exchange(pieces):
        return lax.all_to_all(pieces, "expert", 0, 0, tiled=True)

    info = jnp.stack([half, own_index // plane]).astype(jnp.int32)
    rows = depth // expert_count
    step = math.gcd(rows, BLOCK)
    slots = cluster_ids[:, 0]
    weights = cluster_weights(cluster_ids, frequency)
    scales = jnp.where(half == 0, gate_scales, up_scales)
    row_blocks = (own_index * rows + step * jnp.arange(rows // step, dtype=jnp.int32)) // BLOCK
    factors = jnp.take(scales, row_blocks, axis=1) * weights[:, None, None]
    blocks_of_rows = factors.shape[1:]
    factors = factors.reshape(-1)

    hit_table, position_lookup = route_slots(routes, expert_count, tok_dev)
    positions = jnp.arange(capacity, dtype=jnp.int32)

    blocks = [z * plane + p for p in range(plane) for z in range(PLANES)]

    def in_blocks(table):
        column = lax.dynamic_index_in_dim(table, own_index, 2, keepdims=False)
        column = column.reshape(PLANES, plane, tok_dev).transpose(1, 0, 2)
        return column.reshape(expert_count, 1, tok_dev)

    placing = (
        (in_blocks(hit_table) == 1) & (in_blocks(position_lookup) == positions[None, :, None])
    ).astype(jnp.bfloat16)

    experts = jnp.arange(expert_count, dtype=jnp.int32)
    local_routes = lax.dynamic_slice_in_dim(routes, own_index * tok_dev, tok_dev, 0)
    own_slots = lax.dynamic_index_in_dim(position_lookup, own_index, 0, keepdims=False)
    chosen = local_routes[:, :, None] == experts
    slot_of = jnp.sum(jnp.where(chosen, own_slots[:, None, :], 0), axis=2)
    picking = (chosen[:, :, :, None] & (slot_of[:, :, None, None] == positions)).astype(
        jnp.bfloat16
    )
    picking = picking.reshape(tok_dev * top_count, expert_count * capacity)

    widths = chunk_widths(full // BLOCK)
    starts = [BLOCK * sum(widths[:chunk]) for chunk in range(len(widths))]
    token = jnp.zeros(TOKEN.shape, TOKEN.dtype)
    opposite = lax.ppermute(tokens, "expert", across)
    pieces, gathered, merged, own, partner, hiddens = ({} for _ in range(6))
    outputs, returned, last = (), [], len(widths) - 1
    cut = first_runs(len(widths))
    for name, c in plan(len(widths)):
        start, width = starts[c], widths[c] * BLOCK
        if name == "pack":
            (pieces[c],), token = pack(
                token, info, quant_gate, quant_up, start, width, expert_count
            )
        elif name == "pair":
            both, token = pair(token, tokens, opposite)
            nearby = lax.ppermute(both, "expert", beside)
        elif name == "line":
            whole, token = line(token, info, both, nearby)
            everyone = lax.all_gather(whole, "expert", axis=0, tiled=True, axis_index_groups=by_plane)
            arrived = jnp.einsum(
                "jct,jtd->jcd", placing, everyone, preferred_element_type=jnp.float32
            ).astype(jnp.bfloat16)
            arrived = lax.all_gather(arrived, "mp", axis=2, tiled=True)
            grouped = arrived.reshape(expert_count * capacity, depth)
        elif name == "raw":
            if c == 0:
                pieces[c], token = hold(token, pieces[c], [opposite])
            elif c == 1:
                pieces[c], token = hold(token, pieces[c], [gathered[0], placing, picking])
            else:
                pieces[c], token = hold(token, pieces[c], [own[c - 2]])
            gathered[c] = exchange(pieces[c])
        elif name == "sum":
            merged[c], token = merge(token, slots, factors, gathered[c], start, blocks_of_rows)
        elif name == "back":
            if c < last:
                merged[c], token = hold(token, merged[c], [gathered[c + 1]])
            own[c] = exchange(merged[c]).reshape(depth, width)
            partner[c] = lax.ppermute(own[c], "groups", partners)
        elif name == "run":
            (*outputs, hiddens[c]), token = run_chunk(
                token, info, grouped, own[c], partner[c], outputs, start, full, blocks
            )
        else:
            batch = [hiddens[i] for i in (range(cut) if c == 0 else range(cut, last + 1))]
            hidden, token = hold(token, jnp.concatenate(batch, axis=2), returned[:c])
            returned.append(exchange(hidden))

    finished = [
        jnp.dot(
            picking,
            part.reshape(expert_count * capacity, part.shape[2]),
            preferred_element_type=jnp.float32,
        ).astype(jnp.bfloat16)
        for part in returned
    ]
    output = jnp.concatenate(finished, axis=1)
    merged_gate, merged_up = outputs
    return (merged_gate, merged_up, output.reshape(tok_dev, top_count, full))


def solution(mesh):
    return jax.shard_map(
        shards,
        mesh=mesh,
        in_specs=(
            P(("groups", "expert"), "mp"),
            P("groups", None),
            P("expert", None, "mp"),
            P("expert", None, "mp"),
            P(None, None, "mp"),
            P(None, None, "mp"),
            P(),
            P(),
        ),
        out_specs=(
            P(("groups", "expert"), None, "mp"),
            P(("groups", "expert"), None, "mp"),
            P(("groups", "expert"), None, "mp"),
        ),
        check_vma=False,
    )
```

```python
import math

import jax
import jax.numpy as jnp
from jax import lax
from jax.experimental import pallas as pl
from jax.experimental.pallas import tpu as pltpu
from jax.sharding import PartitionSpec as P

D = 2560
BLOCK = 128
PLANES = 4
TOKEN = jax.ShapeDtypeStruct((8, 128), jnp.float32)
ANY = pl.BlockSpec(memory_space=pl.ANY)
SMEM = pl.BlockSpec(memory_space=pltpu.SMEM)
VMEM = pl.BlockSpec(memory_space=pltpu.VMEM)
VMEM_LIMIT = 60 * 1024 * 1024


def cluster_weights(cluster_ids, frequency):
    ids = cluster_ids[:, 0]
    same = (ids[:, None] == ids[None, :]).astype(jnp.float32)
    return frequency / jnp.sum(same * frequency[None, :], axis=1)


def step_call(kernel, token, operands, in_specs, out_shape, out_specs, **options):
    count = len(operands)

    def ordered(*refs):
        kernel(*refs[:count], *refs[count + 1 : count + 1 + len(out_shape)], *refs[count + 2 + len(out_shape) :])

    *results, token = pl.pallas_call(
        ordered,
        out_shape=[*out_shape, TOKEN],
        in_specs=[*in_specs, ANY],
        out_specs=[*out_specs, ANY],
        compiler_params=pltpu.CompilerParams(vmem_limit_bytes=VMEM_LIMIT),
        cost_estimate=pl.CostEstimate(flops=0, bytes_accessed=0, transcendentals=0),
        **options,
    )(*operands, token)
    return results, token


def pack(token, info, gate, up, start, width, devices):
    sources, depth, _ = gate.shape
    rows = depth // devices

    def kernel(info_ref, gate_ref, up_ref, *rest):
        out, held, in_sems, out_sems = rest

        def move(source):
            loads = [
                pltpu.make_async_copy(
                    source.at[
                        :,
                        pl.ds(part * rows, rows),
                        pl.ds(start, width),
                    ],
                    held.at[part],
                    in_sems.at[part],
                )
                for part in range(devices)
            ]
            stores = [
                pltpu.make_async_copy(held.at[part], out.at[part], out_sems.at[part])
                for part in range(devices)
            ]
            for load in loads:
                load.start()
            for load, store in zip(loads, stores):
                load.wait()
                store.start()
            for store in stores:
                store.wait()

        @pl.when(info_ref[0] == 0)
        def _():
            move(gate_ref)

        @pl.when(info_ref[0] != 0)
        def _():
            move(up_ref)

    return step_call(
        kernel,
        token,
        (info, gate, up),
        [SMEM, ANY, ANY],
        [jax.ShapeDtypeStruct((devices, sources, rows, width), gate.dtype)],
        [ANY],
        scratch_shapes=[
            pltpu.VMEM((devices, sources, rows, width), gate.dtype),
            pltpu.SemaphoreType.DMA((devices,)),
            pltpu.SemaphoreType.DMA((devices,)),
        ],
        name="pack",
    )


def hold(token, value, earlier):
    def kernel(*refs):
        pass

    (value,), token = step_call(
        kernel,
        token,
        (value, *earlier),
        [ANY] * (1 + len(earlier)),
        [jax.ShapeDtypeStruct(value.shape, value.dtype)],
        [ANY],
        input_output_aliases={0: 0},
        name="hold",
    )
    return value, token


def merge(token, slots, factors, rows_of, start, blocks):
    devices, sources, rows, width = rows_of.shape
    steps, column_blocks = blocks
    step = rows // steps
    first = start // BLOCK

    def kernel(slots_ref, factors_ref, rows_ref, out_ref, total):
        piece = pl.program_id(0)

        @pl.when(piece == 0)
        def _():
            total[...] = jnp.zeros_like(total)

        for number in range(sources):
            source = piece * sources + number
            slot = slots_ref[source]
            for index in range(steps):
                for part in range(width // BLOCK):
                    base = (source * steps + index) * column_blocks + first
                    lanes = slice(part * BLOCK, (part + 1) * BLOCK)
                    place = slice(index * step, (index + 1) * step)
                    total[slot, place, lanes] += (
                        rows_ref[0, number, place, lanes].astype(jnp.float32)
                        * factors_ref[base + part]
                    )

        @pl.when(piece == devices - 1)
        def _():
            out_ref[...] = total[...].astype(jnp.bfloat16)

    (merged,), token = step_call(
        kernel,
        token,
        (slots, factors, rows_of),
        [SMEM, SMEM, pl.BlockSpec((1, sources, rows, width), lambda i: (i, 0, 0, 0))],
        [jax.ShapeDtypeStruct((devices, rows, width), jnp.bfloat16)],
        [pl.BlockSpec((devices, rows, width), lambda i: (0, 0, 0))],
        grid=(devices,),
        scratch_shapes=[pltpu.VMEM((devices, rows, width), jnp.float32)],
        name="merge",
    )
    return merged, token


def pair(token, tokens, other):
    def kernel(tokens_ref, other_ref, out_ref):
        out_ref[0] = tokens_ref[...]
        out_ref[1] = other_ref[...]

    (both,), token = step_call(
        kernel,
        token,
        (tokens, other),
        [VMEM, VMEM],
        [jax.ShapeDtypeStruct((2,) + tokens.shape, tokens.dtype)],
        [VMEM],
        name="pair",
    )
    return both, token


def line(token, info, both, nearby):
    _, tok_dev, width = both.shape

    def kernel(info_ref, both_ref, nearby_ref, out_ref):
        level = info_ref[1]
        for index, other in enumerate((both_ref, nearby_ref)):
            out_ref[level ^ index] = other[0]
            out_ref[level ^ index ^ (PLANES // 2)] = other[1]

    (whole,), token = step_call(
        kernel,
        token,
        (info, both, nearby),
        [SMEM, VMEM, VMEM],
        [jax.ShapeDtypeStruct((PLANES, tok_dev, width), both.dtype)],
        [VMEM],
        name="line",
    )
    return whole, token


def run_chunk(token, info, grouped, own, partner, outputs, start, full, blocks, sent):
    begun, sent_width, sent_start = sent
    outputs = (*outputs, *begun)
    given = len(outputs)
    place_of = [0, 1, 2] if len(outputs) == 3 else [0, 1] if given == 2 and not begun else [2][:given]
    depth, width = own.shape
    count = grouped.shape[0]
    each = count // len(blocks)
    factor = 1.0 / math.sqrt(D)

    def kernel(info_ref, grouped_ref, own_ref, partner_ref, *rest):
        gate_out, up_out, hidden_out, whole, hidden_ref, in_sems, out_sems = rest[given:]
        halves = [whole.at[:, pl.ds(index * width, width)] for index in range(2)]

        def fill(*sources):
            loads = [
                pltpu.make_async_copy(source, half, in_sems.at[index])
                for index, (source, half) in enumerate(zip(sources, halves))
            ]
            for load in loads:
                load.start()
            for load in loads:
                load.wait()

        @pl.when(info_ref[0] == 0)
        def _():
            fill(own_ref, partner_ref)

        @pl.when(info_ref[0] != 0)
        def _():
            fill(partner_ref, own_ref)

        stores = [
            pltpu.make_async_copy(half, out.at[0, :, pl.ds(start, width)], out_sems.at[index])
            for index, (half, out) in enumerate(zip(halves, (gate_out, up_out)))
        ]
        for store in stores:
            store.start()
        values = jnp.dot(grouped_ref[...], whole[...], preferred_element_type=jnp.float32)
        gate_value = values[:, :width] * factor
        up_value = values[:, width:] * factor
        hidden = (gate_value / (1.0 + jnp.exp(-gate_value)) * up_value).astype(jnp.bfloat16)
        for index, block in enumerate(blocks):
            hidden_ref[block] = hidden[index * each : (index + 1) * each]
        back = pltpu.make_async_copy(
            hidden_ref, hidden_out.at[:, :, pl.ds(sent_start, width)], out_sems.at[2]
        )
        back.start()
        back.wait()
        for store in stores:
            store.wait()

    weights = jax.ShapeDtypeStruct((1, depth, full), jnp.bfloat16)
    return step_call(
        kernel,
        token,
        (info, grouped, own, partner, *outputs),
        [SMEM, VMEM, ANY, ANY] + [ANY] * len(outputs),
        [weights, weights, jax.ShapeDtypeStruct((len(blocks), each, sent_width), jnp.bfloat16)],
        [ANY, ANY, ANY],
        scratch_shapes=[
            pltpu.VMEM((depth, 2 * width), jnp.bfloat16),
            pltpu.VMEM((len(blocks), each, width), jnp.bfloat16),
            pltpu.SemaphoreType.DMA((2,)),
            pltpu.SemaphoreType.DMA((3,)),
        ],
        input_output_aliases={4 + index: place for index, place in enumerate(place_of)},
        name="run_chunk",
    )


def first_runs(count):
    return max(1, count - 1)


def plan(count):
    cut = first_runs(count)
    order = [("pack", 0), ("raw", 0), ("pack", 1), ("raw", 1), ("sum", 0)]
    for chunk in range(count):
        if chunk + 2 < count:
            order.append(("pack", chunk + 2))
        if chunk == 0:
            order.append(("pair", 0))
        order.append(("back", chunk))
        if chunk + 1 < count:
            order.append(("sum", chunk + 1))
        if chunk == 0:
            order.append(("line", 0))
        if chunk + 1 == count:
            order.extend(("run", earlier) for earlier in range(cut))
        if chunk + 2 < count:
            order.append(("raw", chunk + 2))
    order.append(("give", 0))
    order.extend(("run", later) for later in range(cut, count))
    order.append(("give", 1))
    return order


def route_slots(routes, merged_count, tok_dev):
    experts = jnp.arange(merged_count, dtype=jnp.int32)
    hit_table = jnp.sum((routes[:, :, None] == experts).astype(jnp.int32), axis=1)
    hit_table = hit_table.reshape(-1, tok_dev, merged_count)
    position_lookup = jnp.cumsum(hit_table, axis=1) - hit_table
    return (hit_table, position_lookup)


def chunk_widths(blocks):
    return [max(1, blocks - 2)] + [1] * min(2, blocks - 1)


def shards(tokens, routes, quant_gate, quant_up, gate_scales, up_scales, cluster_ids, frequency):
    expert_count = lax.axis_size("expert")
    own_index = lax.axis_index("expert")
    group_count = lax.axis_size("groups")
    half = lax.axis_index("groups") % 2
    depth, full = quant_gate.shape[1:]
    tok_dev = tokens.shape[0]
    top_count = routes.shape[1]
    capacity = min(tok_dev, 2 * tok_dev * top_count // expert_count)

    plane = expert_count // PLANES
    by_plane = [[z * plane + p for p in range(plane)] for z in range(PLANES)]
    across = [(i, (i + expert_count // 2) % expert_count) for i in range(expert_count)]
    beside = [(i, (i // plane ^ 1) * plane + i % plane) for i in range(expert_count)]
    partners = [(g, g ^ 1) for g in range(group_count)]

    def exchange(pieces):
        return lax.all_to_all(pieces, "expert", 0, 0, tiled=True)

    info = jnp.stack([half, own_index // plane]).astype(jnp.int32)
    rows = depth // expert_count
    step = math.gcd(rows, BLOCK)
    slots = cluster_ids[:, 0]
    weights = cluster_weights(cluster_ids, frequency)
    scales = jnp.where(half == 0, gate_scales, up_scales)
    row_blocks = (own_index * rows + step * jnp.arange(rows // step, dtype=jnp.int32)) // BLOCK
    factors = jnp.take(scales, row_blocks, axis=1) * weights[:, None, None]
    blocks_of_rows = factors.shape[1:]
    factors = factors.reshape(-1)

    hit_table, position_lookup = route_slots(routes, expert_count, tok_dev)
    positions = jnp.arange(capacity, dtype=jnp.int32)

    blocks = [z * plane + p for p in range(plane) for z in range(PLANES)]

    def in_blocks(table):
        column = lax.dynamic_index_in_dim(table, own_index, 2, keepdims=False)
        column = column.reshape(PLANES, plane, tok_dev).transpose(1, 0, 2)
        return column.reshape(expert_count, 1, tok_dev)

    placing = (
        (in_blocks(hit_table) == 1) & (in_blocks(position_lookup) == positions[None, :, None])
    ).astype(jnp.bfloat16)

    experts = jnp.arange(expert_count, dtype=jnp.int32)
    local_routes = lax.dynamic_slice_in_dim(routes, own_index * tok_dev, tok_dev, 0)
    own_slots = lax.dynamic_index_in_dim(position_lookup, own_index, 0, keepdims=False)
    chosen = local_routes[:, :, None] == experts
    slot_of = jnp.sum(jnp.where(chosen, own_slots[:, None, :], 0), axis=2)
    picking = (chosen[:, :, :, None] & (slot_of[:, :, None, None] == positions)).astype(
        jnp.bfloat16
    )
    picking = picking.reshape(tok_dev * top_count, expert_count * capacity)

    widths = chunk_widths(full // BLOCK)
    starts = [BLOCK * sum(widths[:chunk]) for chunk in range(len(widths))]
    token = jnp.zeros(TOKEN.shape, TOKEN.dtype)
    opposite = lax.ppermute(tokens, "expert", across)
    pieces, gathered, merged, own, partner, hiddens = ({} for _ in range(6))
    outputs, returned, last = (), [], len(widths) - 1
    cut = first_runs(len(widths))
    for name, c in plan(len(widths)):
        start, width = starts[c], widths[c] * BLOCK
        if name == "pack":
            (pieces[c],), token = pack(
                token, info, quant_gate, quant_up, start, width, expert_count
            )
        elif name == "pair":
            both, token = pair(token, tokens, opposite)
            nearby = lax.ppermute(both, "expert", beside)
        elif name == "line":
            whole, token = line(token, info, both, nearby)
            everyone = lax.all_gather(whole, "expert", axis=0, tiled=True, axis_index_groups=by_plane)
            arrived = jnp.einsum(
                "jct,jtd->jcd", placing, everyone, preferred_element_type=jnp.float32
            ).astype(jnp.bfloat16)
            arrived = lax.all_gather(arrived, "mp", axis=2, tiled=True)
            grouped = arrived.reshape(expert_count * capacity, depth)
        elif name == "raw":
            if c == 0:
                pieces[c], token = hold(token, pieces[c], [opposite])
            elif c == 1:
                pieces[c], token = hold(token, pieces[c], [gathered[0], placing, picking])
            else:
                pieces[c], token = hold(token, pieces[c], [own[c - 2]])
            gathered[c] = exchange(pieces[c])
        elif name == "sum":
            merged[c], token = merge(token, slots, factors, gathered[c], start, blocks_of_rows)
        elif name == "back":
            if c < last:
                merged[c], token = hold(token, merged[c], [gathered[c + 1]])
            own[c] = exchange(merged[c]).reshape(depth, width)
            partner[c] = lax.ppermute(own[c], "groups", partners)
        elif name == "run":
            batch = 0 if c < cut else 1
            base = starts[cut] if batch else 0
            sent = ([hiddens[batch]] if batch in hiddens else [], (full if batch else starts[cut]) - base, start - base)
            (*outputs, hiddens[batch]), token = run_chunk(
                token, info, grouped, own[c], partner[c], outputs, start, full, blocks, sent
            )
        else:
            hidden, token = hold(token, hiddens[c], returned[:c])
            returned.append(exchange(hidden))

    finished = [
        jnp.dot(
            picking,
            part.reshape(expert_count * capacity, part.shape[2]),
            preferred_element_type=jnp.float32,
        ).astype(jnp.bfloat16)
        for part in returned
    ]
    output = jnp.concatenate(finished, axis=1)
    merged_gate, merged_up = outputs
    return (merged_gate, merged_up, output.reshape(tok_dev, top_count, full))


def solution(mesh):
    return jax.shard_map(
        shards,
        mesh=mesh,
        in_specs=(
            P(("groups", "expert"), "mp"),
            P("groups", None),
            P("expert", None, "mp"),
            P("expert", None, "mp"),
            P(None, None, "mp"),
            P(None, None, "mp"),
            P(),
            P(),
        ),
        out_specs=(
            P(("groups", "expert"), None, "mp"),
            P(("groups", "expert"), None, "mp"),
            P(("groups", "expert"), None, "mp"),
        ),
        check_vma=False,
    )
```

```python
import math

import jax
import jax.numpy as jnp
from jax import lax
from jax.experimental import pallas as pl
from jax.experimental.pallas import tpu as pltpu
from jax.sharding import PartitionSpec as P

D = 2560
BLOCK = 128
PLANES = 4
TOKEN = jax.ShapeDtypeStruct((8, 128), jnp.float32)
ANY = pl.BlockSpec(memory_space=pl.ANY)
SMEM = pl.BlockSpec(memory_space=pltpu.SMEM)
VMEM = pl.BlockSpec(memory_space=pltpu.VMEM)
VMEM_LIMIT = 60 * 1024 * 1024


def cluster_weights(cluster_ids, frequency):
    ids = cluster_ids[:, 0]
    same = (ids[:, None] == ids[None, :]).astype(jnp.float32)
    return frequency / jnp.sum(same * frequency[None, :], axis=1)


def step_call(kernel, token, operands, in_specs, out_shape, out_specs, **options):
    count = len(operands)

    def ordered(*refs):
        kernel(*refs[:count], *refs[count + 1 : count + 1 + len(out_shape)], *refs[count + 2 + len(out_shape) :])

    *results, token = pl.pallas_call(
        ordered,
        out_shape=[*out_shape, TOKEN],
        in_specs=[*in_specs, ANY],
        out_specs=[*out_specs, ANY],
        compiler_params=pltpu.CompilerParams(vmem_limit_bytes=VMEM_LIMIT),
        cost_estimate=pl.CostEstimate(flops=0, bytes_accessed=0, transcendentals=0),
        **options,
    )(*operands, token)
    return results, token


def pack(token, info, gate, up, start, width, devices):
    sources, depth, _ = gate.shape
    rows = depth // devices

    def kernel(info_ref, gate_ref, up_ref, *rest):
        out, held, in_sems, out_sems = rest

        def move(source):
            loads = [
                pltpu.make_async_copy(
                    source.at[
                        :,
                        pl.ds(part * rows, rows),
                        pl.ds(start, width),
                    ],
                    held.at[part],
                    in_sems.at[part],
                )
                for part in range(devices)
            ]
            stores = [
                pltpu.make_async_copy(held.at[part], out.at[part], out_sems.at[part])
                for part in range(devices)
            ]
            for load in loads:
                load.start()
            for load, store in zip(loads, stores):
                load.wait()
                store.start()
            for store in stores:
                store.wait()

        @pl.when(info_ref[0] == 0)
        def _():
            move(gate_ref)

        @pl.when(info_ref[0] != 0)
        def _():
            move(up_ref)

    return step_call(
        kernel,
        token,
        (info, gate, up),
        [SMEM, ANY, ANY],
        [jax.ShapeDtypeStruct((devices, sources, rows, width), gate.dtype)],
        [ANY],
        scratch_shapes=[
            pltpu.VMEM((devices, sources, rows, width), gate.dtype),
            pltpu.SemaphoreType.DMA((devices,)),
            pltpu.SemaphoreType.DMA((devices,)),
        ],
        name="pack",
    )


def corner(part):
    return part[(slice(0, 1),) * (part.ndim - 2) + (slice(0, 16), slice(0, 128))]


def hold(token, value, earlier):
    def kernel(*refs):
        pass

    (value,), token = step_call(
        kernel,
        token,
        (value, *earlier),
        [ANY] * (1 + len(earlier)),
        [jax.ShapeDtypeStruct(value.shape, value.dtype)],
        [ANY],
        input_output_aliases={0: 0},
        name="hold",
    )
    return value, token


def merge(token, slots, factors, rows_of, start, blocks):
    devices, sources, rows, width = rows_of.shape
    steps, column_blocks = blocks
    step = rows // steps
    first = start // BLOCK

    def kernel(slots_ref, factors_ref, rows_ref, out_ref, total):
        piece = pl.program_id(0)

        @pl.when(piece == 0)
        def _():
            total[...] = jnp.zeros_like(total)

        for number in range(sources):
            source = piece * sources + number
            slot = slots_ref[source]
            for index in range(steps):
                for part in range(width // BLOCK):
                    base = (source * steps + index) * column_blocks + first
                    lanes = slice(part * BLOCK, (part + 1) * BLOCK)
                    place = slice(index * step, (index + 1) * step)
                    total[slot, place, lanes] += (
                        rows_ref[0, number, place, lanes].astype(jnp.float32)
                        * factors_ref[base + part]
                    )

        @pl.when(piece == devices - 1)
        def _():
            out_ref[...] = total[...].astype(jnp.bfloat16)

    (merged,), token = step_call(
        kernel,
        token,
        (slots, factors, rows_of),
        [SMEM, SMEM, pl.BlockSpec((1, sources, rows, width), lambda i: (i, 0, 0, 0))],
        [jax.ShapeDtypeStruct((devices, rows, width), jnp.bfloat16)],
        [pl.BlockSpec((devices, rows, width), lambda i: (0, 0, 0))],
        grid=(devices,),
        scratch_shapes=[pltpu.VMEM((devices, rows, width), jnp.float32)],
        name="merge",
    )
    return merged, token


def pair(token, tokens, other):
    def kernel(tokens_ref, other_ref, out_ref):
        out_ref[0] = tokens_ref[...]
        out_ref[1] = other_ref[...]

    (both,), token = step_call(
        kernel,
        token,
        (tokens, other),
        [VMEM, VMEM],
        [jax.ShapeDtypeStruct((2,) + tokens.shape, tokens.dtype)],
        [VMEM],
        name="pair",
    )
    return both, token


def line(token, info, both, nearby):
    _, tok_dev, width = both.shape

    def kernel(info_ref, both_ref, nearby_ref, out_ref):
        level = info_ref[1]
        for index, other in enumerate((both_ref, nearby_ref)):
            out_ref[level ^ index] = other[0]
            out_ref[level ^ index ^ (PLANES // 2)] = other[1]

    (whole,), token = step_call(
        kernel,
        token,
        (info, both, nearby),
        [SMEM, VMEM, VMEM],
        [jax.ShapeDtypeStruct((PLANES, tok_dev, width), both.dtype)],
        [VMEM],
        name="line",
    )
    return whole, token


def run_chunk(token, info, grouped, own, partner, outputs, start, full, blocks, sent):
    begun, sent_width, sent_start = sent
    outputs = (*outputs, *begun)
    given = len(outputs)
    place_of = [0, 1, 2] if len(outputs) == 3 else [0, 1] if given == 2 and not begun else [2][:given]
    depth, width = own.shape
    count = grouped.shape[0]
    each = count // len(blocks)
    factor = 1.0 / math.sqrt(D)

    def kernel(info_ref, grouped_ref, own_ref, partner_ref, *rest):
        gate_out, up_out, hidden_out, whole, hidden_ref, in_sems, out_sems = rest[given:]
        halves = [whole.at[:, pl.ds(index * width, width)] for index in range(2)]

        def fill(*sources):
            loads = [
                pltpu.make_async_copy(source, half, in_sems.at[index])
                for index, (source, half) in enumerate(zip(sources, halves))
            ]
            for load in loads:
                load.start()
            for load in loads:
                load.wait()

        @pl.when(info_ref[0] == 0)
        def _():
            fill(own_ref, partner_ref)

        @pl.when(info_ref[0] != 0)
        def _():
            fill(partner_ref, own_ref)

        stores = [
            pltpu.make_async_copy(half, out.at[0, :, pl.ds(start, width)], out_sems.at[index])
            for index, (half, out) in enumerate(zip(halves, (gate_out, up_out)))
        ]
        for store in stores:
            store.start()
        values = jnp.dot(grouped_ref[...], whole[...], preferred_element_type=jnp.float32)
        gate_value = values[:, :width] * factor
        up_value = values[:, width:] * factor
        hidden = (gate_value / (1.0 + jnp.exp(-gate_value)) * up_value).astype(jnp.bfloat16)
        for index, block in enumerate(blocks):
            hidden_ref[block] = hidden[index * each : (index + 1) * each]
        back = pltpu.make_async_copy(
            hidden_ref, hidden_out.at[:, :, pl.ds(sent_start, width)], out_sems.at[2]
        )
        back.start()
        back.wait()
        for store in stores:
            store.wait()

    weights = jax.ShapeDtypeStruct((1, depth, full), jnp.bfloat16)
    return step_call(
        kernel,
        token,
        (info, grouped, own, partner, *outputs),
        [SMEM, VMEM, ANY, ANY] + [ANY] * len(outputs),
        [weights, weights, jax.ShapeDtypeStruct((len(blocks), each, sent_width), jnp.bfloat16)],
        [ANY, ANY, ANY],
        scratch_shapes=[
            pltpu.VMEM((depth, 2 * width), jnp.bfloat16),
            pltpu.VMEM((len(blocks), each, width), jnp.bfloat16),
            pltpu.SemaphoreType.DMA((2,)),
            pltpu.SemaphoreType.DMA((3,)),
        ],
        input_output_aliases={4 + index: place for index, place in enumerate(place_of)},
        name="run_chunk",
    )


def first_runs(count):
    return max(1, count - 1)


def plan(count):
    cut = first_runs(count)
    order = [("pack", 0), ("raw", 0), ("pack", 1), ("raw", 1), ("sum", 0)]
    for chunk in range(count):
        if chunk + 2 < count:
            order.append(("pack", chunk + 2))
        if chunk == 0:
            order.append(("pair", 0))
        order.append(("back", chunk))
        if chunk + 1 < count:
            order.append(("sum", chunk + 1))
        if chunk == 0:
            order.append(("line", 0))
        if chunk + 1 == count:
            order.extend(("run", earlier) for earlier in range(cut))
        if chunk + 2 < count:
            order.append(("raw", chunk + 2))
    order.append(("give", 0))
    order.extend(("run", later) for later in range(cut, count))
    order.append(("give", 1))
    return order


def route_slots(routes, merged_count, tok_dev):
    experts = jnp.arange(merged_count, dtype=jnp.int32)
    hit_table = jnp.sum((routes[:, :, None] == experts).astype(jnp.int32), axis=1)
    hit_table = hit_table.reshape(-1, tok_dev, merged_count)
    position_lookup = jnp.cumsum(hit_table, axis=1) - hit_table
    return (hit_table, position_lookup)


def chunk_widths(blocks):
    return [max(1, blocks - 2)] + [1] * min(2, blocks - 1)


def shards(tokens, routes, quant_gate, quant_up, gate_scales, up_scales, cluster_ids, frequency):
    expert_count = lax.axis_size("expert")
    own_index = lax.axis_index("expert")
    group_count = lax.axis_size("groups")
    half = lax.axis_index("groups") % 2
    depth, full = quant_gate.shape[1:]
    tok_dev = tokens.shape[0]
    top_count = routes.shape[1]
    capacity = min(tok_dev, 2 * tok_dev * top_count // expert_count)

    plane = expert_count // PLANES
    by_plane = [[z * plane + p for p in range(plane)] for z in range(PLANES)]
    across = [(i, (i + expert_count // 2) % expert_count) for i in range(expert_count)]
    beside = [(i, (i // plane ^ 1) * plane + i % plane) for i in range(expert_count)]
    partners = [(g, g ^ 1) for g in range(group_count)]

    def exchange(pieces):
        return lax.all_to_all(pieces, "expert", 0, 0, tiled=True)

    info = jnp.stack([half, own_index // plane]).astype(jnp.int32)
    rows = depth // expert_count
    step = math.gcd(rows, BLOCK)
    slots = cluster_ids[:, 0]
    weights = cluster_weights(cluster_ids, frequency)
    scales = jnp.where(half == 0, gate_scales, up_scales)
    row_blocks = (own_index * rows + step * jnp.arange(rows // step, dtype=jnp.int32)) // BLOCK
    factors = jnp.take(scales, row_blocks, axis=1) * weights[:, None, None]
    blocks_of_rows = factors.shape[1:]
    factors = factors.reshape(-1)

    hit_table, position_lookup = route_slots(routes, expert_count, tok_dev)
    positions = jnp.arange(capacity, dtype=jnp.int32)

    blocks = [z * plane + p for p in range(plane) for z in range(PLANES)]

    def in_blocks(table):
        column = lax.dynamic_index_in_dim(table, own_index, 2, keepdims=False)
        column = column.reshape(PLANES, plane, tok_dev).transpose(1, 0, 2)
        return column.reshape(expert_count, 1, tok_dev)

    placing = (
        (in_blocks(hit_table) == 1) & (in_blocks(position_lookup) == positions[None, :, None])
    ).astype(jnp.bfloat16)

    experts = jnp.arange(expert_count, dtype=jnp.int32)
    local_routes = lax.dynamic_slice_in_dim(routes, own_index * tok_dev, tok_dev, 0)
    own_slots = lax.dynamic_index_in_dim(position_lookup, own_index, 0, keepdims=False)
    chosen = local_routes[:, :, None] == experts
    slot_of = jnp.sum(jnp.where(chosen, own_slots[:, None, :], 0), axis=2)
    picking = (chosen[:, :, :, None] & (slot_of[:, :, None, None] == positions)).astype(
        jnp.bfloat16
    )
    picking = picking.reshape(tok_dev * top_count, expert_count * capacity)

    widths = chunk_widths(full // BLOCK)
    starts = [BLOCK * sum(widths[:chunk]) for chunk in range(len(widths))]
    token = jnp.zeros(TOKEN.shape, TOKEN.dtype)
    opposite = lax.ppermute(tokens, "expert", across)
    pieces, gathered, merged, own, partner, hiddens = ({} for _ in range(6))
    outputs, returned, last = (), [], len(widths) - 1
    cut = first_runs(len(widths))
    for name, c in plan(len(widths)):
        start, width = starts[c], widths[c] * BLOCK
        if name == "pack":
            (pieces[c],), token = pack(
                token, info, quant_gate, quant_up, start, width, expert_count
            )
        elif name == "pair":
            both, token = pair(token, tokens, opposite)
            nearby = lax.ppermute(both, "expert", beside)
        elif name == "line":
            whole, token = line(token, info, both, nearby)
            everyone = lax.all_gather(whole, "expert", axis=0, tiled=True, axis_index_groups=by_plane)
            arrived = jnp.einsum(
                "jct,jtd->jcd", placing, everyone, preferred_element_type=jnp.float32
            ).astype(jnp.bfloat16)
            arrived = lax.all_gather(arrived, "mp", axis=2, tiled=True)
            grouped = arrived.reshape(expert_count * capacity, depth)
        elif name == "raw":
            if c == 0:
                pieces[c], token = hold(token, pieces[c], [opposite])
            elif c == 1:
                pieces[c], token = hold(token, pieces[c], [gathered[0], placing, picking])
            else:
                pieces[c], token = hold(token, pieces[c], [corner(own[c - 2])])
            gathered[c] = exchange(pieces[c])
        elif name == "sum":
            merged[c], token = merge(token, slots, factors, gathered[c], start, blocks_of_rows)
        elif name == "back":
            if c < last:
                merged[c], token = hold(
                    token, merged[c], [gathered[c + 1] if c else corner(gathered[c + 1])]
                )
            own[c] = exchange(merged[c]).reshape(depth, width)
            partner[c] = lax.ppermute(own[c], "groups", partners)
        elif name == "run":
            batch = 0 if c < cut else 1
            base = starts[cut] if batch else 0
            sent = ([hiddens[batch]] if batch in hiddens else [], (full if batch else starts[cut]) - base, start - base)
            (*outputs, hiddens[batch]), token = run_chunk(
                token, info, grouped, own[c], partner[c], outputs, start, full, blocks, sent
            )
        else:
            hidden, token = hold(token, hiddens[c], [corner(part) for part in returned[:c]])
            returned.append(exchange(hidden))

    finished = [
        jnp.dot(
            picking,
            part.reshape(expert_count * capacity, part.shape[2]),
            preferred_element_type=jnp.float32,
        ).astype(jnp.bfloat16)
        for part in returned
    ]
    output = jnp.concatenate(finished, axis=1)
    merged_gate, merged_up = outputs
    return (merged_gate, merged_up, output.reshape(tok_dev, top_count, full))


def solution(mesh):
    return jax.shard_map(
        shards,
        mesh=mesh,
        in_specs=(
            P(("groups", "expert"), "mp"),
            P("groups", None),
            P("expert", None, "mp"),
            P("expert", None, "mp"),
            P(None, None, "mp"),
            P(None, None, "mp"),
            P(),
            P(),
        ),
        out_specs=(
            P(("groups", "expert"), None, "mp"),
            P(("groups", "expert"), None, "mp"),
            P(("groups", "expert"), None, "mp"),
        ),
        check_vma=False,
    )
```
